256 devices in a mesh: row: 8 (over x, core), col: 32 (over y, z).
Axes of the slice: x: 4, y: 4, z: 8, core: 2. Of those that a mesh axis runs over, the one named last changes fastest.
Arguments:
- expert_matrix: float32 [7168, 32768], P('row', 'col')
- col_signs: int32 [32768], P('col'), may hold values from -1 to 1, as said below
- sample_ids: int32 [1024], replicated, may hold values from 0 to 32767, as said below
Outputs:
- orthobasis: float32 [7168, 1024], P('row')
- projected: float32 [1024, 32768], P('row', 'col')
The draws below stay inside these ranges and needn't reach their ends.
Inputs may be any that keep to these rules, and one draw needn't show every extreme that they name: `col_signs`: each entry is +1 or -1. `sample_ids`: the 1024 indices are distinct.
All inputs are finite; a program needn't handle non-finite values.
Results may differ from the reference program's by a relative error of at most 0.000094.
Values sent between devices are 32-bit elements; how exact they have to be, the bound alone decides.
A program may use at most 128 MiB of HBM per device.

```python
import math
import jax
import jax.numpy as jnp
from jax import lax

D = 7168
SAMPLES = 1024
NCOL = 32768


def draw_expert_matrix(key, part):
    key = jax.random.fold_in(key, 11)
    key_entries, key_rows, key_cols = jax.random.split(key, 3)
    entries = jax.random.normal(key_entries, (D, NCOL), jnp.float32)
    row_scale = jnp.exp(jax.random.uniform(key_rows, (D, 1), jnp.float32, -1.15, 1.15))
    col_scale = jnp.exp(jax.random.uniform(key_cols, (1, NCOL), jnp.float32, -1.15, 1.15))
    return (entries * row_scale * col_scale).astype(jnp.float32)


def draw_col_signs(key, part):
    key = jax.random.fold_in(key, 12)
    return (2 * jax.random.randint(key, (NCOL,), 0, 2) - 1).astype(jnp.int32)


def draw_sample_ids(key, part):
    key = jax.random.fold_in(key, 13)
    key_pick, key_order = jax.random.split(key)
    middle = 1 + jax.random.permutation(key_pick, NCOL - 2)[:SAMPLES - 2]
    chosen = jnp.concatenate([middle.astype(jnp.int32), jnp.array([0, NCOL - 1], jnp.int32)])
    return chosen[jax.random.permutation(key_order, SAMPLES)].astype(jnp.int32)


def setup_inputs(seed: int = 0) -> dict:
    splits = jax.random.split(jax.random.key(seed), 4)
    expert_matrix = draw_expert_matrix(jax.random.fold_in(splits[3], 71), 0)
    col_signs = draw_col_signs(jax.random.fold_in(splits[3], 71), 0)
    sample_ids = draw_sample_ids(jax.random.fold_in(splits[3], 71), 0)
    return dict(expert_matrix=expert_matrix, col_signs=col_signs, sample_ids=sample_ids)


def bit_parity(value):
    folded = value
    for amount in (16, 8, 4, 2, 1):
        folded = jnp.bitwise_xor(folded, jnp.right_shift(folded, amount))
    return jnp.bitwise_and(folded, 1)

def hadamard_table(col_signs, sample_ids, col_offset, col_total):
    col_ids = col_offset + lax.broadcasted_iota(jnp.int32, (col_signs.shape[0], sample_ids.shape[0]), 0)
    parity = bit_parity(jnp.bitwise_and(col_ids, sample_ids[None, :]))
    signed = col_signs[:, None].astype(jnp.float32) * (1 - 2 * parity).astype(jnp.float32)
    return signed / math.sqrt(col_total)

def reference(expert_matrix, col_signs, sample_ids):
    sign_table = hadamard_table(col_signs, sample_ids, 0, NCOL)
    sketch = jnp.dot(expert_matrix.astype(jnp.float32), sign_table.astype(jnp.float32), precision=lax.Precision.HIGHEST, preferred_element_type=jnp.float32)
    gram_matrix = lax.dot_general(sketch.astype(jnp.float32), sketch.astype(jnp.float32), (((0,), (0,)), ((), ())), precision=lax.Precision.HIGHEST, preferred_element_type=jnp.float32)
    lower_factor = jnp.linalg.cholesky(gram_matrix)
    basis_rows = jax.scipy.linalg.solve_triangular(lower_factor, sketch.T, lower=True).T
    projected = lax.dot_general(basis_rows.astype(jnp.float32), expert_matrix.astype(jnp.float32), (((0,), (0,)), ((), ())), precision=lax.Precision.HIGHEST, preferred_element_type=jnp.float32)
    return (basis_rows * math.sqrt(D), projected)
```

```python
import functools
import math

import jax
import jax.numpy as jnp
from jax import lax
from jax.experimental import pallas as pl
from jax.experimental.pallas import tpu as pltpu
from jax.sharding import PartitionSpec as P

MESH = pl.DeviceIdType.MESH
F32 = jnp.float32
BF16 = jnp.bfloat16
NY, NZ, NX = 4, 8, 4
LANES = 128
VMEM = pl.BlockSpec(memory_space=pltpu.VMEM)
LIMIT = 56 << 20


def split(value):
    high = value.astype(BF16)
    return high, (value - high.astype(F32)).astype(BF16)


def mm(a, b, ca, cb):
    return lax.dot_general(a, b, (((ca,), (cb,)), ((), ())), preferred_element_type=F32)


def mm_pair(a, b, ca, cb):
    (ah, al), (bh, bl) = a, b
    return mm(ah, bh, ca, cb) + (mm(ah, bl, ca, cb) + mm(al, bh, ca, cb))


def mm3(a, b, ca, cb):
    return mm_pair(split(a), split(b), ca, cb)


def mm1(a, b, ca, cb):
    return mm(a.astype(BF16), b.astype(BF16), ca, cb)


def sketch_kernel(a_ref, signs_ref, ids_ref, pa_ref, pb_ref, ah, al, *, scale):
    cols = a_ref.shape[1]
    offset = lax.axis_index("col") * cols
    signed = a_ref[...] * signs_ref[...].astype(F32)
    ah[...], al[...] = split(signed)
    wide = 256
    for part in range(ids_ref.shape[1] // wide):
        ids = ids_ref[:, part * wide:(part + 1) * wide]
        col_ids = offset + lax.broadcasted_iota(jnp.int32, (cols, wide), 0)
        parity = lax.population_count(col_ids & ids) & 1
        table = (1 - 2 * parity).astype(F32).astype(BF16)
        out = (mm(ah[...], table, 1, 0) + mm(al[...], table, 1, 0)) * scale
        half = out.shape[0] // (2 * NY)
        for sub in range(wide // LANES):
            block = part * (wide // LANES) + sub
            for y in range(NY):
                piece = out[2 * y * half:2 * (y + 1) * half, sub * LANES:(sub + 1) * LANES]
                pa_ref[block, y] = piece[:half]
                pb_ref[y, block] = piece[half:]


def sketch(a, signs, ids, scale):
    rows, cols = a.shape
    half = rows // (2 * NY)
    return pl.pallas_call(
        functools.partial(sketch_kernel, scale=scale),
        out_shape=(
            jax.ShapeDtypeStruct((NZ, NY, half, LANES), F32),
            jax.ShapeDtypeStruct((NY, NZ, half, LANES), F32),
        ),
        in_specs=[VMEM] * 3,
        out_specs=(VMEM, VMEM),
        scratch_shapes=[pltpu.VMEM((rows, cols), BF16), pltpu.VMEM((rows, cols), BF16)],
        compiler_params=pltpu.CompilerParams(vmem_limit_bytes=LIMIT),
    )(a, signs, ids)


class Wires:
    def __init__(self, send_sems, recv_sems):
        self.send_sems, self.recv_sems = send_sems, recv_sems
        self.copies = []

    def send(self, src, dst, device):
        index = len(self.copies)
        copy = pltpu.make_async_remote_copy(
            src_ref=src,
            dst_ref=dst,
            send_sem=self.send_sems.at[index],
            recv_sem=self.recv_sems.at[index],
            device_id=device,
            device_id_type=MESH,
        )
        copy.start()
        self.copies.append(copy)
        return copy

    def drain(self):
        for copy in self.copies:
            copy.wait_send()


def halves(ref):
    size = ref.shape[0] // 2
    return ref.at[pl.ds(0, size)], ref.at[pl.ds(size, size)]


def ring_reduce(wires, src, n, me, right, left, slots, total):
    far = n // 2
    pending = {}
    for way in (0, 1):
        there, sign = (right, 1) if way == 0 else (left, -1)
        first = lax.rem(me + far, n)
        pending[way, way] = wires.send(
            halves(src.at[first])[way], halves(slots.at[way, 0])[way], there
        )
    for way in (0, 1):
        there, sign = (right, 1) if way == 0 else (left, -1)
        dest = lax.rem(me + sign * (far - 1) + n, n)
        pending[way, 1 - way] = wires.send(
            halves(src.at[dest])[1 - way], halves(slots.at[way, 1])[1 - way], there
        )
    for step in range(1, far):
        subs = [0] if step == 1 else [1, 0]
        for swap in subs:
            for way in (0, 1):
                sub = swap ^ way
                there, sign = (right, 1) if way == 0 else (left, -1)
                dest = lax.rem(me + sign * (far - step) + n, n)
                yield
                pending[way, sub].wait_recv()
                slot = halves(slots.at[way, step - 1])[sub]
                slot[...] = slot[...] + halves(src.at[dest])[sub][...]
                pending[way, sub] = wires.send(slot, halves(slots.at[way, step])[sub], there)
    for swap in (1, 0):
        yield
        for way in (0, 1):
            pending[way, swap ^ way].wait_recv()
    total[...] = src[me] + (slots[0, far - 1] + slots[1, far - 1])


def ring_gather(wires, buf, n, me, right, left, arrived=None):
    far = n // 2
    pending = {}
    for sub in (0, 1):
        for way in (0, 1):
            there = right if way == 0 else left
            block = halves(buf.at[me])[sub ^ way]
            pending[way, sub ^ way] = wires.send(block, block, there)
    for step in range(1, far + 1):
        for swap in (0, 1) if step < far else (0,):
            for way in (0, 1):
                sub = swap ^ way
                there, sign = (right, 1) if way == 0 else (left, -1)
                origin = lax.rem(me - sign * step + n, n)
                yield
                pending[way, sub].wait_recv()
                block = halves(buf.at[origin])[sub]
                if step < far - 1 or (step == far - 1 and swap == 0):
                    pending[way, sub] = wires.send(block, block, there)
                if arrived is not None:
                    arrived(block)


def interleave(*streams):
    streams = list(streams)
    while streams:
        for stream in list(streams):
            try:
                next(stream)
            except StopIteration:
                streams.remove(stream)


def neighbours():
    col = lax.axis_index("col")
    y, z = col // NZ, lax.rem(col, NZ)
    at = lambda yy, zz: {"col": lax.rem(yy + NY, NY) * NZ + lax.rem(zz + NZ, NZ)}
    return y, z, at(y + 1, z), at(y - 1, z), at(y, z + 1), at(y, z - 1)


def greet(devices):
    barrier = pltpu.get_barrier_semaphore()
    for device in devices:
        pl.semaphore_signal(barrier, inc=1, device_id=device, device_id_type=MESH)
    pl.semaphore_wait(barrier, len(devices))


def all_reduce_kernel(
    pa, pb, oa, ob, slots_a, slots_b, mid_a, mid_b, slots_a2, slots_b2, send_sems, recv_sems
):
    y, z, y_up, y_down, z_up, z_down = neighbours()
    greet((y_up, y_down, z_up, z_down))
    wires = Wires(send_sems, recv_sems)

    def first():
        yield from ring_reduce(wires, pa, NZ, z, z_up, z_down, slots_a, mid_a)
        yield from ring_reduce(wires, mid_a, NY, y, y_up, y_down, slots_a2, oa.at[z, y])
        yield from ring_gather(wires, oa.at[z], NY, y, y_up, y_down)
        yield from ring_gather(wires, oa, NZ, z, z_up, z_down)

    def second():
        yield from ring_reduce(wires, pb, NY, y, y_up, y_down, slots_b, mid_b)
        yield from ring_reduce(wires, mid_b, NZ, z, z_up, z_down, slots_b2, ob.at[y, z])
        yield from ring_gather(wires, ob.at[y], NZ, z, z_up, z_down)
        yield from ring_gather(wires, ob, NY, y, y_up, y_down)

    interleave(first(), second())
    wires.drain()


def all_reduce(pa, pb):
    chunk = pa.shape[2:]
    return pl.pallas_call(
        all_reduce_kernel,
        out_shape=(jax.ShapeDtypeStruct(pa.shape, F32), jax.ShapeDtypeStruct(pb.shape, F32)),
        in_specs=[VMEM, VMEM],
        out_specs=(VMEM, VMEM),
        scratch_shapes=[
            pltpu.VMEM((2, NZ // 2, NY) + chunk, F32),
            pltpu.VMEM((2, NY // 2, NZ) + chunk, F32),
            pltpu.VMEM((NY,) + chunk, F32),
            pltpu.VMEM((NZ,) + chunk, F32),
            pltpu.VMEM((2, NY // 2) + chunk, F32),
            pltpu.VMEM((2, NZ // 2) + chunk, F32),
            pltpu.SemaphoreType.DMA((96,)),
            pltpu.SemaphoreType.DMA((96,)),
        ],
        compiler_params=pltpu.CompilerParams(
            collective_id=0, has_side_effects=True, vmem_limit_bytes=LIMIT
        ),
    )(pa, pb)


def gram_kernel(oa, ob, g_ref):
    col = lax.axis_index("col")
    y, z = col // NZ, lax.rem(col, NZ)
    rows = 2 * NY * oa.shape[2]

    def block(index):
        first = oa[index].reshape(rows // 2, LANES)
        second = jnp.concatenate([ob[yy, index] for yy in range(NY)], axis=0)
        return split(jnp.concatenate([first, second], axis=0))

    right = block(z)
    for h in (0, 1):
        g_ref[h] = mm_pair(block(2 * y + h), right, 0, 0)


def gram_block(oa, ob):
    return pl.pallas_call(
        gram_kernel,
        out_shape=jax.ShapeDtypeStruct((2, LANES, LANES), F32),
        in_specs=[VMEM, VMEM],
        out_specs=VMEM,
        compiler_params=pltpu.CompilerParams(vmem_limit_bytes=LIMIT),
    )(oa, ob)


def gram_gather_kernel(g, ga, gb, theirs, mine, slots, send_sems, recv_sems):
    y, z, y_up, y_down, z_up, z_down = neighbours()
    row = lax.axis_index("row")
    x, core = row // 2, lax.rem(row, 2)
    sibling = {"row": x * 2 + (1 - core)}
    others = [{"row": lax.rem(x + step, NX) * 2 + core} for step in range(1, NX)]
    greet([y_up, y_down, z_up, z_down, sibling] + others)
    wires = Wires(send_sems, recv_sems)
    wires.send(g.at[1 - core], theirs, sibling).wait_recv()
    mine[...] = g[core] + theirs[...]
    copies = [
        wires.send(mine, slots.at[step], device) for step, device in enumerate(others)
    ]
    for copy in copies:
        copy.wait_recv()
    total = (mine[...] + slots[1]) + (slots[0] + slots[2])
    half = LANES // 2
    ga[core, z, y] = total[:half]
    gb[core, y, z] = total[half:]
    relayed = []

    def relay(block):
        relayed.append(wires.send(block, block, sibling))

    def first():
        yield from ring_gather(wires, ga.at[core, z], NY, y, y_up, y_down)
        relay(ga.at[core, z])
        yield from ring_gather(wires, ga.at[core], NZ, z, z_up, z_down, relay)

    def second():
        yield from ring_gather(wires, gb.at[core, y], NZ, z, z_up, z_down)
        relay(gb.at[core, y])
        yield from ring_gather(wires, gb.at[core], NY, y, y_up, y_down, relay)

    interleave(first(), second())
    for copy in relayed:
        copy.wait_recv()
    wires.drain()


def gram_gather(g):
    half = LANES // 2
    return pl.pallas_call(
        gram_gather_kernel,
        out_shape=(
            jax.ShapeDtypeStruct((2, NZ, NY, half, LANES), F32),
            jax.ShapeDtypeStruct((2, NY, NZ, half, LANES), F32),
        ),
        in_specs=[VMEM],
        out_specs=(VMEM, VMEM),
        scratch_shapes=[
            pltpu.VMEM((LANES, LANES), F32),
            pltpu.VMEM((LANES, LANES), F32),
            pltpu.VMEM((NX - 1, LANES, LANES), F32),
            pltpu.SemaphoreType.DMA((80,)),
            pltpu.SemaphoreType.DMA((80,)),
        ],
        compiler_params=pltpu.CompilerParams(
            collective_id=1, has_side_effects=True, vmem_limit_bytes=LIMIT
        ),
    )(g)


STEPS = 4
CONVERGED = 4e-4


def load_gram(ga, gb, m):
    half = LANES // 2
    for h in range(2):
        for y in range(NY):
            low = (2 * y + h) * LANES
            for z in range(NZ):
                columns = slice(z * LANES, (z + 1) * LANES)
                m[low:low + half, columns] = ga[h, z, y]
                m[low + half:low + LANES, columns] = gb[h, y, z]


def factor_kernel(ga, gb, x_ref, m, *, nb):
    n = m.shape[0]
    rows = lax.broadcasted_iota(jnp.int32, (nb, nb), 0)
    cols = lax.broadcasted_iota(jnp.int32, (nb, nb), 1)
    eye = (rows == cols).astype(F32)
    half = jnp.where(rows > cols, 1.0, jnp.where(rows == cols, 0.5, 0.0)).astype(F32)
    load_gram(ga, gb, m)
    worst = jnp.zeros((1, nb), F32)
    for low in range(0, n, nb):
        high = low + nb
        block = m[low:high, low:high]
        down = lax.rsqrt(jnp.sum(block * eye, axis=1, keepdims=True))
        across = lax.rsqrt(jnp.sum(block * eye, axis=0, keepdims=True))
        block = block * down * across
        x = eye - half * (block - eye)
        for step in range(STEPS + 2):
            dot = mm1 if step < STEPS else mm3
            residual = dot(dot(x, block, 1, 0), x, 1, 1) - eye
            x = x - dot(half * residual, x, 1, 0)
        off = jnp.where(jnp.abs(residual) < CONVERGED, 0.0, 1.0)
        worst = jnp.maximum(worst, jnp.max(off, axis=0, keepdims=True))
        x = x * across
        m[low:high, low:high] = eye
        pivot = mm3(x, m[low:high, :], 1, 0)
        keep = lax.broadcasted_iota(jnp.int32, (nb, n), 1) < high
        x_ref[low:high, :] = jnp.where(keep, pivot, 0.0)
        if high < n:
            m[high:, low:high] = jnp.zeros((n - high, nb), F32)
            pair = split(pivot)
            m[high:, :] = m[high:, :] - mm_pair(
                (pair[0][:, high:], pair[1][:, high:]), pair, 0, 0
            )

    @pl.when(jnp.max(worst) > 0.0)
    def _():
        load_gram(ga, gb, m)
        lane = lax.broadcasted_iota(jnp.int32, (1, n), 1)
        chunk = 128

        def column(j, carry):
            row = m[pl.ds(j, 1), :]
            scale = lax.rsqrt(jnp.sum(jnp.where(lane == j, row, 0.0), axis=1, keepdims=True))
            pivot = jnp.where(lane == j, 1.0, row) * scale
            x_ref[pl.ds(j, 1), :] = jnp.where(lane <= j, pivot, 0.0)

            def update(part, carry):
                here = pl.ds(pl.multiple_of(part * chunk, chunk), chunk)
                below = part * chunk + lax.broadcasted_iota(jnp.int32, (chunk, 1), 0) > j
                old = m[here, :]
                factor = jnp.sum(jnp.where(lane == j, old, 0.0), axis=1, keepdims=True) * scale
                new = jnp.where(lane == j, 0.0, old) - factor * pivot
                m[here, :] = jnp.where(below, new, old)
                return carry

            return lax.fori_loop(j // chunk, n // chunk, update, carry)

        lax.fori_loop(0, n, column, 0)


def inverse_factor(ga, gb, nb=256):
    n = NZ * LANES
    return pl.pallas_call(
        functools.partial(factor_kernel, nb=nb),
        out_shape=jax.ShapeDtypeStruct((n, n), F32),
        in_specs=[VMEM, VMEM],
        out_specs=VMEM,
        scratch_shapes=[pltpu.VMEM((n, n), F32)],
        compiler_params=pltpu.CompilerParams(vmem_limit_bytes=LIMIT),
    )(ga, gb)


def outputs_kernel(oa, ob, x_ref, a_ref, basis_ref, proj_ref, sh, sl, ah, al, *, root):
    piece = oa.shape[2]
    for y in range(NY):
        for z in range(NZ):
            columns = slice(z * LANES, (z + 1) * LANES)
            low = 2 * y * piece
            sh[low:low + piece, columns], sl[low:low + piece, columns] = split(oa[z, y])
            low += piece
            sh[low:low + piece, columns], sl[low:low + piece, columns] = split(ob[y, z])
    ah[...], al[...] = split(a_ref[...])
    wide = 256
    for low in range(0, x_ref.shape[0], wide):
        high = low + wide
        pair = split(x_ref[low:high, :high])
        basis = mm_pair((sh[:, :high], sl[:, :high]), pair, 1, 1)
        basis_ref[:, low:high] = basis * root
        proj_ref[low:high, :] = mm_pair(split(basis), (ah[...], al[...]), 0, 0)


def outputs(oa, ob, x, a, root):
    rows, cols = a.shape
    n = x.shape[0]
    return pl.pallas_call(
        functools.partial(outputs_kernel, root=root),
        out_shape=(jax.ShapeDtypeStruct((rows, n), F32), jax.ShapeDtypeStruct((n, cols), F32)),
        in_specs=[VMEM] * 4,
        out_specs=(VMEM, VMEM),
        scratch_shapes=[pltpu.VMEM((rows, n), BF16)] * 2 + [pltpu.VMEM((rows, cols), BF16)] * 2,
        compiler_params=pltpu.CompilerParams(vmem_limit_bytes=LIMIT),
    )(oa, ob, x, a)


def body(expert_matrix, col_signs, sample_ids):
    local_cols = expert_matrix.shape[1]
    col_total = local_cols * lax.axis_size("col")
    model_width = expert_matrix.shape[0] * lax.axis_size("row")
    pa, pb = sketch(
        expert_matrix, col_signs[None, :], sample_ids[None, :], 1.0 / math.sqrt(col_total)
    )
    oa, ob = all_reduce(pa, pb)
    ga, gb = gram_gather(gram_block(oa, ob))
    inverse = inverse_factor(ga, gb)
    basis, partial = outputs(oa, ob, inverse, expert_matrix, math.sqrt(model_width))
    projected = lax.psum_scatter(partial, "row", scatter_dimension=0, tiled=True)
    return basis, projected


def solution(mesh):
    in_specs = (P("row", "col"), P("col"), P())
    out_specs = (P("row", None), P("row", "col"))
    return jax.shard_map(body, mesh=mesh, in_specs=in_specs, out_specs=out_specs, check_vma=False)
```

```python
import functools
import math

import jax
import jax.numpy as jnp
from jax import lax
from jax.experimental import pallas as pl
from jax.experimental.pallas import tpu as pltpu
from jax.sharding import PartitionSpec as P

MESH = pl.DeviceIdType.MESH
F32 = jnp.float32
BF16 = jnp.bfloat16
NY, NZ, NX = 4, 8, 4
LANES = 128
VMEM = pl.BlockSpec(memory_space=pltpu.VMEM)
LIMIT = 56 << 20


def split(value):
    high = value.astype(BF16)
    return high, (value - high.astype(F32)).astype(BF16)


def mm(a, b, ca, cb):
    return lax.dot_general(a, b, (((ca,), (cb,)), ((), ())), preferred_element_type=F32)


def mm_pair(a, b, ca, cb):
    (ah, al), (bh, bl) = a, b
    return mm(ah, bh, ca, cb) + (mm(ah, bl, ca, cb) + mm(al, bh, ca, cb))


def mm3(a, b, ca, cb):
    return mm_pair(split(a), split(b), ca, cb)


def mm1(a, b, ca, cb):
    return mm(a.astype(BF16), b.astype(BF16), ca, cb)


GROUPS = 4
ROWS_A, ROWS_B = 24, 32
PERIOD = GROUPS * (ROWS_A + ROWS_B)


def place(group, y, first):
    offset = group * ROWS_A if first else GROUPS * ROWS_A + group * ROWS_B
    low = y * PERIOD + offset
    return slice(low, low + (ROWS_A if first else ROWS_B))


def sketch_kernel(a_ref, signs_ref, ids_ref, pa_ref, pb_ref, top_ref, ah, al, *, scale):
    rows, cols = a_ref.shape
    offset = lax.axis_index("col") * cols
    signed = a_ref[...] * signs_ref[...].astype(F32)
    top_ref[...] = jnp.max(jnp.abs(signed).reshape(rows // 8, 8, cols), axis=0)
    ah[...], al[...] = split(signed)
    wide = 256
    for part in range(ids_ref.shape[1] // wide):
        ids = ids_ref[:, part * wide:(part + 1) * wide]
        col_ids = offset + lax.broadcasted_iota(jnp.int32, (cols, wide), 0)
        parity = lax.population_count(col_ids & ids) & 1
        table = (1 - 2 * parity).astype(F32).astype(BF16)
        out = (mm(ah[...], table, 1, 0) + mm(al[...], table, 1, 0)) * scale
        for sub in range(wide // LANES):
            block = part * (wide // LANES) + sub
            piece = out[:, sub * LANES:(sub + 1) * LANES]
            for group in range(GROUPS):
                for y in range(NY):
                    pa_ref[group, block, y] = piece[place(group, y, True)]
                    pb_ref[group, y, block] = piece[place(group, y, False)]


def sketch(a, signs, ids, scale):
    rows, cols = a.shape
    return pl.pallas_call(
        functools.partial(sketch_kernel, scale=scale),
        out_shape=(
            jax.ShapeDtypeStruct((GROUPS, NZ, NY, ROWS_A, LANES), F32),
            jax.ShapeDtypeStruct((GROUPS, NY, NZ, ROWS_B, LANES), F32),
            jax.ShapeDtypeStruct((8, cols), F32),
        ),
        in_specs=[VMEM] * 3,
        out_specs=(VMEM,) * 3,
        scratch_shapes=[pltpu.VMEM((rows, cols), BF16), pltpu.VMEM((rows, cols), BF16)],
        compiler_params=pltpu.CompilerParams(vmem_limit_bytes=LIMIT),
    )(a, signs, ids)


class Wires:
    def __init__(self, send_sems, recv_sems):
        self.send_sems, self.recv_sems = send_sems, recv_sems
        self.copies = []

    def send(self, src, dst, device):
        index = len(self.copies)
        copy = pltpu.make_async_remote_copy(
            src_ref=src,
            dst_ref=dst,
            send_sem=self.send_sems.at[index],
            recv_sem=self.recv_sems.at[index],
            device_id=device,
            device_id_type=MESH,
        )
        copy.start()
        self.copies.append(copy)
        return copy

    def drain(self):
        for copy in self.copies:
            copy.wait_send()


def ring_reduce(wires, src, n, me, right, left, slots, total, long=0, ready=None):
    far = n // 2
    ways = []
    for way, (there, sign) in enumerate(((right, 1), (left, -1))):
        hops = far if way == long else far - 1
        ways.append((there, sign, hops, 0 if way == long else far))
    ways.sort(key=lambda way: -way[2])
    pending = [None, None]
    for step in range(far):
        for index, (there, sign, hops, base) in enumerate(ways):
            turn = step - (far - hops)
            if turn < 0:
                continue
            dest = lax.rem(me + sign * (hops - turn) + n, n)
            if ready is not None:
                yield from ready(sign * (hops - turn) % n)
            block = src.at[dest]
            if turn > 0:
                yield pending[index]
                pending[index].wait_recv()
                block = slots.at[base + turn - 1]
                block[...] = block[...] + src[dest]
            pending[index] = wires.send(block, slots.at[base + turn], there)
    if ready is not None:
        yield from ready(0)
    for copy in pending:
        yield copy
        copy.wait_recv()
    total[...] = src[me] + (slots[far - 1] + slots[n - 2])


def ring_gather(wires, buf, n, me, right, left, long=0, arrived=None):
    far = n // 2
    ways = ((right, 1, far if long == 0 else far - 1), (left, -1, far if long == 1 else far - 1))
    pending = [wires.send(buf.at[me], buf.at[me], there) for there, _, _ in ways]
    for step in range(1, far + 1):
        for index, (there, sign, hops) in enumerate(ways):
            if step > hops:
                continue
            origin = lax.rem(me - sign * step + n, n)
            yield pending[index]
            pending[index].wait_recv()
            block = buf.at[origin]
            if step < hops:
                pending[index] = wires.send(block, block, there)
            if arrived is not None:
                arrived(block)


def interleave(streams, order):
    streams = list(streams)
    for index in order:
        next(streams[index], None)
    alive = list(streams)
    while alive:
        alive = [stream for stream in alive if next(stream, alive) is not alive]


def neighbours():
    col = lax.axis_index("col")
    y, z = col // NZ, lax.rem(col, NZ)
    at = lambda yy, zz: {"col": lax.rem(yy + NY, NY) * NZ + lax.rem(zz + NZ, NZ)}
    return y, z, at(y + 1, z), at(y - 1, z), at(y, z + 1), at(y, z - 1)


def greet(devices):
    barrier = pltpu.get_barrier_semaphore()
    for device in devices:
        pl.semaphore_signal(barrier, inc=1, device_id=device, device_id_type=MESH)
    pl.semaphore_wait(barrier, len(devices))


def sketch_streams(wires, where, pa, pb, oa, ob, slots_a, slots_b, mid_a, mid_b, tail_a, tail_b):
    y, z, y_up, y_down, z_up, z_down = where

    def first(g):
        long = g % 2
        yield from ring_reduce(
            wires, pa.at[g], NZ, z, z_up, z_down, slots_a.at[g], mid_a.at[g], long
        )
        yield from ring_reduce(
            wires, mid_a.at[g], NY, y, y_up, y_down, tail_a.at[g], oa.at[g, z, y], long
        )
        yield from ring_gather(wires, oa.at[g, z], NY, y, y_up, y_down, long)
        yield from ring_gather(wires, oa.at[g], NZ, z, z_up, z_down, long)

    def second(g):
        long = g % 2
        yield from ring_reduce(
            wires, pb.at[g], NY, y, y_up, y_down, slots_b.at[g], mid_b.at[g], long
        )
        yield from ring_reduce(
            wires, mid_b.at[g], NZ, z, z_up, z_down, tail_b.at[g], ob.at[g, y, z], long
        )
        yield from ring_gather(wires, ob.at[g, y], NZ, z, z_up, z_down, long)
        yield from ring_gather(wires, ob.at[g], NY, y, y_up, y_down, long)

    return [stream(g) for g in range(GROUPS) for stream in (first, second)]


QUARTER = LANES // 4


def gram_streams(wires, where, core, sibling, others, g, theirs, mine, slots, ga, gb):
    y, z, y_up, y_down, z_up, z_down = where

    def relay(block):
        wires.relayed.append(wires.send(block, block, sibling))

    def start():
        copy = wires.send(g.at[1 - core], theirs, sibling)
        yield copy
        copy.wait_recv()
        mine[...] = g[core] + theirs[...]
        copies = [
            wires.send(mine, slots.at[step], device) for step, device in enumerate(others)
        ]
        for copy in copies:
            yield copy
            copy.wait_recv()
        total = (mine[...] + slots[1]) + (slots[0] + slots[2])
        for h in (0, 1):
            ga[core, h, z, y] = total[h * QUARTER:(h + 1) * QUARTER]
            gb[core, h, y, z] = total[(2 + h) * QUARTER:(3 + h) * QUARTER]
        wires.begun.append(True)

    def first(h):
        while not wires.begun:
            yield None
        yield from ring_gather(wires, ga.at[core, h, z], NY, y, y_up, y_down, h)
        relay(ga.at[core, h, z])
        yield from ring_gather(wires, ga.at[core, h], NZ, z, z_up, z_down, h, relay)

    def second(h):
        while not wires.begun:
            yield None
        yield from ring_gather(wires, gb.at[core, h, y], NZ, z, z_up, z_down, h)
        relay(gb.at[core, h, y])
        yield from ring_gather(wires, gb.at[core, h], NY, y, y_up, y_down, h, relay)

    return [start(), first(0), second(0), first(1), second(1)]


def weight_streams(wires, x, sibling, right, left, compute, src, stage, inbox, slots, total):
    order = (2, 1, 3, 0)
    sent, merged = [], []

    def ready(offset):
        turn = order.index(offset)
        while len(sent) < min(turn + 2, NX):
            dest = lax.rem(x + order[len(sent)], NX)
            compute(dest)
            sent.append(wires.send(stage.at[dest], inbox.at[dest], sibling))
            yield None
        if offset not in merged:
            merged.append(offset)
            sent[turn].wait_recv()
            dest = lax.rem(x + offset, NX)
            for h in (0, 1):
                src[h, dest] = src[h, dest] + inbox[dest, h]

    return [
        ring_reduce(wires, src.at[h], NX, x, right, left, slots.at[h], total.at[h], h, ready)
        for h in (0, 1)
    ]


def reduce_kernel(
    pa, pb, top, a_ref, sh, sl, ga, gb, wt, tops_out,
    oa, ob, slots_a, slots_b, mid_a, mid_b, tail_a, tail_b,
    g_ref, theirs, mine, slots_g, tops, src, stage, inbox, slots_w, send_sems, recv_sems,
):
    where = neighbours()
    y, z = where[:2]
    row = lax.axis_index("row")
    x, core = row // 2, lax.rem(row, 2)
    at = lambda xx, cc: {"row": lax.rem(xx, NX) * 2 + cc}
    sibling = at(x, 1 - core)
    others = [at(x + step, core) for step in range(1, NX)]
    crossed = [at(x + step, 1 - core) for step in range(1, NX)]
    greet(list(where[2:]) + [sibling] + others + crossed)
    wires = Wires(send_sems, recv_sems)
    wires.relayed, wires.begun = [], []
    told = [
        wires.send(top, tops.at[index], device)
        for index, device in enumerate([sibling] + others + crossed)
    ]
    interleave(
        sketch_streams(
            wires, where, pa, pb, oa, ob, slots_a, slots_b, mid_a, mid_b, tail_a, tail_b
        ),
        SKETCH_ORDER,
    )

    def block(index):
        parts = [oa[g, index, yy] for g in range(GROUPS) for yy in range(NY)]
        parts += [ob[g, yy, index] for g in range(GROUPS) for yy in range(NY)]
        return split(jnp.concatenate(parts, axis=0))

    right = block(z)
    for h in (0, 1):
        g_ref[h] = mm_pair(block(2 * y + h), right, 0, 0)

    for copy in told:
        copy.wait_recv()
    most = top[...]
    for index in range(len(told)):
        most = jnp.maximum(most, tops[index])
    most = jnp.maximum(jnp.max(most, axis=0, keepdims=True), 1e-30)
    stretch = 1.0 / most
    tops[0] = jnp.broadcast_to(most, top.shape)
    tops[1] = jnp.broadcast_to(stretch, top.shape)
    tops_out[...] = tops[0, :, pl.ds(pl.multiple_of(row * LANES, LANES), LANES)]

    def assemble():
        for yy in range(NY):
            low = yy * PERIOD
            middle, high = low + GROUPS * ROWS_A, low + PERIOD
            for zz in range(NZ):
                columns = slice(zz * LANES, (zz + 1) * LANES)
                first = jnp.concatenate([oa[g, zz, yy] for g in range(GROUPS)], axis=0)
                sh[low:middle, columns], sl[low:middle, columns] = split(first)
                second = jnp.concatenate([ob[g, yy, zz] for g in range(GROUPS)], axis=0)
                sh[middle:high, columns], sl[middle:high, columns] = split(second)

    def compute(dest):
        columns = pl.ds(pl.multiple_of(dest * 2 * LANES, 2 * LANES), 2 * LANES)
        part = a_ref[:, columns] * tops[1, 0:1, columns]
        out = mm_pair(split(part), (sh[...], sl[...]), 0, 0)
        ours = jnp.where(core == 0, out[:LANES], out[LANES:])
        theirs = jnp.where(core == 0, out[LANES:], out[:LANES])
        half = LANES // 2
        for h in (0, 1):
            src[h, dest] = ours[h * half:(h + 1) * half]
            stage[dest, h] = theirs[h * half:(h + 1) * half]

    streams = gram_streams(
        wires, where, core, sibling, others, g_ref, theirs, mine, slots_g, ga, gb
    )
    next(streams[0])
    assemble()
    streams += weight_streams(
        wires, x, sibling, others[0], others[2], compute, src, stage, inbox, slots_w, wt
    )
    interleave(streams, GRAM_ORDER)
    for copy in wires.relayed:
        copy.wait_recv()
    wires.drain()


SKETCH_ORDER = (
    0, 1, 2, 3, 4, 5, 6, 0, 2, 7, 4, 6, 1, 0, 0, 2, 3, 2, 4, 0, 0, 1, 1, 5, 2, 2, 4, 0,
    4, 0, 1, 6, 3, 3, 7, 2, 2, 6, 4, 1, 1, 4, 6, 0, 5, 5, 3, 6, 1, 4, 1, 7, 5, 7, 2, 0,
    0, 6, 3, 3, 4, 6, 1, 1, 2, 2, 5, 5, 7, 0, 0, 3, 3, 4, 4, 6, 1, 1, 2, 2, 5, 5, 0, 7,
    4, 4, 3, 3, 6, 6, 1, 7, 1, 2, 4, 6, 6, 3, 1, 3, 1, 5, 5, 6, 7, 7, 0, 3, 3, 1, 5, 5,
    0, 2, 7, 7, 2, 0, 3, 3, 5, 5, 0, 1, 2, 7, 7, 2, 3, 0, 5, 5, 4, 7, 7, 0, 2, 4, 2, 1,
    1, 5, 0, 6, 6, 7, 7, 4, 4, 3, 3, 2, 6, 6, 7, 4, 4, 6, 6, 4, 3, 5, 6, 5, 7, 7, 5, 7,
)
GRAM_ORDER = (
    0, 1, 2, 3, 4, 5, 6, 0, 0, 0, 1, 2, 3, 4, 5, 1, 1, 2, 2, 3, 3, 4, 4, 5, 6, 1, 2, 2,
    3, 4, 4, 6, 1, 1, 2, 2, 5, 3, 3, 4, 4, 6, 1, 1, 2, 3, 3, 4, 1, 1, 5, 2, 3, 2, 3, 5,
    1, 4, 4, 3, 2, 6, 6, 4,
)
COPIES = 300


def reduce_all(pa, pb, top, a):
    rows, cols = a.shape
    samples = NZ * LANES
    half = LANES // 2
    array = lambda *shape: pltpu.VMEM(shape, F32)
    return pl.pallas_call(
        reduce_kernel,
        out_shape=(
            jax.ShapeDtypeStruct((rows, samples), BF16),
            jax.ShapeDtypeStruct((rows, samples), BF16),
            jax.ShapeDtypeStruct((2, 2, NZ, NY, QUARTER, LANES), F32),
            jax.ShapeDtypeStruct((2, 2, NY, NZ, QUARTER, LANES), F32),
            jax.ShapeDtypeStruct((2, half, samples), F32),
            jax.ShapeDtypeStruct((8, LANES), F32),
        ),
        in_specs=[VMEM] * 4,
        out_specs=(VMEM,) * 6,
        scratch_shapes=[
            array(*pa.shape),
            array(*pb.shape),
            array(GROUPS, NZ - 1, NY, ROWS_A, LANES),
            array(GROUPS, NY - 1, NZ, ROWS_B, LANES),
            array(GROUPS, NY, ROWS_A, LANES),
            array(GROUPS, NZ, ROWS_B, LANES),
            array(GROUPS, NY - 1, ROWS_A, LANES),
            array(GROUPS, NZ - 1, ROWS_B, LANES),
            array(2, LANES, LANES),
            array(LANES, LANES),
            array(LANES, LANES),
            array(NX - 1, LANES, LANES),
            array(2 * NX - 1, 8, cols),
            array(2, NX, half, samples),
            array(NX, 2, half, samples),
            array(NX, 2, half, samples),
            array(2, NX - 1, half, samples),
            pltpu.SemaphoreType.DMA((COPIES,)),
            pltpu.SemaphoreType.DMA((COPIES,)),
        ],
        compiler_params=pltpu.CompilerParams(
            collective_id=0, has_side_effects=True, vmem_limit_bytes=LIMIT
        ),
    )(pa, pb, top, a)


STEPS = 4
CONVERGED = 4e-4


def load_gram(ga, gb, m):
    for core in range(2):
        for y in range(NY):
            for z in range(NZ):
                columns = slice(z * LANES, (z + 1) * LANES)
                pieces = [ga[core, h, z, y] for h in (0, 1)] + [gb[core, h, y, z] for h in (0, 1)]
                for index, piece in enumerate(pieces):
                    low = (2 * y + core) * LANES + index * QUARTER
                    m[low:low + QUARTER, columns] = piece


def factor_kernel(ga, gb, xh, xl, m, *, nb):
    n = m.shape[0]
    rows = lax.broadcasted_iota(jnp.int32, (nb, nb), 0)
    cols = lax.broadcasted_iota(jnp.int32, (nb, nb), 1)
    eye = (rows == cols).astype(F32)
    half = jnp.where(rows > cols, 1.0, jnp.where(rows == cols, 0.5, 0.0)).astype(F32)
    load_gram(ga, gb, m)
    worst = jnp.zeros((1, nb), F32)
    for low in range(0, n, nb):
        high = low + nb
        block = m[low:high, low:high]
        down = lax.rsqrt(jnp.sum(block * eye, axis=1, keepdims=True))
        across = lax.rsqrt(jnp.sum(block * eye, axis=0, keepdims=True))
        block = block * down * across
        x = eye - half * (block - eye)
        for step in range(STEPS + 2):
            dot = mm1 if step < STEPS else mm3
            residual = dot(dot(x, block, 1, 0), x, 1, 1) - eye
            x = x - dot(half * residual, x, 1, 0)
        off = jnp.where(jnp.abs(residual) < CONVERGED, 0.0, 1.0)
        worst = jnp.maximum(worst, jnp.max(off, axis=0, keepdims=True))
        x = x * across
        m[low:high, low:high] = eye
        pivot = mm3(x, m[low:high, :], 1, 0)
        keep = lax.broadcasted_iota(jnp.int32, (nb, n), 1) < high
        pair = split(pivot)
        xh[low:high, :] = jnp.where(keep, pair[0], 0)
        xl[low:high, :] = jnp.where(keep, pair[1], 0)
        if high < n:
            m[high:, low:high] = jnp.zeros((n - high, nb), F32)
            m[high:, :] = m[high:, :] - mm_pair(
                (pair[0][:, high:], pair[1][:, high:]), pair, 0, 0
            )

    @pl.when(jnp.max(worst) > 0.0)
    def _():
        load_gram(ga, gb, m)
        lane = lax.broadcasted_iota(jnp.int32, (1, n), 1)
        chunk = 128

        def column(j, carry):
            row = m[pl.ds(j, 1), :]
            scale = lax.rsqrt(jnp.sum(jnp.where(lane == j, row, 0.0), axis=1, keepdims=True))
            pivot = jnp.where(lane == j, 1.0, row) * scale
            m[pl.ds(j, 1), :] = jnp.where(lane <= j, pivot, 0.0)

            def update(part, carry):
                here = pl.ds(pl.multiple_of(part * chunk, chunk), chunk)
                below = part * chunk + lax.broadcasted_iota(jnp.int32, (chunk, 1), 0) > j
                old = m[here, :]
                factor = jnp.sum(jnp.where(lane == j, old, 0.0), axis=1, keepdims=True) * scale
                new = jnp.where(lane == j, 0.0, old) - factor * pivot
                m[here, :] = jnp.where(below, new, old)
                return carry

            return lax.fori_loop(j // chunk, n // chunk, update, carry)

        lax.fori_loop(0, n, column, 0)
        xh[...], xl[...] = split(m[...])


def inverse_factor(ga, gb, nb=256):
    n = NZ * LANES
    return pl.pallas_call(
        functools.partial(factor_kernel, nb=nb),
        out_shape=(jax.ShapeDtypeStruct((n, n), BF16),) * 2,
        in_specs=[VMEM, VMEM],
        out_specs=(VMEM, VMEM),
        scratch_shapes=[pltpu.VMEM((n, n), F32)],
        compiler_params=pltpu.CompilerParams(vmem_limit_bytes=LIMIT),
    )(ga, gb)


def outputs_kernel(
    sh, sl, xh, xl, wt, tops, basis_ref, proj_ref, stage, inbox, send_sems, recv_sems
):
    row = lax.axis_index("row")
    count = 2 * NX
    peers = [lax.rem(row + step, count) for step in range(1, count)]
    greet([{"row": peer} for peer in peers])
    n = xh.shape[0]
    wide = 256
    pair = split(wt[...].reshape(LANES, xh.shape[0]))
    for low in range(0, n, wide):
        high = low + wide
        out = mm_pair(
            (xh[low:high, :high], xl[low:high, :high]), (pair[0][:, :high], pair[1][:, :high]), 1, 1
        )
        out = out * tops[0:1, :]
        for sub in range(wide // LANES):
            stage[low // LANES + sub] = out[sub * LANES:(sub + 1) * LANES]
    copies = []
    for index, peer in enumerate(peers):
        copy = pltpu.make_async_remote_copy(
            src_ref=stage.at[peer],
            dst_ref=inbox.at[index],
            send_sem=send_sems.at[index],
            recv_sem=recv_sems.at[index],
            device_id={"row": peer},
            device_id_type=MESH,
        )
        copy.start()
        copies.append(copy)
    for low in range(0, n, wide):
        high = low + wide
        basis_ref[:, low:high] = mm_pair(
            (sh[:, :high], sl[:, :high]), (xh[low:high, :high], xl[low:high, :high]), 1, 1
        )
    columns = lambda owner: pl.ds(pl.multiple_of(owner * LANES, LANES), LANES)
    proj_ref[:, columns(row)] = stage[row]
    for index, copy in enumerate(copies):
        copy.wait()
        sender = lax.rem(row - index - 1 + count, count)
        proj_ref[:, columns(sender)] = inbox[index]


def outputs(sh, sl, xh, xl, wt, tops):
    rows, n = sh.shape
    count = 2 * NX
    return pl.pallas_call(
        outputs_kernel,
        out_shape=(
            jax.ShapeDtypeStruct((rows, n), F32),
            jax.ShapeDtypeStruct((n // count, count * LANES), F32),
        ),
        in_specs=[VMEM] * 6,
        out_specs=(VMEM, VMEM),
        scratch_shapes=[
            pltpu.VMEM((count, LANES, LANES), F32),
            pltpu.VMEM((count - 1, LANES, LANES), F32),
            pltpu.SemaphoreType.DMA((count - 1,)),
            pltpu.SemaphoreType.DMA((count - 1,)),
        ],
        compiler_params=pltpu.CompilerParams(
            collective_id=1, has_side_effects=True, vmem_limit_bytes=LIMIT
        ),
    )(sh, sl, xh, xl, wt, tops)


def body(expert_matrix, col_signs, sample_ids):
    local_cols = expert_matrix.shape[1]
    col_total = local_cols * lax.axis_size("col")
    model_width = expert_matrix.shape[0] * lax.axis_size("row")
    pa, pb, top = sketch(
        expert_matrix, col_signs[None, :], sample_ids[None, :], 1.0 / math.sqrt(col_total)
    )
    sh, sl, ga, gb, wt, tops = reduce_all(pa, pb, top, expert_matrix)
    xh, xl = inverse_factor(ga, gb)
    basis, projected = outputs(sh, sl, xh, xl, wt, tops)
    return basis * math.sqrt(model_width), projected


def solution(mesh):
    in_specs = (P("row", "col"), P("col"), P())
    out_specs = (P("row", None), P("row", "col"))
    return jax.shard_map(body, mesh=mesh, in_specs=in_specs, out_specs=out_specs, check_vma=False)
```

```python
import functools
import math

import jax
import jax.numpy as jnp
from jax import lax
from jax.experimental import pallas as pl
from jax.experimental.pallas import tpu as pltpu
from jax.sharding import PartitionSpec as P

MESH = pl.DeviceIdType.MESH
F32 = jnp.float32
BF16 = jnp.bfloat16
NY, NZ, NX = 4, 8, 4
LANES = 128
VMEM = pl.BlockSpec(memory_space=pltpu.VMEM)
MEGA_LIMIT = 40 << 20
GUARD_LIMIT = 20 << 20
OUTPUT_LIMIT = 16 << 20


def split(value):
    high = value.astype(BF16)
    return high, (value - high.astype(F32)).astype(BF16)


def mm(a, b, ca, cb):
    return lax.dot_general(a, b, (((ca,), (cb,)), ((), ())), preferred_element_type=F32)


def mm_pair(a, b, ca, cb):
    (ah, al), (bh, bl) = a, b
    return mm(ah, bh, ca, cb) + (mm(ah, bl, ca, cb) + mm(al, bh, ca, cb))


def mm3(a, b, ca, cb):
    return mm_pair(split(a), split(b), ca, cb)


def mm1(a, b, ca, cb):
    return mm(a.astype(BF16), b.astype(BF16), ca, cb)


GROUPS = 4
ROWS_A, ROWS_B = 24, 32
PERIOD = GROUPS * (ROWS_A + ROWS_B)


def signs_of(value):
    for amount in (8, 4, 2, 1):
        value = value ^ (value >> amount)
    return (1 - 2 * (value & 1)).astype(F32)


def fill_table(table, ids, offset):
    cols, samples = table.shape
    step = 32
    index = lax.broadcasted_iota(jnp.int32, (step, samples), 0)
    low = signs_of(index & ids)
    high = signs_of((offset + step * index) & ids)
    for part in range(cols // step):
        table[part * step:(part + 1) * step, :] = (low * high[part:part + 1, :]).astype(BF16)


def sketch_group(g, a_ref, signs, table, pa, pb, scale):
    size = ROWS_A + ROWS_B
    parts = [a_ref[y * PERIOD + g * size:y * PERIOD + (g + 1) * size, :] for y in range(NY)]
    high, low = split(jnp.concatenate(parts, axis=0) * signs)
    wide = 256
    for part in range(table.shape[1] // wide):
        columns = slice(part * wide, (part + 1) * wide)
        out = (mm(high, table[:, columns], 1, 0) + mm(low, table[:, columns], 1, 0)) * scale
        for sub in range(wide // LANES):
            block = part * (wide // LANES) + sub
            for y in range(NY):
                piece = out[y * size:(y + 1) * size, sub * LANES:(sub + 1) * LANES]
                pa[g, block, y] = piece[:ROWS_A]
                pb[g, y, block] = piece[ROWS_A:]


class Wires:
    def __init__(self, send_sems, recv_sems):
        self.send_sems, self.recv_sems = send_sems, recv_sems
        self.copies = []

    def send(self, src, dst, device):
        index = len(self.copies)
        copy = pltpu.make_async_remote_copy(
            src_ref=src,
            dst_ref=dst,
            send_sem=self.send_sems.at[index],
            recv_sem=self.recv_sems.at[index],
            device_id=device,
            device_id_type=MESH,
        )
        copy.start()
        self.copies.append(copy)
        return copy

    def drain(self):
        for copy in self.copies:
            copy.wait_send()


def ring_reduce(wires, src, n, me, right, left, slots, total, long=0, ready=None):
    far = n // 2
    ways = []
    for way, (there, sign) in enumerate(((right, 1), (left, -1))):
        hops = far if way == long else far - 1
        ways.append((there, sign, hops, 0 if way == long else far))
    ways.sort(key=lambda way: -way[2])
    pending = [None, None]
    for step in range(far):
        for index, (there, sign, hops, base) in enumerate(ways):
            turn = step - (far - hops)
            if turn < 0:
                continue
            dest = lax.rem(me + sign * (hops - turn) + n, n)
            if ready is not None:
                yield from ready(sign * (hops - turn) % n)
            block = src.at[dest]
            if turn > 0:
                yield pending[index]
                pending[index].wait_recv()
                block = slots.at[base + turn - 1]
                block[...] = block[...] + src[dest]
            pending[index] = wires.send(block, slots.at[base + turn], there)
    if ready is not None:
        yield from ready(0)
    for copy in pending:
        yield copy
        copy.wait_recv()
    total[...] = src[me] + (slots[far - 1] + slots[n - 2])


def ring_gather(wires, buf, n, me, right, left, long=0, arrived=None):
    far = n // 2
    ways = ((right, 1, far if long == 0 else far - 1), (left, -1, far if long == 1 else far - 1))
    pending = [wires.send(buf.at[me], buf.at[me], there) for there, _, _ in ways]
    for step in range(1, far + 1):
        for index, (there, sign, hops) in enumerate(ways):
            if step > hops:
                continue
            origin = lax.rem(me - sign * step + n, n)
            yield pending[index]
            pending[index].wait_recv()
            block = buf.at[origin]
            if step < hops:
                pending[index] = wires.send(block, block, there)
            if arrived is not None:
                arrived(block)


def interleave(streams, order):
    streams = list(streams)
    for index in order:
        next(streams[index], None)
    alive = [] if order else list(streams)
    while alive:
        alive = [stream for stream in alive if next(stream, alive) is not alive]


def neighbours():
    col = lax.axis_index("col")
    y, z = col // NZ, lax.rem(col, NZ)
    at = lambda yy, zz: {"col": lax.rem(yy + NY, NY) * NZ + lax.rem(zz + NZ, NZ)}
    return y, z, at(y + 1, z), at(y - 1, z), at(y, z + 1), at(y, z - 1)


def greet(devices):
    barrier = pltpu.get_barrier_semaphore()
    for device in devices:
        pl.semaphore_signal(barrier, inc=1, device_id=device, device_id_type=MESH)
    return lambda: pl.semaphore_wait(barrier, len(devices))


def sketch_streams(wires, where, pa, pb, oa, ob, slots_a, slots_b, mid_a, mid_b, tail_a, tail_b):
    y, z, y_up, y_down, z_up, z_down = where

    def first(g):
        long = g % 2
        yield from ring_reduce(
            wires, pa.at[g], NZ, z, z_up, z_down, slots_a.at[g], mid_a.at[g], long
        )
        yield from ring_reduce(
            wires, mid_a.at[g], NY, y, y_up, y_down, tail_a.at[g], oa.at[g, z, y], long
        )
        yield from ring_gather(wires, oa.at[g, z], NY, y, y_up, y_down, long)
        yield from ring_gather(wires, oa.at[g], NZ, z, z_up, z_down, long)

    def second(g):
        long = g % 2
        yield from ring_reduce(
            wires, pb.at[g], NY, y, y_up, y_down, slots_b.at[g], mid_b.at[g], long
        )
        yield from ring_reduce(
            wires, mid_b.at[g], NZ, z, z_up, z_down, tail_b.at[g], ob.at[g, y, z], long
        )
        yield from ring_gather(wires, ob.at[g, y], NZ, z, z_up, z_down, long)
        yield from ring_gather(wires, ob.at[g], NY, y, y_up, y_down, long)

    return [stream(g) for g in range(GROUPS) for stream in (first, second)]


QUARTER = LANES // 4


def gram_streams(wires, where, core, sibling, others, g, theirs, mine, slots, ga, gb):
    y, z, y_up, y_down, z_up, z_down = where

    def relay(block):
        wires.relayed.append(wires.send(block, block, sibling))

    def start():
        copy = wires.send(g.at[1 - core], theirs, sibling)
        yield copy
        copy.wait_recv()
        mine[...] = g[core] + theirs[...]
        copies = [
            wires.send(mine, slots.at[step], device) for step, device in enumerate(others)
        ]
        for copy in copies:
            yield copy
            copy.wait_recv()
        total = (mine[...] + slots[1]) + (slots[0] + slots[2])
        for h in (0, 1):
            ga[core, h, z, y] = total[h * QUARTER:(h + 1) * QUARTER]
            gb[core, h, y, z] = total[(2 + h) * QUARTER:(3 + h) * QUARTER]
        wires.begun.append(True)

    def first(h):
        while not wires.begun:
            yield None
        yield from ring_gather(wires, ga.at[core, h, z], NY, y, y_up, y_down, h)
        relay(ga.at[core, h, z])
        yield from ring_gather(wires, ga.at[core, h], NZ, z, z_up, z_down, h, relay)

    def second(h):
        while not wires.begun:
            yield None
        yield from ring_gather(wires, gb.at[core, h, y], NZ, z, z_up, z_down, h)
        relay(gb.at[core, h, y])
        yield from ring_gather(wires, gb.at[core, h], NY, y, y_up, y_down, h, relay)

    return [start(), first(0), second(0), first(1), second(1)]


def weight_streams(wires, x, sibling, right, left, compute, src, stage, inbox, slots, total):
    order = (2, 1, 3, 0)
    sent, merged = [], []

    def ready(offset):
        turn = order.index(offset)
        while len(sent) < min(turn + 2, NX):
            dest = lax.rem(x + order[len(sent)], NX)
            compute(dest)
            sent.append(wires.send(stage.at[dest], inbox.at[dest], sibling))
            yield None
        if offset not in merged:
            merged.append(offset)
            sent[turn].wait_recv()
            dest = lax.rem(x + offset, NX)
            for h in (0, 1):
                src[h, dest] = src[h, dest] + inbox[dest, h]

    return [
        ring_reduce(wires, src.at[h], NX, x, right, left, slots.at[h], total.at[h], h, ready)
        for h in (0, 1)
    ]


def reduce_kernel(
    a_ref, signs_ref, ids_ref, sh, sl, xh, xl, wt, tops_out, worst_out, ga_out, gb_out,
    table, pa, pb, top, oa, ob, slots_a, slots_b, mid_a, mid_b, tail_a, tail_b,
    g_ref, theirs, mine, slots_g, ga, gb, tops, src, stage, inbox, slots_w, m,
    send_sems, recv_sems, keep_sems, *, scale,
):
    where = neighbours()
    y, z = where[:2]
    row = lax.axis_index("row")
    x, core = row // 2, lax.rem(row, 2)
    at = lambda xx, cc: {"row": lax.rem(xx, NX) * 2 + cc}
    sibling = at(x, 1 - core)
    others = [at(x + step, core) for step in range(1, NX)]
    crossed = [at(x + step, 1 - core) for step in range(1, NX)]
    arrive = greet(list(where[2:]) + [sibling] + others + crossed)
    rows, cols = a_ref.shape
    signs = signs_ref[...].astype(F32)
    fill_table(table, ids_ref[...], (y * NZ + z) * cols)
    sketch_group(0, a_ref, signs, table, pa, pb, scale)
    arrive()
    wires = Wires(send_sems, recv_sems)
    wires.relayed, wires.begun = [], []
    streams = sketch_streams(
        wires, where, pa, pb, oa, ob, slots_a, slots_b, mid_a, mid_b, tail_a, tail_b
    )
    for g in range(GROUPS):
        if g > 0:
            sketch_group(g, a_ref, signs, table, pa, pb, scale)
        for stream in streams[2 * g:2 * g + 2]:
            next(stream)
    top[...] = jnp.max(jnp.abs(a_ref[...]).reshape(rows // 8, 8, cols), axis=0)
    told = [
        wires.send(top, tops.at[index], device)
        for index, device in enumerate([sibling] + others + crossed)
    ]
    interleave(streams, SKETCH_ORDER)
    interleave(streams, ())

    def block(index):
        parts = [oa[g, index, yy] for g in range(GROUPS) for yy in range(NY)]
        parts += [ob[g, yy, index] for g in range(GROUPS) for yy in range(NY)]
        return split(jnp.concatenate(parts, axis=0))

    right = block(z)
    for h in (0, 1):
        g_ref[h] = mm_pair(block(2 * y + h), right, 0, 0)

    for copy in told:
        copy.wait_recv()
    most = top[...]
    for index in range(len(told)):
        most = jnp.maximum(most, tops[index])
    most = jnp.maximum(jnp.max(most, axis=0, keepdims=True), 1e-30)
    stretch = 1.0 / most
    tops[0] = jnp.broadcast_to(most, top.shape)
    tops[1] = jnp.broadcast_to(stretch, top.shape)
    tops_out[...] = tops[0, :, pl.ds(pl.multiple_of(row * LANES, LANES), LANES)]

    def assemble():
        for yy in range(NY):
            here = slice(yy * PERIOD, (yy + 1) * PERIOD)
            for zz in range(NZ):
                columns = slice(zz * LANES, (zz + 1) * LANES)
                pieces = [r for g in range(GROUPS) for r in (oa[g, zz, yy], ob[g, yy, zz])]
                sh[here, columns], sl[here, columns] = split(jnp.concatenate(pieces, axis=0))

    def compute(dest):
        columns = pl.ds(pl.multiple_of(dest * 2 * LANES, 2 * LANES), 2 * LANES)
        part = a_ref[:, columns] * tops[1, 0:1, columns]
        out = mm_pair(split(part), (sh[...], sl[...]), 0, 0)
        ours = jnp.where(core == 0, out[:LANES], out[LANES:])
        theirs = jnp.where(core == 0, out[LANES:], out[:LANES])
        half = LANES // 2
        for h in (0, 1):
            src[h, dest] = ours[h * half:(h + 1) * half]
            stage[dest, h] = theirs[h * half:(h + 1) * half]

    streams = gram_streams(
        wires, where, core, sibling, others, g_ref, theirs, mine, slots_g, ga, gb
    )
    next(streams[0])
    assemble()
    weights = weight_streams(
        wires, x, sibling, others[0], others[2], compute, src, stage, inbox, slots_w, wt
    )
    interleave(streams + weights, GRAM_ORDER)
    interleave(streams, ())
    for copy in wires.relayed:
        copy.wait_recv()
    kept = [
        pltpu.make_async_copy(ga, ga_out, keep_sems.at[0]),
        pltpu.make_async_copy(gb, gb_out, keep_sems.at[1]),
    ]
    for copy in kept:
        copy.start()
    factor(ga, gb, xh, xl, m, worst_out, lambda: [next(stream, None) for stream in weights * 2])
    interleave(weights, ())
    wires.drain()
    for copy in kept:
        copy.wait()


SKETCH_ORDER = (
    0, 2, 4, 1, 0, 0, 2, 2, 3, 0, 0, 4, 2, 2, 1, 1, 5, 0, 4, 0, 6, 2, 4, 3, 3, 1, 2, 4,
    7, 6, 3, 0, 1, 1, 2, 4, 4, 6, 5, 5, 1, 3, 3, 1, 6, 7, 7, 0, 0, 2, 2, 3, 1, 4, 1, 3,
    5, 7, 3, 4, 6, 4, 6, 0, 3, 5, 5, 7, 7, 0, 1, 1, 0, 2, 2, 6, 5, 5, 7, 7, 1, 1, 3, 3,
    6, 5, 2, 5, 7, 7, 1, 6, 1, 3, 6, 3, 4, 4, 0, 0, 5, 5, 7, 1, 3, 7, 3, 4, 6, 6, 2, 0,
    5, 5, 7, 7, 0, 3, 2, 4, 4, 1, 1, 2, 6, 0, 0, 5, 5, 7, 7, 2, 4, 3, 3, 4, 2, 7, 6, 6,
    1, 2, 0, 5, 4, 3, 4, 6, 6, 2, 7, 4, 7, 6, 6, 5, 5, 6, 7, 5,
)
GRAM_ORDER = (
    0, 1, 2, 3, 4, 5, 6, 0, 0, 0, 1, 2, 3, 4, 5, 1, 1, 2, 2, 3, 3, 4, 4, 5, 6, 1, 2, 2,
    3, 4, 4, 6, 1, 1, 2, 2, 5, 3, 3, 4, 4, 6, 1, 1, 2, 3, 3, 4, 1, 1, 5, 3, 5, 2, 3, 2,
    1, 4, 4, 3, 6, 6, 2, 4,
)
COPIES = 300


def reduce_all(a, signs, ids, scale):
    rows, cols = a.shape
    samples = ids.shape[1]
    half = LANES // 2
    array = lambda *shape: pltpu.VMEM(shape, F32)
    blocks_a = (GROUPS, NZ, NY, ROWS_A, LANES)
    blocks_b = (GROUPS, NY, NZ, ROWS_B, LANES)
    gram_a = (2, 2, NZ, NY, QUARTER, LANES)
    gram_b = (2, 2, NY, NZ, QUARTER, LANES)
    far = pl.BlockSpec(memory_space=pltpu.HBM)
    return pl.pallas_call(
        functools.partial(reduce_kernel, scale=scale),
        out_shape=(
            jax.ShapeDtypeStruct((rows, samples), BF16),
            jax.ShapeDtypeStruct((rows, samples), BF16),
            jax.ShapeDtypeStruct((samples, samples), BF16),
            jax.ShapeDtypeStruct((samples, samples), BF16),
            jax.ShapeDtypeStruct((2, half, samples), F32),
            jax.ShapeDtypeStruct((8, LANES), F32),
            jax.ShapeDtypeStruct((8, NB), F32),
            jax.ShapeDtypeStruct(gram_a, F32),
            jax.ShapeDtypeStruct(gram_b, F32),
        ),
        in_specs=[VMEM] * 3,
        out_specs=(VMEM,) * 7 + (far,) * 2,
        scratch_shapes=[
            pltpu.VMEM((cols, samples), BF16),
            array(*blocks_a),
            array(*blocks_b),
            array(8, cols),
            array(*blocks_a),
            array(*blocks_b),
            array(GROUPS, NZ - 1, NY, ROWS_A, LANES),
            array(GROUPS, NY - 1, NZ, ROWS_B, LANES),
            array(GROUPS, NY, ROWS_A, LANES),
            array(GROUPS, NZ, ROWS_B, LANES),
            array(GROUPS, NY - 1, ROWS_A, LANES),
            array(GROUPS, NZ - 1, ROWS_B, LANES),
            array(2, LANES, LANES),
            array(LANES, LANES),
            array(LANES, LANES),
            array(NX - 1, LANES, LANES),
            array(*gram_a),
            array(*gram_b),
            array(2 * NX - 1, 8, cols),
            array(2, NX, half, samples),
            array(NX, 2, half, samples),
            array(NX, 2, half, samples),
            array(2, NX - 1, half, samples),
            array(samples, samples),
            pltpu.SemaphoreType.DMA((COPIES,)),
            pltpu.SemaphoreType.DMA((COPIES,)),
            pltpu.SemaphoreType.DMA((2,)),
        ],
        compiler_params=pltpu.CompilerParams(
            collective_id=0, has_side_effects=True, vmem_limit_bytes=MEGA_LIMIT
        ),
    )(a, signs, ids)


NB = 256
STEPS = 4
CONVERGED = 4e-4


def load_gram(ga, gb, m):
    for core in range(2):
        for y in range(NY):
            for z in range(NZ):
                columns = slice(z * LANES, (z + 1) * LANES)
                pieces = [ga[core, h, z, y] for h in (0, 1)] + [gb[core, h, y, z] for h in (0, 1)]
                for index, piece in enumerate(pieces):
                    low = (2 * y + core) * LANES + index * QUARTER
                    m[low:low + QUARTER, columns] = piece


def factor(ga, gb, xh, xl, m, worst_out, between):
    n, nb = m.shape[0], NB
    rows = lax.broadcasted_iota(jnp.int32, (nb, nb), 0)
    cols = lax.broadcasted_iota(jnp.int32, (nb, nb), 1)
    eye = (rows == cols).astype(F32)
    half = jnp.where(rows > cols, 1.0, jnp.where(rows == cols, 0.5, 0.0)).astype(F32)
    load_gram(ga, gb, m)
    worst = jnp.zeros((1, nb), F32)
    for low in range(0, n, nb):
        high = low + nb
        block = m[low:high, low:high]
        down = lax.rsqrt(jnp.sum(block * eye, axis=1, keepdims=True))
        across = lax.rsqrt(jnp.sum(block * eye, axis=0, keepdims=True))
        block = block * down * across
        x = eye - half * (block - eye)
        for step in range(STEPS + 2):
            dot = mm1 if step < STEPS else mm3
            residual = dot(dot(x, block, 1, 0), x, 1, 1) - eye
            x = x - dot(half * residual, x, 1, 0)
        off = jnp.where(jnp.abs(residual) < CONVERGED, 0.0, 1.0)
        worst = jnp.maximum(worst, jnp.max(off, axis=0, keepdims=True))
        x = x * across
        m[low:high, low:high] = eye
        pivot = mm3(x, m[low:high, :], 1, 0)
        keep = lax.broadcasted_iota(jnp.int32, (nb, n), 1) < high
        pair = split(pivot)
        xh[low:high, :] = jnp.where(keep, pair[0], 0)
        xl[low:high, :] = jnp.where(keep, pair[1], 0)
        if high < n:
            m[high:, low:high] = jnp.zeros((n - high, nb), F32)
            m[high:, :] = m[high:, :] - mm_pair(
                (pair[0][:, high:], pair[1][:, high:]), pair, 0, 0
            )
        between()
    worst_out[...] = jnp.broadcast_to(worst, worst_out.shape)


def guard_kernel(worst, ga_in, gb_in, xh_in, xl_in, xh_out, xl_out, ga, gb, m, sems):
    @pl.when(jnp.max(worst[...]) > 0.0)
    def _():
        loads = [
            pltpu.make_async_copy(ga_in, ga, sems.at[0]),
            pltpu.make_async_copy(gb_in, gb, sems.at[1]),
        ]
        for copy in loads:
            copy.start()
        for copy in loads:
            copy.wait()
        load_gram(ga, gb, m)
        n = m.shape[0]
        lane = lax.broadcasted_iota(jnp.int32, (1, n), 1)
        chunk = 128

        def column(j, carry):
            row = m[pl.ds(j, 1), :]
            scale = lax.rsqrt(jnp.sum(jnp.where(lane == j, row, 0.0), axis=1, keepdims=True))
            pivot = jnp.where(lane == j, 1.0, row) * scale
            m[pl.ds(j, 1), :] = jnp.where(lane <= j, pivot, 0.0)

            def update(part, carry):
                here = pl.ds(pl.multiple_of(part * chunk, chunk), chunk)
                below = part * chunk + lax.broadcasted_iota(jnp.int32, (chunk, 1), 0) > j
                old = m[here, :]
                entry = jnp.sum(jnp.where(lane == j, old, 0.0), axis=1, keepdims=True) * scale
                new = jnp.where(lane == j, 0.0, old) - entry * pivot
                m[here, :] = jnp.where(below, new, old)
                return carry

            return lax.fori_loop(j // chunk, n // chunk, update, carry)

        lax.fori_loop(0, n, column, 0)
        xh_out[...], xl_out[...] = split(m[...])


def guard(worst, ga, gb, xh, xl):
    n = xh.shape[0]
    far = pl.BlockSpec(memory_space=pltpu.HBM)
    return pl.pallas_call(
        guard_kernel,
        out_shape=(jax.ShapeDtypeStruct((n, n), BF16),) * 2,
        in_specs=[VMEM, far, far, VMEM, VMEM],
        out_specs=(VMEM, VMEM),
        input_output_aliases={3: 0, 4: 1},
        scratch_shapes=[
            pltpu.VMEM(ga.shape, F32),
            pltpu.VMEM(gb.shape, F32),
            pltpu.VMEM((n, n), F32),
            pltpu.SemaphoreType.DMA((2,)),
        ],
        compiler_params=pltpu.CompilerParams(vmem_limit_bytes=GUARD_LIMIT),
    )(worst, ga, gb, xh, xl)


def outputs_kernel(
    sh, sl, xh, xl, wt, tops, basis_ref, proj_ref, stage, inbox, send_sems, recv_sems
):
    row = lax.axis_index("row")
    count = 2 * NX
    peers = [lax.rem(row + step, count) for step in range(1, count)]
    greet([{"row": peer} for peer in peers])()
    n = xh.shape[0]
    wide = 256
    pair = split(wt[...].reshape(LANES, xh.shape[0]))
    for low in range(0, n, wide):
        high = low + wide
        out = mm_pair(
            (xh[low:high, :high], xl[low:high, :high]), (pair[0][:, :high], pair[1][:, :high]), 1, 1
        )
        out = out * tops[0:1, :]
        for sub in range(wide // LANES):
            stage[low // LANES + sub] = out[sub * LANES:(sub + 1) * LANES]
    copies = []
    for index, peer in enumerate(peers):
        copy = pltpu.make_async_remote_copy(
            src_ref=stage.at[peer],
            dst_ref=inbox.at[index],
            send_sem=send_sems.at[index],
            recv_sem=recv_sems.at[index],
            device_id={"row": peer},
            device_id_type=MESH,
        )
        copy.start()
        copies.append(copy)
    for low in range(0, n, wide):
        high = low + wide
        basis_ref[:, low:high] = mm_pair(
            (sh[:, :high], sl[:, :high]), (xh[low:high, :high], xl[low:high, :high]), 1, 1
        )
    columns = lambda owner: pl.ds(pl.multiple_of(owner * LANES, LANES), LANES)
    proj_ref[:, columns(row)] = stage[row]
    for index, copy in enumerate(copies):
        copy.wait()
        sender = lax.rem(row - index - 1 + count, count)
        proj_ref[:, columns(sender)] = inbox[index]


def outputs(sh, sl, xh, xl, wt, tops):
    rows, n = sh.shape
    count = 2 * NX
    return pl.pallas_call(
        outputs_kernel,
        out_shape=(
            jax.ShapeDtypeStruct((rows, n), F32),
            jax.ShapeDtypeStruct((n // count, count * LANES), F32),
        ),
        in_specs=[VMEM] * 6,
        out_specs=(VMEM, VMEM),
        scratch_shapes=[
            pltpu.VMEM((count, LANES, LANES), F32),
            pltpu.VMEM((count - 1, LANES, LANES), F32),
            pltpu.SemaphoreType.DMA((count - 1,)),
            pltpu.SemaphoreType.DMA((count - 1,)),
        ],
        compiler_params=pltpu.CompilerParams(
            collective_id=1, has_side_effects=True, vmem_limit_bytes=OUTPUT_LIMIT
        ),
    )(sh, sl, xh, xl, wt, tops)


def body(expert_matrix, col_signs, sample_ids):
    local_cols = expert_matrix.shape[1]
    col_total = local_cols * lax.axis_size("col")
    model_width = expert_matrix.shape[0] * lax.axis_size("row")
    sh, sl, xh, xl, wt, tops, worst, ga, gb = reduce_all(
        expert_matrix, col_signs[None, :], sample_ids[None, :], 1.0 / math.sqrt(col_total)
    )
    xh, xl = guard(worst, ga, gb, xh, xl)
    basis, projected = outputs(sh, sl, xh, xl, wt, tops)
    return basis * math.sqrt(model_width), projected


def solution(mesh):
    in_specs = (P("row", "col"), P("col"), P())
    out_specs = (P("row", None), P("row", "col"))
    return jax.shard_map(body, mesh=mesh, in_specs=in_specs, out_specs=out_specs, check_vma=False)
```

```python
import functools
import math

import jax
import jax.numpy as jnp
from jax import lax
from jax.experimental import pallas as pl
from jax.experimental.pallas import tpu as pltpu
from jax.sharding import PartitionSpec as P

MESH = pl.DeviceIdType.MESH
F32 = jnp.float32
BF16 = jnp.bfloat16
NY, NZ, NX = 4, 8, 4
LANES = 128
VMEM = pl.BlockSpec(memory_space=pltpu.VMEM)
MEGA_LIMIT = 40 << 20
GUARD_LIMIT = 20 << 20
OUTPUT_LIMIT = 16 << 20


def split(value):
    high = value.astype(BF16)
    return high, (value - high.astype(F32)).astype(BF16)


def mm(a, b, ca, cb):
    return lax.dot_general(a, b, (((ca,), (cb,)), ((), ())), preferred_element_type=F32)


def mm_pair(a, b, ca, cb):
    (ah, al), (bh, bl) = a, b
    return mm(ah, bh, ca, cb) + (mm(ah, bl, ca, cb) + mm(al, bh, ca, cb))


def mm3(a, b, ca, cb):
    return mm_pair(split(a), split(b), ca, cb)


def mm1(a, b, ca, cb):
    return mm(a.astype(BF16), b.astype(BF16), ca, cb)


GROUPS = 4
ROWS_A, ROWS_B = 24, 32
PERIOD = GROUPS * (ROWS_A + ROWS_B)


def signs_of(value):
    for amount in (8, 4, 2, 1):
        value = value ^ (value >> amount)
    return (1 - 2 * (value & 1)).astype(F32)


def fill_table(table, ids, offset):
    cols, samples = table.shape
    step = 32
    index = lax.broadcasted_iota(jnp.int32, (step, samples), 0)
    low = signs_of(index & ids)
    high = signs_of((offset + step * index) & ids)
    for part in range(cols // step):
        table[part * step:(part + 1) * step, :] = (low * high[part:part + 1, :]).astype(BF16)


def sketch_group(g, a_ref, signs, table, pa, pb, scale):
    size = ROWS_A + ROWS_B
    parts = [a_ref[y * PERIOD + g * size:y * PERIOD + (g + 1) * size, :] for y in range(NY)]
    high, low = split(jnp.concatenate(parts, axis=0) * signs)
    wide = 256
    for part in range(table.shape[1] // wide):
        columns = slice(part * wide, (part + 1) * wide)
        out = (mm(high, table[:, columns], 1, 0) + mm(low, table[:, columns], 1, 0)) * scale
        for sub in range(wide // LANES):
            block = part * (wide // LANES) + sub
            for y in range(NY):
                piece = out[y * size:(y + 1) * size, sub * LANES:(sub + 1) * LANES]
                pa[g, block, y] = piece[:ROWS_A]
                pb[g, y, block] = piece[ROWS_A:]


class Wires:
    def __init__(self, send_sems, recv_sems):
        self.send_sems, self.recv_sems = send_sems, recv_sems
        self.copies = []

    def send(self, src, dst, device):
        index = len(self.copies)
        copy = pltpu.make_async_remote_copy(
            src_ref=src,
            dst_ref=dst,
            send_sem=self.send_sems.at[index],
            recv_sem=self.recv_sems.at[index],
            device_id=device,
            device_id_type=MESH,
        )
        copy.start()
        self.copies.append(copy)
        return copy

    def drain(self):
        for copy in self.copies:
            copy.wait_send()


def ring_reduce(wires, src, n, me, right, left, slots, total, long=0, ready=None):
    far = n // 2
    ways = []
    for way, (there, sign) in enumerate(((right, 1), (left, -1))):
        hops = far if way == long else far - 1
        ways.append((there, sign, hops, 0 if way == long else far))
    ways.sort(key=lambda way: -way[2])
    pending = [None, None]
    for step in range(far):
        for index, (there, sign, hops, base) in enumerate(ways):
            turn = step - (far - hops)
            if turn < 0:
                continue
            dest = lax.rem(me + sign * (hops - turn) + n, n)
            if ready is not None:
                yield from ready(sign * (hops - turn) % n)
            block = src.at[dest]
            if turn > 0:
                yield pending[index]
                pending[index].wait_recv()
                block = slots.at[base + turn - 1]
                block[...] = block[...] + src[dest]
            pending[index] = wires.send(block, slots.at[base + turn], there)
    if ready is not None:
        yield from ready(0)
    for copy in pending:
        yield copy
        copy.wait_recv()
    total[...] = src[me] + (slots[far - 1] + slots[n - 2])


def ring_gather(wires, buf, n, me, right, left, long=0, arrived=None):
    far = n // 2
    ways = ((right, 1, far if long == 0 else far - 1), (left, -1, far if long == 1 else far - 1))
    pending = [wires.send(buf.at[me], buf.at[me], there) for there, _, _ in ways]
    for step in range(1, far + 1):
        for index, (there, sign, hops) in enumerate(ways):
            if step > hops:
                continue
            origin = lax.rem(me - sign * step + n, n)
            yield pending[index]
            pending[index].wait_recv()
            block = buf.at[origin]
            if step < hops:
                pending[index] = wires.send(block, block, there)
            if arrived is not None:
                arrived(block)


def swift_reduce(wires, src, n, me, ways, slots, total, long=0):
    inner, sums = [], []
    for way, (near, far) in enumerate(ways):
        sign, base = (1, 0) if way == 0 else (-1, 4)
        dest = lambda hops: lax.rem(me + sign * hops + n, n)
        first = [wires.send(src.at[dest(3)], slots.at[base], near)]
        if way == long:
            first.append(wires.send(src.at[dest(4)], slots.at[base + 1], far))
        inner.append(first)
        sums.append(wires.send(src.at[dest(1)], slots.at[base + 2], near))
    for way in (1 - long, long):
        sign, base = (1, 0) if way == 0 else (-1, 4)
        for copy in inner[way]:
            yield copy
            copy.wait_recv()
        part = slots.at[base]
        held = src[lax.rem(me + sign * 2 + n, n)] + part[...]
        if way == long:
            held = held + slots[base + 1]
        part[...] = held
        sums.append(wires.send(part, slots.at[base + 3], ways[way][1]))
    for copy in sums:
        yield copy
        copy.wait_recv()
    total[...] = (src[me] + (slots[2] + slots[6])) + (slots[3] + slots[7])


def swift_gather(wires, buf, n, me, ways, long=0, arrived=None):
    block = lambda hops: buf.at[lax.rem(me + hops + n, n)]
    own = buf.at[me]
    far_copies = [wires.send(own, own, ways[way][1]) for way in (1 - long, long)]
    copies = [(wires.send(own, own, ways[way][0]), way, 1) for way in (0, 1)]
    for index, way in enumerate((1 - long, long)):
        sign = 1 if way == 0 else -1
        yield far_copies[index]
        far_copies[index].wait_recv()
        held = block(-2 * sign)
        copies.append((wires.send(held, held, ways[way][0]), way, 3))
        if way == long:
            copies.append((wires.send(held, held, ways[way][1]), way, 4))
        if arrived is not None:
            arrived(held)
    for copy, way, hops in copies:
        yield copy
        copy.wait_recv()
        if arrived is not None:
            arrived(block(-hops if way == 0 else hops))


def direct_gather(wires, buf, n, me, ways, long=0, arrived=None):
    own = buf.at[me]
    copies = []
    for way, (near, far) in enumerate(ways):
        sign = 1 if way == 0 else -1
        if way == long:
            copies.append((wires.send(own, own, far), 2))
        copies.append((wires.send(own, own, near), -sign))
    for copy, hops in copies:
        yield copy
        copy.wait_recv()
        if arrived is not None:
            arrived(buf.at[lax.rem(me + hops + n, n)])


def interleave(streams, order):
    streams = list(streams)
    for index in order:
        next(streams[index], None)
    alive = [] if order else list(streams)
    while alive:
        alive = [stream for stream in alive if next(stream, alive) is not alive]


def neighbours():
    col = lax.axis_index("col")
    y, z = col // NZ, lax.rem(col, NZ)
    at = lambda yy, zz: {"col": lax.rem(yy + NY, NY) * NZ + lax.rem(zz + NZ, NZ)}
    return y, z, at(y + 1, z), at(y - 1, z), at(y, z + 1), at(y, z - 1), at(y, z + 2), at(y, z - 2), at(y + 2, z)


def greet(devices):
    barrier = pltpu.get_barrier_semaphore()
    for device in devices:
        pl.semaphore_signal(barrier, inc=1, device_id=device, device_id_type=MESH)
    return lambda: pl.semaphore_wait(barrier, len(devices))


def sketch_streams(wires, where, pa, pb, oa, ob, slots_a, slots_b, mid_a, mid_b, tail_a, tail_b):
    y, z, y_up, y_down, z_up, z_down, z_up2, z_down2, _ = where
    z_ways = ((z_up, z_up2), (z_down, z_down2))

    def first(g):
        long = g % 2
        yield from ring_reduce(
            wires, pa.at[g], NZ, z, z_up, z_down, slots_a.at[g], mid_a.at[g], long
        )
        yield from ring_reduce(
            wires, mid_a.at[g], NY, y, y_up, y_down, tail_a.at[g], oa.at[g, z, y], long
        )
        yield from ring_gather(wires, oa.at[g, z], NY, y, y_up, y_down, long)
        yield from ring_gather(wires, oa.at[g], NZ, z, z_up, z_down, long)

    def second(g):
        long = g % 2
        yield from ring_reduce(
            wires, pb.at[g], NY, y, y_up, y_down, slots_b.at[g], mid_b.at[g], long
        )
        yield from swift_reduce(
            wires, mid_b.at[g], NZ, z, z_ways, tail_b.at[g], ob.at[g, y, z], long
        )
        yield from swift_gather(wires, ob.at[g, y], NZ, z, z_ways, long)
        yield from ring_gather(wires, ob.at[g], NY, y, y_up, y_down, long)

    return [stream(g) for g in range(GROUPS) for stream in (first, second)]


QUARTER = LANES // 4


def gram_streams(wires, where, core, sibling, others, g, theirs, mine, slots, ga, gb):
    y, z, y_up, y_down, z_up, z_down, z_up2, z_down2, y_far = where
    z_ways = ((z_up, z_up2), (z_down, z_down2))
    y_ways = ((y_up, y_far), (y_down, y_far))

    def relay(block):
        wires.relayed.append(wires.send(block, block, sibling))

    def start():
        copy = wires.send(g.at[1 - core], theirs, sibling)
        yield copy
        copy.wait_recv()
        mine[...] = g[core] + theirs[...]
        copies = [
            wires.send(mine, slots.at[step], device) for step, device in enumerate(others)
        ]
        for copy in copies:
            yield copy
            copy.wait_recv()
        total = (mine[...] + slots[1]) + (slots[0] + slots[2])
        for h in (0, 1):
            ga[core, h, z, y] = total[h * QUARTER:(h + 1) * QUARTER]
            gb[core, h, y, z] = total[(2 + h) * QUARTER:(3 + h) * QUARTER]
        wires.begun.append(True)

    def first(h):
        while not wires.begun:
            yield None
        yield from direct_gather(wires, ga.at[core, h, z], NY, y, y_ways, h)
        relay(ga.at[core, h, z])
        yield from ring_gather(wires, ga.at[core, h], NZ, z, z_up, z_down, h, relay)

    def second(h):
        while not wires.begun:
            yield None
        yield from swift_gather(wires, gb.at[core, h, y], NZ, z, z_ways, h)
        relay(gb.at[core, h, y])
        yield from ring_gather(wires, gb.at[core, h], NY, y, y_up, y_down, h, relay)

    return [start(), first(0), second(0), first(1), second(1)]


def weight_streams(wires, x, sibling, right, left, compute, src, stage, inbox, slots, total):
    order = (2, 1, 3, 0)
    sent, merged = [], []

    def ready(offset):
        turn = order.index(offset)
        while len(sent) < min(turn + 2, NX):
            dest = lax.rem(x + order[len(sent)], NX)
            compute(dest)
            sent.append(wires.send(stage.at[dest], inbox.at[dest], sibling))
            yield None
        if offset not in merged:
            merged.append(offset)
            sent[turn].wait_recv()
            dest = lax.rem(x + offset, NX)
            for h in (0, 1):
                src[h, dest] = src[h, dest] + inbox[dest, h]

    return [
        ring_reduce(wires, src.at[h], NX, x, right, left, slots.at[h], total.at[h], h, ready)
        for h in (0, 1)
    ]


def reduce_kernel(
    a_hbm, signs_ref, ids_ref, sh, sl, xh, xl, wt, tops_out, worst_out, ga_out, gb_out,
    a_ref, table, pa, pb, top, oa, ob, slots_a, slots_b, mid_a, mid_b, tail_a, tail_b,
    g_ref, theirs, mine, slots_g, ga, gb, tops, src, stage, inbox, slots_w, m,
    send_sems, recv_sems, keep_sems, *, scale,
):
    where = neighbours()
    y, z = where[:2]
    row = lax.axis_index("row")
    x, core = row // 2, lax.rem(row, 2)
    at = lambda xx, cc: {"row": lax.rem(xx, NX) * 2 + cc}
    sibling = at(x, 1 - core)
    others = [at(x + step, core) for step in range(1, NX)]
    crossed = [at(x + step, 1 - core) for step in range(1, NX)]
    arrive = greet(list(where[2:]) + [sibling] + others + crossed)
    rows, cols = a_ref.shape
    fetch = pltpu.make_async_copy(a_hbm, a_ref, keep_sems.at[2])
    fetch.start()
    signs = signs_ref[...].astype(F32)
    fill_table(table, ids_ref[...], (y * NZ + z) * cols)
    fetch.wait()
    sketch_group(0, a_ref, signs, table, pa, pb, scale)
    arrive()
    wires = Wires(send_sems, recv_sems)
    wires.relayed, wires.begun = [], []
    streams = sketch_streams(
        wires, where, pa, pb, oa, ob, slots_a, slots_b, mid_a, mid_b, tail_a, tail_b
    )
    for g in range(GROUPS):
        if g > 0:
            sketch_group(g, a_ref, signs, table, pa, pb, scale)
        for stream in streams[2 * g:2 * g + 2]:
            next(stream)
    top[...] = jnp.max(jnp.abs(a_ref[...]).reshape(rows // 8, 8, cols), axis=0)
    told = [
        wires.send(top, tops.at[index], device)
        for index, device in enumerate([sibling] + others + crossed)
    ]
    interleave(streams, SKETCH_ORDER)
    interleave(streams, ())

    def block(index):
        parts = [oa[g, index, yy] for g in range(GROUPS) for yy in range(NY)]
        parts += [ob[g, yy, index] for g in range(GROUPS) for yy in range(NY)]
        return split(jnp.concatenate(parts, axis=0))

    right = block(z)
    for h in (0, 1):
        g_ref[h] = mm_pair(block(2 * y + h), right, 0, 0)

    for copy in told:
        copy.wait_recv()
    most = top[...]
    for index in range(len(told)):
        most = jnp.maximum(most, tops[index])
    most = jnp.maximum(jnp.max(most, axis=0, keepdims=True), 1e-30)
    stretch = 1.0 / most
    tops[0] = jnp.broadcast_to(most, top.shape)
    tops[1] = jnp.broadcast_to(stretch, top.shape)
    tops_out[...] = tops[0, :, pl.ds(pl.multiple_of(row * LANES, LANES), LANES)]

    def assemble():
        for yy in range(NY):
            here = slice(yy * PERIOD, (yy + 1) * PERIOD)
            for zz in range(NZ):
                columns = slice(zz * LANES, (zz + 1) * LANES)
                pieces = [r for g in range(GROUPS) for r in (oa[g, zz, yy], ob[g, yy, zz])]
                sh[here, columns], sl[here, columns] = split(jnp.concatenate(pieces, axis=0))

    def compute(dest):
        columns = pl.ds(pl.multiple_of(dest * 2 * LANES, 2 * LANES), 2 * LANES)
        part = a_ref[:, columns] * tops[1, 0:1, columns]
        out = mm_pair(split(part), (sh[...], sl[...]), 0, 0)
        ours = jnp.where(core == 0, out[:LANES], out[LANES:])
        theirs = jnp.where(core == 0, out[LANES:], out[:LANES])
        half = LANES // 2
        for h in (0, 1):
            src[h, dest] = ours[h * half:(h + 1) * half]
            stage[dest, h] = theirs[h * half:(h + 1) * half]

    streams = gram_streams(
        wires, where, core, sibling, others, g_ref, theirs, mine, slots_g, ga, gb
    )
    next(streams[0])
    assemble()
    weights = weight_streams(
        wires, x, sibling, others[0], others[2], compute, src, stage, inbox, slots_w, wt
    )
    interleave(streams + weights, GRAM_ORDER)
    interleave(streams, ())
    for copy in wires.relayed:
        copy.wait_recv()
    kept = [
        pltpu.make_async_copy(ga, ga_out, keep_sems.at[0]),
        pltpu.make_async_copy(gb, gb_out, keep_sems.at[1]),
    ]
    for copy in kept:
        copy.start()
    factor(ga, gb, xh, xl, m, worst_out, lambda: [next(stream, None) for stream in weights * 2])
    interleave(weights, ())
    wires.drain()
    for copy in kept:
        copy.wait()


SKETCH_ORDER = (
    0, 2, 1, 4, 3, 6, 0, 0, 2, 2, 4, 5, 4, 6, 6, 0, 1, 1, 0, 7, 2, 2, 4, 4, 3, 3, 6, 0,
    6, 1, 1, 5, 0, 1, 1, 1, 5, 2, 2, 4, 4, 3, 3, 7, 7, 0, 3, 3, 3, 4, 2, 6, 6, 1, 1, 0,
    0, 5, 5, 5, 5, 5, 4, 4, 3, 7, 2, 2, 7, 6, 7, 7, 7, 3, 0, 0, 1, 1, 1, 1, 4, 2, 4, 2,
    6, 6, 5, 5, 7, 7, 0, 3, 3, 3, 3, 4, 1, 1, 2, 6, 6, 1, 5, 5, 5, 5, 7, 7, 7, 7, 6, 0,
    0, 3, 3, 1, 1, 3, 4, 4, 2, 2, 5, 5, 5, 7, 7, 7, 6, 6, 0, 0, 4, 4, 1, 3, 3, 2, 2, 6,
    6, 0, 5, 0, 5, 4, 4, 2, 2, 7, 7, 6, 3, 6, 0, 2, 4, 5, 6, 7,
)
GRAM_ORDER = (
    0, 1, 2, 3, 4, 5, 6, 0, 0, 0, 1, 2, 3, 4, 5, 1, 1, 1, 2, 2, 3, 2, 2, 3, 3, 5, 6, 4,
    4, 4, 4, 1, 1, 6, 5, 2, 2, 2, 3, 3, 6, 4, 4, 4, 1, 1, 3, 3, 2, 2, 5, 1, 1, 3, 3, 4,
    4, 5, 1, 3, 2, 4,
)
COPIES = 300


def reduce_all(a, signs, ids, scale):
    rows, cols = a.shape
    samples = ids.shape[1]
    half = LANES // 2
    array = lambda *shape: pltpu.VMEM(shape, F32)
    blocks_a = (GROUPS, NZ, NY, ROWS_A, LANES)
    blocks_b = (GROUPS, NY, NZ, ROWS_B, LANES)
    gram_a = (2, 2, NZ, NY, QUARTER, LANES)
    gram_b = (2, 2, NY, NZ, QUARTER, LANES)
    far = pl.BlockSpec(memory_space=pltpu.HBM)
    return pl.pallas_call(
        functools.partial(reduce_kernel, scale=scale),
        out_shape=(
            jax.ShapeDtypeStruct((rows, samples), BF16),
            jax.ShapeDtypeStruct((rows, samples), BF16),
            jax.ShapeDtypeStruct((samples, samples), BF16),
            jax.ShapeDtypeStruct((samples, samples), BF16),
            jax.ShapeDtypeStruct((2, half, samples), F32),
            jax.ShapeDtypeStruct((8, LANES), F32),
            jax.ShapeDtypeStruct((8, NB), F32),
            jax.ShapeDtypeStruct(gram_a, F32),
            jax.ShapeDtypeStruct(gram_b, F32),
        ),
        in_specs=[far, VMEM, VMEM],
        out_specs=(VMEM,) * 7 + (far,) * 2,
        scratch_shapes=[
            array(rows, cols),
            pltpu.VMEM((cols, samples), BF16),
            array(*blocks_a),
            array(*blocks_b),
            array(8, cols),
            array(*blocks_a),
            array(*blocks_b),
            array(GROUPS, NZ - 1, NY, ROWS_A, LANES),
            array(GROUPS, NY - 1, NZ, ROWS_B, LANES),
            array(GROUPS, NY, ROWS_A, LANES),
            array(GROUPS, NZ, ROWS_B, LANES),
            array(GROUPS, NY - 1, ROWS_A, LANES),
            array(GROUPS, NZ, ROWS_B, LANES),
            array(2, LANES, LANES),
            array(LANES, LANES),
            array(LANES, LANES),
            array(NX - 1, LANES, LANES),
            array(*gram_a),
            array(*gram_b),
            array(2 * NX - 1, 8, cols),
            array(2, NX, half, samples),
            array(NX, 2, half, samples),
            array(NX, 2, half, samples),
            array(2, NX - 1, half, samples),
            array(samples, samples),
            pltpu.SemaphoreType.DMA((COPIES,)),
            pltpu.SemaphoreType.DMA((COPIES,)),
            pltpu.SemaphoreType.DMA((3,)),
        ],
        compiler_params=pltpu.CompilerParams(
            collective_id=0, has_side_effects=True, vmem_limit_bytes=MEGA_LIMIT
        ),
    )(a, signs, ids)


NB = 256
STEPS = 3
CONVERGED = 4e-4


def load_gram(ga, gb, m, upper):
    for core in range(2):
        for y in range(NY):
            for z in range(2 * y if upper else 0, NZ):
                columns = slice(z * LANES, (z + 1) * LANES)
                pieces = [ga[core, h, z, y] for h in (0, 1)] + [gb[core, h, y, z] for h in (0, 1)]
                for index, piece in enumerate(pieces):
                    low = (2 * y + core) * LANES + index * QUARTER
                    m[low:low + QUARTER, columns] = piece


def factor(ga, gb, xh, xl, m, worst_out, between):
    n, nb = m.shape[0], NB
    rows = lax.broadcasted_iota(jnp.int32, (nb, nb), 0)
    cols = lax.broadcasted_iota(jnp.int32, (nb, nb), 1)
    eye = (rows == cols).astype(F32)
    half = jnp.where(rows > cols, 1.0, jnp.where(rows == cols, 0.5, 0.0)).astype(F32)
    load_gram(ga, gb, m, True)
    worst = jnp.zeros((1, nb), F32)
    for low in range(0, n, nb):
        high = low + nb
        block = m[low:high, low:high]
        down = lax.rsqrt(jnp.sum(block * eye, axis=1, keepdims=True))
        across = lax.rsqrt(jnp.sum(block * eye, axis=0, keepdims=True))
        block = block * down * across
        x = eye - half * (block - eye)
        for step in range(STEPS + 2):
            dot = mm1 if step < STEPS else mm3
            residual = dot(dot(x, block, 1, 0), x, 1, 1) - eye
            x = x - dot(half * residual, x, 1, 0)
        off = jnp.where(jnp.abs(residual) < CONVERGED, 0.0, 1.0)
        worst = jnp.maximum(worst, jnp.max(off, axis=0, keepdims=True))
        x = x * across
        m[low:high, low:high] = eye
        pivot = mm3(x, m[low:high, :], 1, 0)
        keep = lax.broadcasted_iota(jnp.int32, (nb, n), 1) < high
        pair = split(pivot)
        xh[low:high, :] = jnp.where(keep, pair[0], 0)
        xl[low:high, :] = jnp.where(keep, pair[1], 0)
        if high < n:
            m[high:, low:high] = jnp.zeros((n - high, nb), F32)
            for here in range(high, n, nb):
                rest = slice(here, here + nb)
                left = (pair[0][:, rest], pair[1][:, rest])
                for columns in (slice(0, high), slice(here, n)):
                    m[rest, columns] = m[rest, columns] - mm_pair(
                        left, (pair[0][:, columns], pair[1][:, columns]), 0, 0
                    )
        between()
    worst_out[...] = jnp.broadcast_to(worst, worst_out.shape)


def guard_kernel(worst, ga_in, gb_in, xh_in, xl_in, xh_out, xl_out, ga, gb, m, sems):
    @pl.when(jnp.max(worst[...]) > 0.0)
    def _():
        loads = [
            pltpu.make_async_copy(ga_in, ga, sems.at[0]),
            pltpu.make_async_copy(gb_in, gb, sems.at[1]),
        ]
        for copy in loads:
            copy.start()
        for copy in loads:
            copy.wait()
        load_gram(ga, gb, m, False)
        n = m.shape[0]
        lane = lax.broadcasted_iota(jnp.int32, (1, n), 1)
        chunk = 128

        def column(j, carry):
            row = m[pl.ds(j, 1), :]
            scale = lax.rsqrt(jnp.sum(jnp.where(lane == j, row, 0.0), axis=1, keepdims=True))
            pivot = jnp.where(lane == j, 1.0, row) * scale
            m[pl.ds(j, 1), :] = jnp.where(lane <= j, pivot, 0.0)

            def update(part, carry):
                here = pl.ds(pl.multiple_of(part * chunk, chunk), chunk)
                below = part * chunk + lax.broadcasted_iota(jnp.int32, (chunk, 1), 0) > j
                old = m[here, :]
                entry = jnp.sum(jnp.where(lane == j, old, 0.0), axis=1, keepdims=True) * scale
                new = jnp.where(lane == j, 0.0, old) - entry * pivot
                m[here, :] = jnp.where(below, new, old)
                return carry

            return lax.fori_loop(j // chunk, n // chunk, update, carry)

        lax.fori_loop(0, n, column, 0)
        xh_out[...], xl_out[...] = split(m[...])


def guard(worst, ga, gb, xh, xl):
    n = xh.shape[0]
    far = pl.BlockSpec(memory_space=pltpu.HBM)
    return pl.pallas_call(
        guard_kernel,
        out_shape=(jax.ShapeDtypeStruct((n, n), BF16),) * 2,
        in_specs=[VMEM, far, far, VMEM, VMEM],
        out_specs=(VMEM, VMEM),
        input_output_aliases={3: 0, 4: 1},
        scratch_shapes=[
            pltpu.VMEM(ga.shape, F32),
            pltpu.VMEM(gb.shape, F32),
            pltpu.VMEM((n, n), F32),
            pltpu.SemaphoreType.DMA((2,)),
        ],
        compiler_params=pltpu.CompilerParams(vmem_limit_bytes=GUARD_LIMIT),
    )(worst, ga, gb, xh, xl)


def outputs_kernel(
    sh, sl, xh, xl, wt, tops, basis_ref, proj_ref, stage, inbox, send_sems, recv_sems
):
    row = lax.axis_index("row")
    x, core = row // 2, lax.rem(row, 2)
    turns = [(step, flip) for step in (2, 1, 3) for flip in (0, 1)] + [(0, 1)]
    place_of = lambda step, flip: lax.rem(x + step, NX) * 2 + (1 - core if flip else core)
    peers = [place_of(step, flip) for step, flip in turns]
    arrive = greet([{"row": peer} for peer in peers])
    n = xh.shape[0]
    wide = 256
    pair = split(wt[...].reshape(LANES, xh.shape[0]))
    for low in range(0, n, wide):
        high = low + wide
        out = mm_pair(
            (xh[low:high, :high], xl[low:high, :high]), (pair[0][:, :high], pair[1][:, :high]), 1, 1
        )
        out = out * tops[0:1, :]
        for sub in range(wide // LANES):
            stage[low // LANES + sub] = out[sub * LANES:(sub + 1) * LANES]
    arrive()
    copies = []
    for index, peer in enumerate(peers):
        copy = pltpu.make_async_remote_copy(
            src_ref=stage.at[peer],
            dst_ref=inbox.at[index],
            send_sem=send_sems.at[index],
            recv_sem=recv_sems.at[index],
            device_id={"row": peer},
            device_id_type=MESH,
        )
        copy.start()
        copies.append(copy)
    for low in range(0, n, wide):
        high = low + wide
        basis_ref[:, low:high] = mm_pair(
            (sh[:, :high], sl[:, :high]), (xh[low:high, :high], xl[low:high, :high]), 1, 1
        )
    columns = lambda owner: pl.ds(pl.multiple_of(owner * LANES, LANES), LANES)
    proj_ref[:, columns(row)] = stage[row]
    for index, copy in enumerate(copies):
        copy.wait()
        step, flip = turns[index]
        proj_ref[:, columns(place_of(NX - step, flip))] = inbox[index]


def outputs(sh, sl, xh, xl, wt, tops):
    rows, n = sh.shape
    count = 2 * NX
    return pl.pallas_call(
        outputs_kernel,
        out_shape=(
            jax.ShapeDtypeStruct((rows, n), F32),
            jax.ShapeDtypeStruct((n // count, count * LANES), F32),
        ),
        in_specs=[VMEM] * 6,
        out_specs=(VMEM, VMEM),
        scratch_shapes=[
            pltpu.VMEM((count, LANES, LANES), F32),
            pltpu.VMEM((count - 1, LANES, LANES), F32),
            pltpu.SemaphoreType.DMA((count - 1,)),
            pltpu.SemaphoreType.DMA((count - 1,)),
        ],
        compiler_params=pltpu.CompilerParams(
            collective_id=1, has_side_effects=True, vmem_limit_bytes=OUTPUT_LIMIT
        ),
    )(sh, sl, xh, xl, wt, tops)


def body(expert_matrix, col_signs, sample_ids):
    local_cols = expert_matrix.shape[1]
    col_total = local_cols * lax.axis_size("col")
    model_width = expert_matrix.shape[0] * lax.axis_size("row")
    sh, sl, xh, xl, wt, tops, worst, ga, gb = reduce_all(
        expert_matrix, col_signs[None, :], sample_ids[None, :], 1.0 / math.sqrt(col_total)
    )
    xh, xl = guard(worst, ga, gb, xh, xl)
    basis, projected = outputs(sh, sl, xh, xl, wt, tops)
    return basis * math.sqrt(model_width), projected


def solution(mesh):
    in_specs = (P("row", "col"), P("col"), P())
    out_specs = (P("row", None), P("row", "col"))
    return jax.shard_map(body, mesh=mesh, in_specs=in_specs, out_specs=out_specs, check_vma=False)
```

```python
import functools
import math

import jax
import jax.numpy as jnp
from jax import lax
from jax.experimental import pallas as pl
from jax.experimental.pallas import tpu as pltpu
from jax.sharding import PartitionSpec as P

MESH = pl.DeviceIdType.MESH
F32 = jnp.float32
BF16 = jnp.bfloat16
NY, NZ, NX = 4, 8, 4
LANES = 128
VMEM = pl.BlockSpec(memory_space=pltpu.VMEM)
MEGA_LIMIT = 40 << 20
GUARD_LIMIT = 24 << 20
OUTPUT_LIMIT = 16 << 20


def split(value):
    high = value.astype(BF16)
    return high, (value - high.astype(F32)).astype(BF16)


def mm(a, b, ca, cb):
    return lax.dot_general(a, b, (((ca,), (cb,)), ((), ())), preferred_element_type=F32)


def mm_pair(a, b, ca, cb):
    (ah, al), (bh, bl) = a, b
    return mm(ah, bh, ca, cb) + (mm(ah, bl, ca, cb) + mm(al, bh, ca, cb))


def mm3(a, b, ca, cb):
    return mm_pair(split(a), split(b), ca, cb)


def mm1(a, b, ca, cb):
    return mm(a.astype(BF16), b.astype(BF16), ca, cb)


GROUPS = 4
ROWS_A, ROWS_B = 24, 32
PERIOD = GROUPS * (ROWS_A + ROWS_B)


def signs_of(value):
    for amount in (8, 4, 2, 1):
        value = value ^ (value >> amount)
    return (1 - 2 * (value & 1)).astype(F32)


def fill_table(table, ids, offset):
    cols, samples = table.shape
    step = 32
    index = lax.broadcasted_iota(jnp.int32, (step, samples), 0)
    low = signs_of(index & ids)
    high = signs_of((offset + step * index) & ids)
    for part in range(cols // step):
        table[part * step:(part + 1) * step, :] = (low * high[part:part + 1, :]).astype(BF16)


def sketch_group(g, a_ref, signs, table, pa, pb, scale):
    size = ROWS_A + ROWS_B
    parts = [a_ref[y * PERIOD + g * size:y * PERIOD + (g + 1) * size, :] for y in range(NY)]
    high, low = split(jnp.concatenate(parts, axis=0) * signs)
    wide = 256
    for part in range(table.shape[1] // wide):
        columns = slice(part * wide, (part + 1) * wide)
        out = (mm(high, table[:, columns], 1, 0) + mm(low, table[:, columns], 1, 0)) * scale
        for sub in range(wide // LANES):
            block = part * (wide // LANES) + sub
            for y in range(NY):
                piece = out[y * size:(y + 1) * size, sub * LANES:(sub + 1) * LANES]
                pa[g, block, y] = piece[:ROWS_A]
                pb[g, y, block] = piece[ROWS_A:]


class Wires:
    def __init__(self, send_sems, recv_sems):
        self.send_sems, self.recv_sems = send_sems, recv_sems
        self.copies = []

    def send(self, src, dst, device):
        index = len(self.copies)
        copy = pltpu.make_async_remote_copy(
            src_ref=src,
            dst_ref=dst,
            send_sem=self.send_sems.at[index],
            recv_sem=self.recv_sems.at[index],
            device_id=device,
            device_id_type=MESH,
        )
        copy.start()
        self.copies.append(copy)
        return copy

    def drain(self):
        for copy in self.copies:
            copy.wait_send()


def ring_reduce(wires, src, n, me, right, left, slots, total, long=0, ready=None):
    far = n // 2
    ways = []
    for way, (there, sign) in enumerate(((right, 1), (left, -1))):
        hops = far if way == long else far - 1
        ways.append((there, sign, hops, 0 if way == long else far))
    ways.sort(key=lambda way: -way[2])
    pending = [None, None]
    for step in range(far):
        for index, (there, sign, hops, base) in enumerate(ways):
            turn = step - (far - hops)
            if turn < 0:
                continue
            dest = lax.rem(me + sign * (hops - turn) + n, n)
            if ready is not None:
                yield from ready(sign * (hops - turn) % n)
            block = src.at[dest]
            if turn > 0:
                yield pending[index]
                pending[index].wait_recv()
                block = slots.at[base + turn - 1]
                block[...] = block[...] + src[dest]
            pending[index] = wires.send(block, slots.at[base + turn], there)
    if ready is not None:
        yield from ready(0)
    for copy in pending:
        yield copy
        copy.wait_recv()
    total[...] = src[me] + (slots[far - 1] + slots[n - 2])


def ring_gather(wires, buf, n, me, right, left, long=0, arrived=None):
    far = n // 2
    ways = ((right, 1, far if long == 0 else far - 1), (left, -1, far if long == 1 else far - 1))
    pending = [wires.send(buf.at[me], buf.at[me], there) for there, _, _ in ways]
    for step in range(1, far + 1):
        for index, (there, sign, hops) in enumerate(ways):
            if step > hops:
                continue
            origin = lax.rem(me - sign * step + n, n)
            yield pending[index]
            pending[index].wait_recv()
            block = buf.at[origin]
            if step < hops:
                pending[index] = wires.send(block, block, there)
            if arrived is not None:
                arrived(block)


def swift_reduce(wires, src, n, me, ways, slots, total, long=0):
    inner, sums = [], []
    for way, (near, far) in enumerate(ways):
        sign, base = (1, 0) if way == 0 else (-1, 4)
        dest = lambda hops: lax.rem(me + sign * hops + n, n)
        first = [wires.send(src.at[dest(3)], slots.at[base], near)]
        if way == long:
            first.append(wires.send(src.at[dest(4)], slots.at[base + 1], far))
        inner.append(first)
        sums.append(wires.send(src.at[dest(1)], slots.at[base + 2], near))
    for way in (1 - long, long):
        sign, base = (1, 0) if way == 0 else (-1, 4)
        for copy in inner[way]:
            yield copy
            copy.wait_recv()
        part = slots.at[base]
        held = src[lax.rem(me + sign * 2 + n, n)] + part[...]
        if way == long:
            held = held + slots[base + 1]
        part[...] = held
        sums.append(wires.send(part, slots.at[base + 3], ways[way][1]))
    for copy in sums:
        yield copy
        copy.wait_recv()
    total[...] = (src[me] + (slots[2] + slots[6])) + (slots[3] + slots[7])


def swift_gather(wires, buf, n, me, ways, long=0, arrived=None):
    block = lambda hops: buf.at[lax.rem(me + hops + n, n)]
    own = buf.at[me]
    far_copies = [wires.send(own, own, ways[way][1]) for way in (1 - long, long)]
    copies = [(wires.send(own, own, ways[way][0]), way, 1) for way in (0, 1)]
    for index, way in enumerate((1 - long, long)):
        sign = 1 if way == 0 else -1
        yield far_copies[index]
        far_copies[index].wait_recv()
        held = block(-2 * sign)
        copies.append((wires.send(held, held, ways[way][0]), way, 3))
        if way == long:
            copies.append((wires.send(held, held, ways[way][1]), way, 4))
        if arrived is not None:
            arrived(held)
    for copy, way, hops in copies:
        yield copy
        copy.wait_recv()
        if arrived is not None:
            arrived(block(-hops if way == 0 else hops))


def direct_gather(wires, buf, n, me, ways, long=0, arrived=None):
    own = buf.at[me]
    copies = []
    for way, (near, far) in enumerate(ways):
        sign = 1 if way == 0 else -1
        if way == long:
            copies.append((wires.send(own, own, far), 2))
        copies.append((wires.send(own, own, near), -sign))
    for copy, hops in copies:
        yield copy
        copy.wait_recv()
        if arrived is not None:
            arrived(buf.at[lax.rem(me + hops + n, n)])


def interleave(streams, order):
    streams = list(streams)
    for index in order:
        next(streams[index], None)
    alive = [] if order else list(streams)
    while alive:
        alive = [stream for stream in alive if next(stream, alive) is not alive]


def neighbours():
    col = lax.axis_index("col")
    y, z = col // NZ, lax.rem(col, NZ)
    at = lambda yy, zz: {"col": lax.rem(yy + NY, NY) * NZ + lax.rem(zz + NZ, NZ)}
    return y, z, at(y + 1, z), at(y - 1, z), at(y, z + 1), at(y, z - 1), at(y, z + 2), at(y, z - 2), at(y + 2, z)


def greet(devices):
    barrier = pltpu.get_barrier_semaphore()
    for device in devices:
        pl.semaphore_signal(barrier, inc=1, device_id=device, device_id_type=MESH)
    return lambda: pl.semaphore_wait(barrier, len(devices))


def sketch_streams(wires, where, pa, pb, oa, ob, slots_a, slots_b, mid_a, mid_b, tail_a, tail_b):
    y, z, y_up, y_down, z_up, z_down, z_up2, z_down2, _ = where
    z_ways = ((z_up, z_up2), (z_down, z_down2))

    def first(g):
        long = g % 2
        yield from ring_reduce(
            wires, pa.at[g], NZ, z, z_up, z_down, slots_a.at[g], mid_a.at[g], long
        )
        yield from ring_reduce(
            wires, mid_a.at[g], NY, y, y_up, y_down, tail_a.at[g], oa.at[g, z, y], long
        )
        yield from ring_gather(wires, oa.at[g, z], NY, y, y_up, y_down, long)
        yield from ring_gather(wires, oa.at[g], NZ, z, z_up, z_down, long)

    def second(g):
        long = g % 2
        yield from ring_reduce(
            wires, pb.at[g], NY, y, y_up, y_down, slots_b.at[g], mid_b.at[g], long
        )
        yield from swift_reduce(
            wires, mid_b.at[g], NZ, z, z_ways, tail_b.at[g], ob.at[g, y, z], long
        )
        yield from swift_gather(wires, ob.at[g, y], NZ, z, z_ways, long)
        yield from ring_gather(wires, ob.at[g], NY, y, y_up, y_down, long)

    return [stream(g) for g in range(GROUPS) for stream in (first, second)]


QUARTER = LANES // 4


def gram_streams(wires, where, core, sibling, others, g, theirs, mine, slots, ga, gb):
    y, z, y_up, y_down, z_up, z_down, z_up2, z_down2, y_far = where
    z_ways = ((z_up, z_up2), (z_down, z_down2))
    y_ways = ((y_up, y_far), (y_down, y_far))

    def relay(h):
        return lambda block: wires.relayed[h].append(wires.send(block, block, sibling))

    def start():
        copy = wires.send(g.at[1 - core], theirs, sibling)
        yield copy
        copy.wait_recv()
        mine[...] = g[core] + theirs[...]
        copies = [
            wires.send(mine, slots.at[step], device) for step, device in enumerate(others)
        ]
        for copy in copies:
            yield copy
            copy.wait_recv()
        total = (mine[...] + slots[1]) + (slots[0] + slots[2])
        for h in (0, 1):
            low = 2 * h * QUARTER
            ga[core, h, z, y] = total[low:low + QUARTER]
            gb[core, h, y, z] = total[low + QUARTER:low + 2 * QUARTER]
        wires.begun.append(True)

    def first(h):
        while not wires.begun:
            yield None
        yield from direct_gather(wires, ga.at[core, h, z], NY, y, y_ways, h)
        relay(h)(ga.at[core, h, z])
        yield from ring_gather(wires, ga.at[core, h], NZ, z, z_up, z_down, h, relay(h))
        wires.ended[h].append(True)

    def second(h):
        while not wires.begun:
            yield None
        yield from swift_gather(wires, gb.at[core, h, y], NZ, z, z_ways, h)
        relay(h)(gb.at[core, h, y])
        yield from ring_gather(wires, gb.at[core, h], NY, y, y_up, y_down, h, relay(h))
        wires.ended[h].append(True)

    return [start(), first(0), second(0), first(1), second(1)]


def weight_streams(wires, x, sibling, right, left, compute, src, stage, inbox, slots, total):
    order = (2, 1, 3, 0)
    sent, merged = [], []

    def produce():
        for offset in order:
            dest = lax.rem(x + offset, NX)
            for part in range(2):
                compute(dest, part)
                if part == 1:
                    sent.append(wires.send(stage.at[dest], inbox.at[dest], sibling))
                yield None

    def ready(offset):
        turn = order.index(offset)
        while len(sent) <= turn:
            yield None
        if offset not in merged:
            merged.append(offset)
            sent[turn].wait_recv()
            dest = lax.rem(x + offset, NX)
            for h in (0, 1):
                src[h, dest] = src[h, dest] + inbox[dest, h]

    return [produce()] + [
        ring_reduce(wires, src.at[h], NX, x, right, left, slots.at[h], total.at[h], h, ready)
        for h in (0, 1)
    ]


def reduce_kernel(
    a_hbm, lists_ref, sh, sl, xh, xl, wt, tops_out, worst_out, ga_out, gb_out,
    a_ref, table, pa, pb, top, oa, ob, slots_a, slots_b, mid_a, mid_b, tail_a, tail_b,
    g_ref, theirs, mine, slots_g, ga, gb, tops, src, stage, inbox, slots_w, m, rh, rl,
    send_sems, recv_sems, keep_sems, *, scale,
):
    where = neighbours()
    y, z = where[:2]
    row = lax.axis_index("row")
    x, core = row // 2, lax.rem(row, 2)
    at = lambda xx, cc: {"row": lax.rem(xx, NX) * 2 + cc}
    sibling = at(x, 1 - core)
    others = [at(x + step, core) for step in range(1, NX)]
    crossed = [at(x + step, 1 - core) for step in range(1, NX)]
    arrive = greet(list(where[2:]) + [sibling] + others + crossed)
    rows, cols = a_ref.shape
    fetch = pltpu.make_async_copy(a_hbm, a_ref, keep_sems.at[2])
    fetch.start()
    signs = lists_ref[0:1, :].astype(F32)
    fill_table(table, lists_ref[1:2, :], (y * NZ + z) * cols)
    fetch.wait()
    sketch_group(0, a_ref, signs, table, pa, pb, scale)
    arrive()
    wires = Wires(send_sems, recv_sems)
    wires.relayed, wires.ended, wires.begun = ([], []), ([], []), []
    streams = sketch_streams(
        wires, where, pa, pb, oa, ob, slots_a, slots_b, mid_a, mid_b, tail_a, tail_b
    )
    for g in range(GROUPS):
        if g > 0:
            sketch_group(g, a_ref, signs, table, pa, pb, scale)
        for stream in streams[2 * g:2 * g + 2]:
            next(stream)
    top[...] = jnp.max(jnp.abs(a_ref[...]).reshape(rows // 8, 8, cols), axis=0)
    told = [
        wires.send(top, tops.at[index], device)
        for index, device in enumerate([sibling] + others + crossed)
    ]
    interleave(streams, SKETCH_ORDER)
    interleave(streams, ())

    def block(index):
        parts = [oa[g, index, yy] for g in range(GROUPS) for yy in range(NY)]
        parts += [ob[g, yy, index] for g in range(GROUPS) for yy in range(NY)]
        return split(jnp.concatenate(parts, axis=0))

    right = block(z)
    half = LANES // 2
    for h in (0, 1):
        out = mm_pair(block(NY * h + y), right, 0, 0)
        for c in (0, 1):
            g_ref[c, h * half:(h + 1) * half] = out[c * half:(c + 1) * half]

    for copy in told:
        copy.wait_recv()
    most = top[...]
    for index in range(len(told)):
        most = jnp.maximum(most, tops[index])
    most = jnp.maximum(jnp.max(most, axis=0, keepdims=True), 1e-30)
    stretch = 1.0 / most
    tops[0] = jnp.broadcast_to(most, top.shape)
    tops[1] = jnp.broadcast_to(stretch, top.shape)
    tops_out[...] = tops[0, :, pl.ds(pl.multiple_of(row * LANES, LANES), LANES)]

    def assemble():
        for yy in range(NY):
            here = slice(yy * PERIOD, (yy + 1) * PERIOD)
            for zz in range(NZ):
                columns = slice(zz * LANES, (zz + 1) * LANES)
                pieces = [r for g in range(GROUPS) for r in (oa[g, zz, yy], ob[g, yy, zz])]
                sh[here, columns], sl[here, columns] = split(jnp.concatenate(pieces, axis=0))

    def compute(dest, part):
        columns = pl.ds(pl.multiple_of(dest * 2 * LANES, 2 * LANES), 2 * LANES)
        wide = sh.shape[1] // 2
        samples = slice(part * wide, (part + 1) * wide)
        left = split(a_ref[:, columns] * tops[1, 0:1, columns])
        out = mm_pair(left, (sh[:, samples], sl[:, samples]), 0, 0)
        ours = jnp.where(core == 0, out[:LANES], out[LANES:])
        theirs = jnp.where(core == 0, out[LANES:], out[:LANES])
        for h in (0, 1):
            src[h, dest, :, samples] = ours[h * half:(h + 1) * half]
            stage[dest, h, :, samples] = theirs[h * half:(h + 1) * half]

    streams = gram_streams(
        wires, where, core, sibling, others, g_ref, theirs, mine, slots_g, ga, gb
    )
    next(streams[0])
    assemble()
    weights = weight_streams(
        wires, x, sibling, others[0], others[2], compute, src, stage, inbox, slots_w, wt
    )
    early = factor_first(wires, ga, gb, xh, xl, m, rh, rl)
    interleave(streams + [early] + weights, GRAM_ORDER)
    interleave(streams + [early], ())
    for copy in wires.relayed[1]:
        copy.wait_recv()
    kept = [
        pltpu.make_async_copy(ga, ga_out, keep_sems.at[0]),
        pltpu.make_async_copy(gb, gb_out, keep_sems.at[1]),
    ]
    for copy in kept:
        copy.start()
    for turn, _ in enumerate(factor_second(wires, ga, gb, xh, xl, m, rh, rl)):
        if turn % 2:
            for stream in weights:
                next(stream, None)
    worst = functools.reduce(jnp.maximum, wires.worst)
    worst_out[...] = jnp.broadcast_to(worst, worst_out.shape)
    interleave(weights, ())
    wires.drain()
    for copy in kept:
        copy.wait()


SKETCH_ORDER = (
    0, 2, 1, 4, 3, 6, 0, 0, 2, 2, 4, 5, 4, 6, 6, 0, 1, 1, 0, 7, 2, 2, 4, 4, 3, 3, 6, 0,
    6, 1, 1, 5, 0, 1, 1, 1, 5, 2, 2, 4, 4, 3, 3, 7, 7, 0, 3, 3, 3, 4, 2, 6, 6, 1, 1, 0,
    0, 5, 5, 5, 5, 5, 4, 4, 3, 7, 2, 2, 7, 6, 7, 7, 7, 3, 0, 0, 1, 1, 1, 1, 4, 2, 4, 2,
    6, 6, 5, 5, 7, 7, 0, 3, 3, 3, 3, 4, 1, 1, 2, 6, 6, 1, 5, 5, 5, 5, 7, 7, 7, 7, 6, 0,
    0, 3, 3, 1, 1, 3, 4, 4, 2, 2, 5, 5, 5, 7, 7, 7, 6, 6, 0, 0, 4, 4, 1, 3, 3, 2, 2, 6,
    6, 0, 5, 0, 5, 4, 4, 2, 2, 7, 7, 6, 3, 6, 0, 2, 4, 5, 6, 7,
)
GRAM_ORDER = (
    6, 0, 6, 6, 6, 0, 6, 0, 0, 2, 1, 4, 3, 6, 6, 2, 2, 2, 2, 1, 1, 1, 3, 6, 4, 4, 4, 4,
    3, 3, 6, 7, 2, 2, 8, 2, 1, 1, 4, 4, 4, 3, 3, 2, 2, 1, 1, 7, 8, 3, 3, 4, 4, 1, 1, 3,
    3, 2, 7, 1, 5, 5, 5, 5, 5, 5, 5, 5, 5, 5, 5, 7, 4, 5, 5, 5, 5, 5, 5, 5, 5, 5, 5, 5,
    5, 5, 3,
)
COPIES = 300


def reduce_all(a, lists, scale):
    rows, cols = a.shape
    samples = lists.shape[1]
    half = LANES // 2
    array = lambda *shape: pltpu.VMEM(shape, F32)
    blocks_a = (GROUPS, NZ, NY, ROWS_A, LANES)
    blocks_b = (GROUPS, NY, NZ, ROWS_B, LANES)
    gram_a = (2, 2, NZ, NY, QUARTER, LANES)
    gram_b = (2, 2, NY, NZ, QUARTER, LANES)
    far = pl.BlockSpec(memory_space=pltpu.HBM)
    return pl.pallas_call(
        functools.partial(reduce_kernel, scale=scale),
        out_shape=(
            jax.ShapeDtypeStruct((rows, samples), BF16),
            jax.ShapeDtypeStruct((rows, samples), BF16),
            jax.ShapeDtypeStruct((samples, samples), BF16),
            jax.ShapeDtypeStruct((samples, samples), BF16),
            jax.ShapeDtypeStruct((2, half, samples), F32),
            jax.ShapeDtypeStruct((8, LANES), F32),
            jax.ShapeDtypeStruct((8, NB), F32),
            jax.ShapeDtypeStruct(gram_a, F32),
            jax.ShapeDtypeStruct(gram_b, F32),
        ),
        in_specs=[far, VMEM],
        out_specs=(VMEM,) * 7 + (far,) * 2,
        scratch_shapes=[
            array(rows, cols),
            pltpu.VMEM((cols, samples), BF16),
            array(*blocks_a),
            array(*blocks_b),
            array(8, cols),
            array(*blocks_a),
            array(*blocks_b),
            array(GROUPS, NZ - 1, NY, ROWS_A, LANES),
            array(GROUPS, NY - 1, NZ, ROWS_B, LANES),
            array(GROUPS, NY, ROWS_A, LANES),
            array(GROUPS, NZ, ROWS_B, LANES),
            array(GROUPS, NY - 1, ROWS_A, LANES),
            array(GROUPS, NZ, ROWS_B, LANES),
            array(2, LANES, LANES),
            array(LANES, LANES),
            array(LANES, LANES),
            array(NX - 1, LANES, LANES),
            array(*gram_a),
            array(*gram_b),
            array(2 * NX - 1, 8, cols),
            array(2, NX, half, samples),
            array(NX, 2, half, samples),
            array(NX, 2, half, samples),
            array(2, NX - 1, half, samples),
            array(samples, samples),
            pltpu.VMEM((samples // 2, samples), BF16),
            pltpu.VMEM((samples // 2, samples), BF16),
            pltpu.SemaphoreType.DMA((COPIES,)),
            pltpu.SemaphoreType.DMA((COPIES,)),
            pltpu.SemaphoreType.DMA((3,)),
        ],
        compiler_params=pltpu.CompilerParams(
            collective_id=0, has_side_effects=True, vmem_limit_bytes=MEGA_LIMIT
        ),
    )(a, lists)


NB = 256
STEPS = 2
CONVERGED = 4e-4


def load_gram(ga, gb, m, h, upper):
    for core in range(2):
        for y in range(NY):
            low = (h * NY + y) * LANES + core * 2 * QUARTER
            for z in range(low // NB * 2 if upper else 0, NZ):
                columns = slice(z * LANES, (z + 1) * LANES)
                m[low:low + QUARTER, columns] = ga[core, h, z, y]
                m[low + QUARTER:low + 2 * QUARTER, columns] = gb[core, h, y, z]


def masks():
    rows = lax.broadcasted_iota(jnp.int32, (NB, NB), 0)
    cols = lax.broadcasted_iota(jnp.int32, (NB, NB), 1)
    eye = (rows == cols).astype(F32)
    half = jnp.where(rows > cols, 1.0, jnp.where(rows == cols, 0.5, 0.0)).astype(F32)
    return eye, half


def subtract(m, rest, columns, left, right):
    m[rest, columns] = m[rest, columns] - mm_pair(left, right, 0, 0)


def eliminate(wires, low, last, xh, xl, m, rh, rl):
    n, nb = m.shape[0], NB
    high = low + nb
    eye, half = masks()
    block = m[low:high, low:high]
    down = lax.rsqrt(jnp.sum(block * eye, axis=1, keepdims=True))
    across = lax.rsqrt(jnp.sum(block * eye, axis=0, keepdims=True))
    block = block * down * across
    x = eye - half * (block - eye)
    for step in range(STEPS + 2):
        dot = mm1 if step < STEPS else mm3
        residual = dot(dot(x, block, 1, 0), x, 1, 1) - eye
        x = x - mm1(half * residual, x, 1, 0)
        yield None
    off = jnp.where(jnp.abs(residual) < CONVERGED, 0.0, 1.0)
    wires.worst.append(jnp.max(off, axis=0, keepdims=True))
    x = x * across
    m[low:high, low:high] = eye
    pivot = mm3(x, m[low:high, :], 1, 0)
    keep = lax.broadcasted_iota(jnp.int32, (nb, n), 1) < high
    pair = split(pivot)
    xh[low:high, :] = jnp.where(keep, pair[0], 0)
    xl[low:high, :] = jnp.where(keep, pair[1], 0)
    if high < n // 2 + 1:
        rh[low:high, :], rl[low:high, :] = pair
    yield None
    if high < last:
        m[high:last, low:high] = jnp.zeros((last - high, nb), F32)
        left = (pair[0][:, high:last], pair[1][:, high:last])
        for columns in (slice(0, high), slice(high, n)):
            subtract(m, slice(high, last), columns, left, (pair[0][:, columns], pair[1][:, columns]))
        yield None


def factor_first(wires, ga, gb, xh, xl, m, rh, rl):
    wires.worst = []
    while len(wires.ended[0]) < 2:
        yield None
    for copy in wires.relayed[0]:
        yield copy
        copy.wait_recv()
    n = m.shape[0]
    load_gram(ga, gb, m, 0, True)
    for low in range(0, n // 2, NB):
        yield from eliminate(wires, low, n // 2, xh, xl, m, rh, rl)


def factor_second(wires, ga, gb, xh, xl, m, rh, rl):
    n = m.shape[0]
    middle = n // 2
    load_gram(ga, gb, m, 1, True)
    m[middle:, :middle] = jnp.zeros((n - middle, middle), F32)
    for low in range(middle, n, NB):
        rest = slice(low, low + NB)
        left = (rh[:, rest], rl[:, rest])
        subtract(m, rest, slice(low, n), left, (rh[:, low:], rl[:, low:]))
        above = slice(0, middle)
        subtract(m, rest, above, left, (xh[above, above], xl[above, above]))
        yield None
    for low in range(middle, n, NB):
        yield from eliminate(wires, low, n, xh, xl, m, rh, rl)


def guard_kernel(worst, ga_in, gb_in, xh_in, xl_in, xh_out, xl_out, ga, gb, m, xh, xl, sems):
    @pl.when(jnp.max(worst[...]) > 0.0)
    def _():
        loads = [
            pltpu.make_async_copy(ga_in, ga, sems.at[0]),
            pltpu.make_async_copy(gb_in, gb, sems.at[1]),
        ]
        for copy in loads:
            copy.start()
        for copy in loads:
            copy.wait()
        load_gram(ga, gb, m, 0, False)
        load_gram(ga, gb, m, 1, False)
        n = m.shape[0]
        lane = lax.broadcasted_iota(jnp.int32, (1, n), 1)
        chunk = 128

        def column(j, carry):
            row = m[pl.ds(j, 1), :]
            scale = lax.rsqrt(jnp.sum(jnp.where(lane == j, row, 0.0), axis=1, keepdims=True))
            pivot = jnp.where(lane == j, 1.0, row) * scale
            m[pl.ds(j, 1), :] = jnp.where(lane <= j, pivot, 0.0)

            def update(part, carry):
                here = pl.ds(pl.multiple_of(part * chunk, chunk), chunk)
                below = part * chunk + lax.broadcasted_iota(jnp.int32, (chunk, 1), 0) > j
                old = m[here, :]
                entry = jnp.sum(jnp.where(lane == j, old, 0.0), axis=1, keepdims=True) * scale
                new = jnp.where(lane == j, 0.0, old) - entry * pivot
                m[here, :] = jnp.where(below, new, old)
                return carry

            return lax.fori_loop(j // chunk, n // chunk, update, carry)

        lax.fori_loop(0, n, column, 0)
        xh[...], xl[...] = split(m[...])
        stores = [
            pltpu.make_async_copy(xh, xh_out, sems.at[0]),
            pltpu.make_async_copy(xl, xl_out, sems.at[1]),
        ]
        for copy in stores:
            copy.start()
        for copy in stores:
            copy.wait()


def guard(worst, ga, gb, xh, xl):
    n = xh.shape[0]
    anywhere = pl.BlockSpec(memory_space=pl.ANY)
    return pl.pallas_call(
        guard_kernel,
        out_shape=(jax.ShapeDtypeStruct((n, n), BF16),) * 2,
        in_specs=[VMEM] + [anywhere] * 4,
        out_specs=(anywhere, anywhere),
        input_output_aliases={3: 0, 4: 1},
        scratch_shapes=[
            pltpu.VMEM(ga.shape, F32),
            pltpu.VMEM(gb.shape, F32),
            pltpu.VMEM((n, n), F32),
            pltpu.VMEM((n, n), BF16),
            pltpu.VMEM((n, n), BF16),
            pltpu.SemaphoreType.DMA((2,)),
        ],
        compiler_params=pltpu.CompilerParams(vmem_limit_bytes=GUARD_LIMIT),
    )(worst, ga, gb, xh, xl)


def outputs_kernel(
    sh, sl, xh, xl, wt, tops, basis_ref, proj_ref, stage, inbox, send_sems, recv_sems, *, root
):
    row = lax.axis_index("row")
    x, core = row // 2, lax.rem(row, 2)
    turns = [(step, flip) for step in (2, 1, 3) for flip in (0, 1)] + [(0, 1)]
    place_of = lambda step, flip: lax.rem(x + step, NX) * 2 + (1 - core if flip else core)
    peers = [place_of(step, flip) for step, flip in turns]
    arrive = greet([{"row": peer} for peer in peers])
    n = xh.shape[0]
    wide = 256
    pair = split(wt[...].reshape(LANES, xh.shape[0]))
    for low in range(0, n, wide):
        high = low + wide
        out = mm_pair(
            (xh[low:high, :high], xl[low:high, :high]), (pair[0][:, :high], pair[1][:, :high]), 1, 1
        )
        out = out * tops[0:1, :]
        for sub in range(wide // LANES):
            stage[low // LANES + sub] = out[sub * LANES:(sub + 1) * LANES]
    arrive()
    copies = []
    for index, peer in enumerate(peers):
        copy = pltpu.make_async_remote_copy(
            src_ref=stage.at[peer],
            dst_ref=inbox.at[index],
            send_sem=send_sems.at[index],
            recv_sem=recv_sems.at[index],
            device_id={"row": peer},
            device_id_type=MESH,
        )
        copy.start()
        copies.append(copy)
    for low in range(0, n, wide):
        high = low + wide
        basis = mm_pair(
            (sh[:, :high], sl[:, :high]), (xh[low:high, :high], xl[low:high, :high]), 1, 1
        )
        basis_ref[:, low:high] = basis * root
    columns = lambda owner: pl.ds(pl.multiple_of(owner * LANES, LANES), LANES)
    proj_ref[:, columns(row)] = stage[row]
    for index, copy in enumerate(copies):
        copy.wait()
        step, flip = turns[index]
        proj_ref[:, columns(place_of(NX - step, flip))] = inbox[index]


def outputs(sh, sl, xh, xl, wt, tops, root):
    rows, n = sh.shape
    count = 2 * NX
    return pl.pallas_call(
        functools.partial(outputs_kernel, root=root),
        out_shape=(
            jax.ShapeDtypeStruct((rows, n), F32),
            jax.ShapeDtypeStruct((n // count, count * LANES), F32),
        ),
        in_specs=[VMEM] * 6,
        out_specs=(VMEM, VMEM),
        scratch_shapes=[
            pltpu.VMEM((count, LANES, LANES), F32),
            pltpu.VMEM((count - 1, LANES, LANES), F32),
            pltpu.SemaphoreType.DMA((count - 1,)),
            pltpu.SemaphoreType.DMA((count - 1,)),
        ],
        compiler_params=pltpu.CompilerParams(
            collective_id=1, has_side_effects=True, vmem_limit_bytes=OUTPUT_LIMIT
        ),
    )(sh, sl, xh, xl, wt, tops)


def body(expert_matrix, col_signs, sample_ids):
    local_cols = expert_matrix.shape[1]
    col_total = local_cols * lax.axis_size("col")
    model_width = expert_matrix.shape[0] * lax.axis_size("row")
    lists = jnp.stack([col_signs, sample_ids])
    sh, sl, xh, xl, wt, tops, worst, ga, gb = reduce_all(
        expert_matrix, lists, 1.0 / math.sqrt(col_total)
    )
    xh, xl = guard(worst, ga, gb, xh, xl)
    return outputs(sh, sl, xh, xl, wt, tops, math.sqrt(model_width))


def solution(mesh):
    in_specs = (P("row", "col"), P("col"), P())
    out_specs = (P("row", None), P("row", "col"))
    return jax.shard_map(body, mesh=mesh, in_specs=in_specs, out_specs=out_specs, check_vma=False)
```

```python
import functools
import math

import jax
import jax.numpy as jnp
from jax import lax
from jax.experimental import pallas as pl
from jax.experimental.pallas import tpu as pltpu
from jax.sharding import PartitionSpec as P

MESH = pl.DeviceIdType.MESH
F32 = jnp.float32
BF16 = jnp.bfloat16
NY, NZ, NX = 4, 8, 4
LANES = 128
VMEM = pl.BlockSpec(memory_space=pltpu.VMEM)
MEGA_LIMIT = 40 << 20
GUARD_LIMIT = 24 << 20
OUTPUT_LIMIT = 16 << 20


def split(value):
    high = value.astype(BF16)
    return high, (value - high.astype(F32)).astype(BF16)


def mm(a, b, ca, cb):
    return lax.dot_general(a, b, (((ca,), (cb,)), ((), ())), preferred_element_type=F32)


def mm_pair(a, b, ca, cb):
    (ah, al), (bh, bl) = a, b
    return mm(ah, bh, ca, cb) + (mm(ah, bl, ca, cb) + mm(al, bh, ca, cb))


def mm3(a, b, ca, cb):
    return mm_pair(split(a), split(b), ca, cb)


def mm1(a, b, ca, cb):
    return mm(a.astype(BF16), b.astype(BF16), ca, cb)


GROUPS = 4
ROWS_A, ROWS_B = 24, 32
PERIOD = GROUPS * (ROWS_A + ROWS_B)


def signs_of(value):
    for amount in (8, 4, 2, 1):
        value = value ^ (value >> amount)
    return (1 - 2 * (value & 1)).astype(F32)


def fill_table(table, ids, offset):
    cols, samples = table.shape
    step = 32
    index = lax.broadcasted_iota(jnp.int32, (step, samples), 0)
    low = signs_of(index & ids)
    high = signs_of((offset + step * index) & ids)
    for part in range(cols // step):
        table[part * step:(part + 1) * step, :] = (low * high[part:part + 1, :]).astype(BF16)


def sketch_group(g, a_ref, signs, table, pa, pb, scale):
    size = ROWS_A + ROWS_B
    parts = [a_ref[y * PERIOD + g * size:y * PERIOD + (g + 1) * size, :] for y in range(NY)]
    high, low = split(jnp.concatenate(parts, axis=0) * signs)
    wide = 256
    for part in range(table.shape[1] // wide):
        columns = slice(part * wide, (part + 1) * wide)
        out = (mm(high, table[:, columns], 1, 0) + mm(low, table[:, columns], 1, 0)) * scale
        for sub in range(wide // LANES):
            block = part * (wide // LANES) + sub
            for y in range(NY):
                piece = out[y * size:(y + 1) * size, sub * LANES:(sub + 1) * LANES]
                pa[g, block, y] = piece[:ROWS_A]
                pb[g, y, block] = piece[ROWS_A:]


class Wires:
    def __init__(self, send_sems, recv_sems):
        self.send_sems, self.recv_sems = send_sems, recv_sems
        self.copies = []

    def send(self, src, dst, device):
        index = len(self.copies)
        copy = pltpu.make_async_remote_copy(
            src_ref=src,
            dst_ref=dst,
            send_sem=self.send_sems.at[index],
            recv_sem=self.recv_sems.at[index],
            device_id=device,
            device_id_type=MESH,
        )
        copy.start()
        self.copies.append(copy)
        return copy

    def drain(self):
        for copy in self.copies:
            copy.wait_send()


def ring_reduce(wires, src, n, me, right, left, slots, total, long=0, ready=None):
    far = n // 2
    ways = []
    for way, (there, sign) in enumerate(((right, 1), (left, -1))):
        hops = far if way == long else far - 1
        ways.append((there, sign, hops, 0 if way == long else far))
    ways.sort(key=lambda way: -way[2])
    pending = [None, None]
    for step in range(far):
        for index, (there, sign, hops, base) in enumerate(ways):
            turn = step - (far - hops)
            if turn < 0:
                continue
            dest = lax.rem(me + sign * (hops - turn) + n, n)
            if ready is not None:
                yield from ready(sign * (hops - turn) % n)
            block = src.at[dest]
            if turn > 0:
                yield pending[index]
                pending[index].wait_recv()
                block = slots.at[base + turn - 1]
                block[...] = block[...] + src[dest]
            pending[index] = wires.send(block, slots.at[base + turn], there)
    if ready is not None:
        yield from ready(0)
    for copy in pending:
        yield copy
        copy.wait_recv()
    total[...] = src[me] + (slots[far - 1] + slots[n - 2])


def ring_gather(wires, buf, n, me, right, left, long=0, arrived=None):
    far = n // 2
    ways = ((right, 1, far if long == 0 else far - 1), (left, -1, far if long == 1 else far - 1))
    pending = [wires.send(buf.at[me], buf.at[me], there) for there, _, _ in ways]
    for step in range(1, far + 1):
        for index, (there, sign, hops) in enumerate(ways):
            if step > hops:
                continue
            origin = lax.rem(me - sign * step + n, n)
            yield pending[index]
            pending[index].wait_recv()
            block = buf.at[origin]
            if step < hops:
                pending[index] = wires.send(block, block, there)
            if arrived is not None:
                arrived(block)


def swift_reduce(wires, src, n, me, ways, slots, total, long=0):
    inner, sums = [], []
    for way, (near, far) in enumerate(ways):
        sign, base = (1, 0) if way == 0 else (-1, 4)
        dest = lambda hops: lax.rem(me + sign * hops + n, n)
        first = [wires.send(src.at[dest(3)], slots.at[base], near)]
        if way == long:
            first.append(wires.send(src.at[dest(4)], slots.at[base + 1], far))
        inner.append(first)
        sums.append(wires.send(src.at[dest(1)], slots.at[base + 2], near))
    for way in (1 - long, long):
        sign, base = (1, 0) if way == 0 else (-1, 4)
        for copy in inner[way]:
            yield copy
            copy.wait_recv()
        part = slots.at[base]
        held = src[lax.rem(me + sign * 2 + n, n)] + part[...]
        if way == long:
            held = held + slots[base + 1]
        part[...] = held
        sums.append(wires.send(part, slots.at[base + 3], ways[way][1]))
    for copy in sums:
        yield copy
        copy.wait_recv()
    total[...] = (src[me] + (slots[2] + slots[6])) + (slots[3] + slots[7])


def swift_gather(wires, buf, n, me, ways, long=0, arrived=None):
    block = lambda hops: buf.at[lax.rem(me + hops + n, n)]
    own = buf.at[me]
    far_copies = [wires.send(own, own, ways[way][1]) for way in (1 - long, long)]
    copies = [(wires.send(own, own, ways[way][0]), way, 1) for way in (0, 1)]
    for index, way in enumerate((1 - long, long)):
        sign = 1 if way == 0 else -1
        yield far_copies[index]
        far_copies[index].wait_recv()
        held = block(-2 * sign)
        copies.append((wires.send(held, held, ways[way][0]), way, 3))
        if way == long:
            copies.append((wires.send(held, held, ways[way][1]), way, 4))
        if arrived is not None:
            arrived(held)
    for copy, way, hops in copies:
        yield copy
        copy.wait_recv()
        if arrived is not None:
            arrived(block(-hops if way == 0 else hops))


def direct_gather(wires, buf, n, me, ways, long=0, arrived=None):
    own = buf.at[me]
    copies = []
    for way, (near, far) in enumerate(ways):
        sign = 1 if way == 0 else -1
        if way == long:
            copies.append((wires.send(own, own, far), 2))
        copies.append((wires.send(own, own, near), -sign))
    for copy, hops in copies:
        yield copy
        copy.wait_recv()
        if arrived is not None:
            arrived(buf.at[lax.rem(me + hops + n, n)])


def interleave(streams, order):
    streams = list(streams)
    for index in order:
        next(streams[index], None)
    alive = [] if order else list(streams)
    while alive:
        alive = [stream for stream in alive if next(stream, alive) is not alive]


def neighbours():
    col = lax.axis_index("col")
    y, z = col // NZ, lax.rem(col, NZ)
    at = lambda yy, zz: {"col": lax.rem(yy + NY, NY) * NZ + lax.rem(zz + NZ, NZ)}
    return y, z, at(y + 1, z), at(y - 1, z), at(y, z + 1), at(y, z - 1), at(y, z + 2), at(y, z - 2), at(y + 2, z)


def greet(devices):
    barrier = pltpu.get_barrier_semaphore()
    for device in devices:
        pl.semaphore_signal(barrier, inc=1, device_id=device, device_id_type=MESH)
    return lambda: pl.semaphore_wait(barrier, len(devices))


def sketch_streams(wires, where, pa, pb, oa, ob, slots_a, slots_b, mid_a, mid_b, tail_a, tail_b):
    y, z, y_up, y_down, z_up, z_down, z_up2, z_down2, _ = where
    z_ways = ((z_up, z_up2), (z_down, z_down2))

    def first(g):
        long = g % 2
        yield from ring_reduce(
            wires, pa.at[g], NZ, z, z_up, z_down, slots_a.at[g], mid_a.at[g], long
        )
        yield from ring_reduce(
            wires, mid_a.at[g], NY, y, y_up, y_down, tail_a.at[g], oa.at[g, z, y], long
        )
        yield from ring_gather(wires, oa.at[g, z], NY, y, y_up, y_down, long)
        yield from ring_gather(wires, oa.at[g], NZ, z, z_up, z_down, long)

    def second(g):
        long = g % 2
        yield from ring_reduce(
            wires, pb.at[g], NY, y, y_up, y_down, slots_b.at[g], mid_b.at[g], long
        )
        yield from swift_reduce(
            wires, mid_b.at[g], NZ, z, z_ways, tail_b.at[g], ob.at[g, y, z], long
        )
        yield from swift_gather(wires, ob.at[g, y], NZ, z, z_ways, long)
        yield from ring_gather(wires, ob.at[g], NY, y, y_up, y_down, long)

    return [stream(g) for g in range(GROUPS) for stream in (first, second)]


QUARTER = LANES // 4


def gram_streams(wires, where, core, sibling, others, g, theirs, mine, slots, ga, gb):
    y, z, y_up, y_down, z_up, z_down, z_up2, z_down2, y_far = where
    z_ways = ((z_up, z_up2), (z_down, z_down2))
    y_ways = ((y_up, y_far), (y_down, y_far))

    def relay(h):
        return lambda block: wires.relayed[h].append(wires.send(block, block, sibling))

    def start():
        copy = wires.send(g.at[1 - core], theirs, sibling)
        yield copy
        copy.wait_recv()
        mine[...] = g[core] + theirs[...]
        copies = [
            wires.send(mine, slots.at[step], device) for step, device in enumerate(others)
        ]
        for copy in copies:
            yield copy
            copy.wait_recv()
        total = (mine[...] + slots[1]) + (slots[0] + slots[2])
        ga[core, z, y] = total[:QUARTER]
        for k in range(3):
            gb[core, k, y, z] = total[(k + 1) * QUARTER:(k + 2) * QUARTER]
        wires.begun.append(True)

    def first():
        while not wires.begun:
            yield None
        yield from direct_gather(wires, ga.at[core, z], NY, y, y_ways, 0)
        relay(0)(ga.at[core, z])
        yield from ring_gather(wires, ga.at[core], NZ, z, z_up, z_down, 0, relay(0))
        wires.ended[0].append(True)

    def second(k):
        h = min(k, 1)
        while not wires.begun:
            yield None
        yield from swift_gather(wires, gb.at[core, k, y], NZ, z, z_ways, k % 2)
        part = gb.at[core, k, :, pl.ds(h * NZ // 2, NZ - h * NZ // 2)]
        relay(h)(part.at[y])
        yield from ring_gather(wires, part, NY, y, y_up, y_down, k % 2, relay(h))
        wires.ended[h].append(True)

    return [start(), first(), second(0), second(1), second(2)]


def weight_streams(
    wires, x, sibling, right, left, prepare, compute, src, stage, inbox, slots, total
):
    order = (2, 1, 3, 0)
    sent, merged = wires.sent, []

    def produce():
        yield from prepare()
        for offset in order:
            dest = lax.rem(x + offset, NX)
            for part in range(2):
                compute(dest, part)
                if part == 1:
                    sent.append(wires.send(stage.at[dest], inbox.at[dest], sibling))
                yield None

    def ready(offset):
        turn = order.index(offset)
        while len(sent) <= turn:
            yield None
        if offset not in merged:
            merged.append(offset)
            sent[turn].wait_recv()
            dest = lax.rem(x + offset, NX)
            for h in (0, 1):
                src[h, dest] = src[h, dest] + inbox[dest, h]

    return [produce()] + [
        ring_reduce(wires, src.at[h], NX, x, right, left, slots.at[h], total.at[h], h, ready)
        for h in (0, 1)
    ]


def reduce_kernel(
    a_hbm, lists_ref, sh, sl, xh, xl, wt, tops_out, worst_out, ga_out, gb_out,
    a_ref, table, pa, pb, top, oa, ob, slots_a, slots_b, mid_a, mid_b, tail_a, tail_b,
    g_ref, theirs, mine, slots_g, ga, gb, tops, src, stage, inbox, slots_w, m, rh, rl,
    send_sems, recv_sems, keep_sems, *, scale,
):
    where = neighbours()
    y, z = where[:2]
    row = lax.axis_index("row")
    x, core = row // 2, lax.rem(row, 2)
    at = lambda xx, cc: {"row": lax.rem(xx, NX) * 2 + cc}
    sibling = at(x, 1 - core)
    others = [at(x + step, core) for step in range(1, NX)]
    crossed = [at(x + step, 1 - core) for step in range(1, NX)]
    arrive = greet(list(where[2:]) + [sibling] + others + crossed)
    rows, cols = a_ref.shape
    fetch = pltpu.make_async_copy(a_hbm, a_ref, keep_sems.at[2])
    fetch.start()
    signs = lists_ref[0:1, :].astype(F32)
    fill_table(table, lists_ref[1:2, :], (y * NZ + z) * cols)
    fetch.wait()
    sketch_group(0, a_ref, signs, table, pa, pb, scale)
    arrive()
    wires = Wires(send_sems, recv_sems)
    wires.relayed, wires.ended, wires.begun = ([], []), ([], []), []
    wires.sent, wires.halved, wires.worst = [], [], []
    streams = sketch_streams(
        wires, where, pa, pb, oa, ob, slots_a, slots_b, mid_a, mid_b, tail_a, tail_b
    )
    for g in range(GROUPS):
        if g > 0:
            sketch_group(g, a_ref, signs, table, pa, pb, scale)
        for stream in streams[2 * g:2 * g + 2]:
            next(stream)
    top[...] = jnp.max(jnp.abs(a_ref[...]).reshape(rows // 8, 8, cols), axis=0)
    told = [
        wires.send(top, tops.at[index], device)
        for index, device in enumerate([sibling] + others + crossed)
    ]
    interleave(streams, SKETCH_ORDER)
    interleave(streams, ())

    def block(index):
        parts = [oa[g, index, yy] for g in range(GROUPS) for yy in range(NY)]
        parts += [ob[g, yy, index] for g in range(GROUPS) for yy in range(NY)]
        return split(jnp.concatenate(parts, axis=0))

    right = block(z)
    half = LANES // 2
    for h in (0, 1):
        out = mm_pair(block(NY * h + y), right, 0, 0)
        for c in (0, 1):
            g_ref[c, h * half:(h + 1) * half] = out[c * half:(c + 1) * half]

    def prepare():
        for copy in told:
            copy.wait_recv()
        most = top[...]
        for index in range(len(told)):
            most = jnp.maximum(most, tops[index])
        most = jnp.maximum(jnp.max(most, axis=0, keepdims=True), 1e-30)
        tops[0] = jnp.broadcast_to(most, top.shape)
        tops[1] = jnp.broadcast_to(1.0 / most, top.shape)
        tops_out[...] = tops[0, :, pl.ds(pl.multiple_of(row * LANES, LANES), LANES)]
        yield None
        for yy in range(NY):
            here = slice(yy * PERIOD, (yy + 1) * PERIOD)
            for zz in range(NZ):
                columns = slice(zz * LANES, (zz + 1) * LANES)
                pieces = [r for g in range(GROUPS) for r in (oa[g, zz, yy], ob[g, yy, zz])]
                sh[here, columns], sl[here, columns] = split(jnp.concatenate(pieces, axis=0))
            yield None

    def compute(dest, part):
        columns = pl.ds(pl.multiple_of(dest * 2 * LANES, 2 * LANES), 2 * LANES)
        wide = sh.shape[1] // 2
        samples = slice(part * wide, (part + 1) * wide)
        left = split(a_ref[:, columns] * tops[1, 0:1, columns])
        out = mm_pair(left, (sh[:, samples], sl[:, samples]), 0, 0)
        ours = jnp.where(core == 0, out[:LANES], out[LANES:])
        theirs = jnp.where(core == 0, out[LANES:], out[:LANES])
        for h in (0, 1):
            src[h, dest, :, samples] = ours[h * half:(h + 1) * half]
            stage[dest, h, :, samples] = theirs[h * half:(h + 1) * half]

    streams = gram_streams(
        wires, where, core, sibling, others, g_ref, theirs, mine, slots_g, ga, gb
    )
    next(streams[0])
    weights = weight_streams(
        wires, x, sibling, others[0], others[2], prepare, compute, src, stage, inbox, slots_w, wt
    )
    kept = [
        pltpu.make_async_copy(ga, ga_out, keep_sems.at[0]),
        pltpu.make_async_copy(gb, gb_out, keep_sems.at[1]),
    ]
    early = factor_first(wires, ga, gb, xh, xl, m, rh, rl)
    late = factor_second(wires, kept, ga, gb, xh, xl, m, rh, rl)
    streams = streams + [early] + weights + [late]
    interleave(streams, GRAM_ORDER)
    interleave(streams, ())
    worst = functools.reduce(jnp.maximum, wires.worst)
    worst_out[...] = jnp.broadcast_to(worst, worst_out.shape)
    wires.drain()
    for copy in kept:
        copy.wait()


SKETCH_ORDER = (
    0, 2, 1, 4, 3, 6, 0, 0, 2, 2, 4, 5, 4, 6, 6, 0, 1, 1, 0, 7, 2, 2, 4, 4, 3, 3, 6, 0,
    6, 1, 1, 5, 0, 1, 1, 1, 5, 2, 2, 4, 4, 3, 3, 7, 7, 0, 3, 3, 3, 4, 2, 6, 6, 1, 1, 0,
    0, 5, 5, 5, 5, 5, 4, 4, 3, 7, 2, 2, 7, 6, 7, 7, 7, 3, 0, 0, 1, 1, 1, 1, 4, 2, 4, 2,
    6, 6, 5, 5, 7, 7, 0, 3, 3, 3, 3, 4, 1, 1, 2, 6, 6, 1, 5, 5, 5, 5, 7, 7, 7, 7, 6, 0,
    0, 3, 3, 1, 1, 3, 4, 4, 2, 2, 5, 5, 5, 7, 7, 7, 6, 6, 0, 0, 4, 4, 1, 3, 3, 2, 2, 6,
    6, 0, 5, 0, 5, 4, 4, 2, 2, 7, 7, 6, 3, 6, 0, 2, 4, 5, 6, 7,
)
GRAM_ORDER = (
    6, 6, 6, 0, 6, 6, 6, 6, 6, 0, 0, 0, 2, 1, 3, 6, 6, 6, 2, 2, 2, 2, 1, 1, 1, 3, 3, 3,
    3, 6, 6, 2, 2, 6, 4, 7, 2, 8, 1, 1, 3, 3, 3, 4, 4, 4, 4, 1, 2, 2, 1, 7, 4, 4, 8, 3,
    3, 4, 1, 1, 2, 3, 1, 5, 5, 5, 5, 5, 5, 5, 5, 5, 5, 5, 5, 4, 4, 5, 5, 5, 5, 5, 4, 5,
    5, 5, 5, 5, 5, 5, 7, 7, 8, 8, 9, 9, 9, 9, 9, 9, 9, 9, 9, 9, 9, 9, 9, 9, 9, 9, 9, 9,
    9, 9, 9, 9,
)
COPIES = 300


def reduce_all(a, lists, scale):
    rows, cols = a.shape
    samples = lists.shape[1]
    half = LANES // 2
    array = lambda *shape: pltpu.VMEM(shape, F32)
    blocks_a = (GROUPS, NZ, NY, ROWS_A, LANES)
    blocks_b = (GROUPS, NY, NZ, ROWS_B, LANES)
    gram_a = (2, NZ, NY, QUARTER, LANES)
    gram_b = (2, 3, NY, NZ, QUARTER, LANES)
    far = pl.BlockSpec(memory_space=pltpu.HBM)
    return pl.pallas_call(
        functools.partial(reduce_kernel, scale=scale),
        out_shape=(
            jax.ShapeDtypeStruct((rows, samples), BF16),
            jax.ShapeDtypeStruct((rows, samples), BF16),
            jax.ShapeDtypeStruct((samples, samples), BF16),
            jax.ShapeDtypeStruct((samples, samples), BF16),
            jax.ShapeDtypeStruct((2, half, samples), F32),
            jax.ShapeDtypeStruct((8, LANES), F32),
            jax.ShapeDtypeStruct((8, NB), F32),
            jax.ShapeDtypeStruct(gram_a, F32),
            jax.ShapeDtypeStruct(gram_b, F32),
        ),
        in_specs=[far, VMEM],
        out_specs=(VMEM,) * 7 + (far,) * 2,
        scratch_shapes=[
            array(rows, cols),
            pltpu.VMEM((cols, samples), BF16),
            array(*blocks_a),
            array(*blocks_b),
            array(8, cols),
            array(*blocks_a),
            array(*blocks_b),
            array(GROUPS, NZ - 1, NY, ROWS_A, LANES),
            array(GROUPS, NY - 1, NZ, ROWS_B, LANES),
            array(GROUPS, NY, ROWS_A, LANES),
            array(GROUPS, NZ, ROWS_B, LANES),
            array(GROUPS, NY - 1, ROWS_A, LANES),
            array(GROUPS, NZ, ROWS_B, LANES),
            array(2, LANES, LANES),
            array(LANES, LANES),
            array(LANES, LANES),
            array(NX - 1, LANES, LANES),
            array(*gram_a),
            array(*gram_b),
            array(2 * NX - 1, 8, cols),
            array(2, NX, half, samples),
            array(NX, 2, half, samples),
            array(NX, 2, half, samples),
            array(2, NX - 1, half, samples),
            array(samples, samples),
            pltpu.VMEM((samples // 2, samples), BF16),
            pltpu.VMEM((samples // 2, samples), BF16),
            pltpu.SemaphoreType.DMA((COPIES,)),
            pltpu.SemaphoreType.DMA((COPIES,)),
            pltpu.SemaphoreType.DMA((3,)),
        ],
        compiler_params=pltpu.CompilerParams(
            collective_id=0, has_side_effects=True, vmem_limit_bytes=MEGA_LIMIT
        ),
    )(a, lists)


NB = 256
STEPS = 2
CONVERGED = 4e-4


def load_gram(ga, gb, m, h, upper):
    for core in range(2):
        for y in range(NY):
            low = (h * NY + y) * LANES + core * 2 * QUARTER
            for z in range(low // NB * 2 if upper else h * NZ // 2, NZ):
                columns = slice(z * LANES, (z + 1) * LANES)
                above = ga[core, z, y] if h == 0 else gb[core, 1, y, z]
                m[low:low + QUARTER, columns] = above
                m[low + QUARTER:low + 2 * QUARTER, columns] = gb[core, 2 * h, y, z]


def masks():
    rows = lax.broadcasted_iota(jnp.int32, (NB, NB), 0)
    cols = lax.broadcasted_iota(jnp.int32, (NB, NB), 1)
    eye = (rows == cols).astype(F32)
    half = jnp.where(rows > cols, 1.0, jnp.where(rows == cols, 0.5, 0.0)).astype(F32)
    return eye, half


def subtract(m, rest, columns, left, right):
    m[rest, columns] = m[rest, columns] - mm_pair(left, right, 0, 0)


def eliminate(wires, low, last, xh, xl, m, rh, rl):
    n, nb = m.shape[0], NB
    high = low + nb
    eye, half = masks()
    block = m[low:high, low:high]
    down = lax.rsqrt(jnp.sum(block * eye, axis=1, keepdims=True))
    across = lax.rsqrt(jnp.sum(block * eye, axis=0, keepdims=True))
    block = block * down * across
    x = eye - half * (block - eye)
    for step in range(STEPS + 2):
        dot = mm1 if step < STEPS else mm3
        residual = dot(dot(x, block, 1, 0), x, 1, 1) - eye
        x = x - mm1(half * residual, x, 1, 0)
        yield None
    off = jnp.where(jnp.abs(residual) < CONVERGED, 0.0, 1.0)
    wires.worst.append(jnp.max(off, axis=0, keepdims=True))
    x = x * across
    m[low:high, low:high] = eye
    pivot = mm3(x, m[low:high, :], 1, 0)
    keep = lax.broadcasted_iota(jnp.int32, (nb, n), 1) < high
    pair = split(pivot)
    xh[low:high, :] = jnp.where(keep, pair[0], 0)
    xl[low:high, :] = jnp.where(keep, pair[1], 0)
    if high < n // 2 + 1:
        rh[low:high, :], rl[low:high, :] = pair
    yield None
    if high < last:
        m[high:last, low:high] = jnp.zeros((last - high, nb), F32)
        left = (pair[0][:, high:last], pair[1][:, high:last])
        for columns in (slice(0, high), slice(high, n)):
            subtract(m, slice(high, last), columns, left, (pair[0][:, columns], pair[1][:, columns]))
        yield None


def factor_first(wires, ga, gb, xh, xl, m, rh, rl):
    while len(wires.ended[0]) < 2:
        yield None
    for copy in wires.relayed[0]:
        yield copy
        copy.wait_recv()
    n = m.shape[0]
    load_gram(ga, gb, m, 0, True)
    for low in range(0, n // 2, NB):
        yield from eliminate(wires, low, n // 2, xh, xl, m, rh, rl)
    wires.halved.append(True)


def factor_second(wires, kept, ga, gb, xh, xl, m, rh, rl):
    while not wires.halved or len(wires.ended[1]) < 2:
        yield None
    for copy in wires.relayed[1]:
        yield copy
        copy.wait_recv()
    for copy in kept:
        copy.start()
    n = m.shape[0]
    middle = n // 2
    load_gram(ga, gb, m, 1, True)
    m[middle:, :middle] = jnp.zeros((n - middle, middle), F32)
    for low in range(middle, n, NB):
        rest = slice(low, low + NB)
        left = (rh[:, rest], rl[:, rest])
        subtract(m, rest, slice(low, n), left, (rh[:, low:], rl[:, low:]))
        above = slice(0, middle)
        subtract(m, rest, above, left, (xh[above, above], xl[above, above]))
        yield None
    for low in range(middle, n, NB):
        yield from eliminate(wires, low, n, xh, xl, m, rh, rl)


def guard_kernel(worst, ga_in, gb_in, xh_in, xl_in, xh_out, xl_out, ga, gb, m, xh, xl, sems):
    @pl.when(jnp.max(worst[...]) > 0.0)
    def _():
        loads = [
            pltpu.make_async_copy(ga_in, ga, sems.at[0]),
            pltpu.make_async_copy(gb_in, gb, sems.at[1]),
        ]
        for copy in loads:
            copy.start()
        for copy in loads:
            copy.wait()
        load_gram(ga, gb, m, 0, False)
        load_gram(ga, gb, m, 1, False)
        n = m.shape[0]
        m[n // 2:, :n // 2] = m[:n // 2, n // 2:].T
        lane = lax.broadcasted_iota(jnp.int32, (1, n), 1)
        chunk = 128

        def column(j, carry):
            row = m[pl.ds(j, 1), :]
            scale = lax.rsqrt(jnp.sum(jnp.where(lane == j, row, 0.0), axis=1, keepdims=True))
            pivot = jnp.where(lane == j, 1.0, row) * scale
            m[pl.ds(j, 1), :] = jnp.where(lane <= j, pivot, 0.0)

            def update(part, carry):
                here = pl.ds(pl.multiple_of(part * chunk, chunk), chunk)
                below = part * chunk + lax.broadcasted_iota(jnp.int32, (chunk, 1), 0) > j
                old = m[here, :]
                entry = jnp.sum(jnp.where(lane == j, old, 0.0), axis=1, keepdims=True) * scale
                new = jnp.where(lane == j, 0.0, old) - entry * pivot
                m[here, :] = jnp.where(below, new, old)
                return carry

            return lax.fori_loop(j // chunk, n // chunk, update, carry)

        lax.fori_loop(0, n, column, 0)
        xh[...], xl[...] = split(m[...])
        stores = [
            pltpu.make_async_copy(xh, xh_out, sems.at[0]),
            pltpu.make_async_copy(xl, xl_out, sems.at[1]),
        ]
        for copy in stores:
            copy.start()
        for copy in stores:
            copy.wait()


def guard(worst, ga, gb, xh, xl):
    n = xh.shape[0]
    anywhere = pl.BlockSpec(memory_space=pl.ANY)
    return pl.pallas_call(
        guard_kernel,
        out_shape=(jax.ShapeDtypeStruct((n, n), BF16),) * 2,
        in_specs=[VMEM] + [anywhere] * 4,
        out_specs=(anywhere, anywhere),
        input_output_aliases={3: 0, 4: 1},
        scratch_shapes=[
            pltpu.VMEM(ga.shape, F32),
            pltpu.VMEM(gb.shape, F32),
            pltpu.VMEM((n, n), F32),
            pltpu.VMEM((n, n), BF16),
            pltpu.VMEM((n, n), BF16),
            pltpu.SemaphoreType.DMA((2,)),
        ],
        compiler_params=pltpu.CompilerParams(vmem_limit_bytes=GUARD_LIMIT),
    )(worst, ga, gb, xh, xl)


def outputs_kernel(
    sh, sl, xh, xl, wt, tops, basis_ref, proj_ref, stage, inbox, send_sems, recv_sems, *, root
):
    row = lax.axis_index("row")
    x, core = row // 2, lax.rem(row, 2)
    turns = [(step, flip) for step in (2, 1, 3) for flip in (0, 1)] + [(0, 1)]
    place_of = lambda step, flip: lax.rem(x + step, NX) * 2 + (1 - core if flip else core)
    peers = [place_of(step, flip) for step, flip in turns]
    arrive = greet([{"row": peer} for peer in peers])
    n = xh.shape[0]
    wide = 256
    pair = split(wt[...].reshape(LANES, xh.shape[0]))
    for low in range(0, n, wide):
        high = low + wide
        out = mm_pair(
            (xh[low:high, :high], xl[low:high, :high]), (pair[0][:, :high], pair[1][:, :high]), 1, 1
        )
        out = out * tops[0:1, :]
        for sub in range(wide // LANES):
            stage[low // LANES + sub] = out[sub * LANES:(sub + 1) * LANES]
    arrive()
    copies = []
    for index, peer in enumerate(peers):
        copy = pltpu.make_async_remote_copy(
            src_ref=stage.at[peer],
            dst_ref=inbox.at[index],
            send_sem=send_sems.at[index],
            recv_sem=recv_sems.at[index],
            device_id={"row": peer},
            device_id_type=MESH,
        )
        copy.start()
        copies.append(copy)
    for low in range(0, n, wide):
        high = low + wide
        basis = mm_pair(
            (sh[:, :high], sl[:, :high]), (xh[low:high, :high], xl[low:high, :high]), 1, 1
        )
        basis_ref[:, low:high] = basis * root
    columns = lambda owner: pl.ds(pl.multiple_of(owner * LANES, LANES), LANES)
    proj_ref[:, columns(row)] = stage[row]
    for index, copy in enumerate(copies):
        copy.wait()
        step, flip = turns[index]
        proj_ref[:, columns(place_of(NX - step, flip))] = inbox[index]


def outputs(sh, sl, xh, xl, wt, tops, root):
    rows, n = sh.shape
    count = 2 * NX
    return pl.pallas_call(
        functools.partial(outputs_kernel, root=root),
        out_shape=(
            jax.ShapeDtypeStruct((rows, n), F32),
            jax.ShapeDtypeStruct((n // count, count * LANES), F32),
        ),
        in_specs=[VMEM] * 6,
        out_specs=(VMEM, VMEM),
        scratch_shapes=[
            pltpu.VMEM((count, LANES, LANES), F32),
            pltpu.VMEM((count - 1, LANES, LANES), F32),
            pltpu.SemaphoreType.DMA((count - 1,)),
            pltpu.SemaphoreType.DMA((count - 1,)),
        ],
        compiler_params=pltpu.CompilerParams(
            collective_id=1, has_side_effects=True, vmem_limit_bytes=OUTPUT_LIMIT
        ),
    )(sh, sl, xh, xl, wt, tops)


def body(expert_matrix, col_signs, sample_ids):
    local_cols = expert_matrix.shape[1]
    col_total = local_cols * lax.axis_size("col")
    model_width = expert_matrix.shape[0] * lax.axis_size("row")
    lists = jnp.stack([col_signs, sample_ids])
    sh, sl, xh, xl, wt, tops, worst, ga, gb = reduce_all(
        expert_matrix, lists, 1.0 / math.sqrt(col_total)
    )
    xh, xl = guard(worst, ga, gb, xh, xl)
    return outputs(sh, sl, xh, xl, wt, tops, math.sqrt(model_width))


def solution(mesh):
    in_specs = (P("row", "col"), P("col"), P())
    out_specs = (P("row", None), P("row", "col"))
    return jax.shard_map(body, mesh=mesh, in_specs=in_specs, out_specs=out_specs, check_vma=False)
```

```python
import functools
import math

import jax
import jax.numpy as jnp
from jax import lax
from jax.experimental import pallas as pl
from jax.experimental.pallas import tpu as pltpu
from jax.sharding import PartitionSpec as P

MESH = pl.DeviceIdType.MESH
F32 = jnp.float32
BF16 = jnp.bfloat16
NY, NZ, NX = 4, 8, 4
LANES = 128
VMEM = pl.BlockSpec(memory_space=pltpu.VMEM)
MEGA_LIMIT = 40 << 20
GUARD_LIMIT = 24 << 20
OUTPUT_LIMIT = 16 << 20


def split(value):
    high = value.astype(BF16)
    return high, (value - high.astype(F32)).astype(BF16)


def mm(a, b, ca, cb):
    return lax.dot_general(a, b, (((ca,), (cb,)), ((), ())), preferred_element_type=F32)


def mm_pair(a, b, ca, cb):
    (ah, al), (bh, bl) = a, b
    return mm(ah, bh, ca, cb) + (mm(ah, bl, ca, cb) + mm(al, bh, ca, cb))


def mm3(a, b, ca, cb):
    return mm_pair(split(a), split(b), ca, cb)


def mm1(a, b, ca, cb):
    return mm(a.astype(BF16), b.astype(BF16), ca, cb)


GROUPS = 4
ROWS_A, ROWS_B = 24, 32
PERIOD = GROUPS * (ROWS_A + ROWS_B)


def signs_of(value):
    for amount in (8, 4, 2, 1):
        value = value ^ (value >> amount)
    return (1 - 2 * (value & 1)).astype(F32)


def fill_table(table, ids, offset):
    cols, samples = table.shape
    step = 32
    index = lax.broadcasted_iota(jnp.int32, (step, samples), 0)
    low = signs_of(index & ids)
    high = signs_of((offset + step * index) & ids)
    for part in range(cols // step):
        table[part * step:(part + 1) * step, :] = (low * high[part:part + 1, :]).astype(BF16)


def sketch_group(g, a_ref, signs, table, pa, pb, scale):
    size = ROWS_A + ROWS_B
    parts = [a_ref[y * PERIOD + g * size:y * PERIOD + (g + 1) * size, :] for y in range(NY)]
    high, low = split(jnp.concatenate(parts, axis=0) * signs)
    wide = 256
    for part in range(table.shape[1] // wide):
        columns = slice(part * wide, (part + 1) * wide)
        out = (mm(high, table[:, columns], 1, 0) + mm(low, table[:, columns], 1, 0)) * scale
        for sub in range(wide // LANES):
            block = part * (wide // LANES) + sub
            for y in range(NY):
                piece = out[y * size:(y + 1) * size, sub * LANES:(sub + 1) * LANES]
                pa[g, block, y] = piece[:ROWS_A]
                pb[g, y, block] = piece[ROWS_A:]


class Wires:
    def __init__(self, send_sems, recv_sems):
        self.send_sems, self.recv_sems = send_sems, recv_sems
        self.copies = []

    def send(self, src, dst, device):
        index = len(self.copies)
        copy = pltpu.make_async_remote_copy(
            src_ref=src,
            dst_ref=dst,
            send_sem=self.send_sems.at[index],
            recv_sem=self.recv_sems.at[index],
            device_id=device,
            device_id_type=MESH,
        )
        copy.start()
        self.copies.append(copy)
        return copy

    def drain(self):
        for copy in self.copies:
            copy.wait_send()


def ring_reduce(wires, src, n, me, right, left, slots, total, long=0, ready=None):
    far = n // 2
    ways = []
    for way, (there, sign) in enumerate(((right, 1), (left, -1))):
        hops = far if way == long else far - 1
        ways.append((there, sign, hops, 0 if way == long else far))
    ways.sort(key=lambda way: -way[2])
    pending = [None, None]
    for step in range(far):
        for index, (there, sign, hops, base) in enumerate(ways):
            turn = step - (far - hops)
            if turn < 0:
                continue
            dest = lax.rem(me + sign * (hops - turn) + n, n)
            if ready is not None:
                yield from ready(sign * (hops - turn) % n)
            block = src.at[dest]
            if turn > 0:
                yield pending[index]
                pending[index].wait_recv()
                block = slots.at[base + turn - 1]
                block[...] = block[...] + src[dest]
            pending[index] = wires.send(block, slots.at[base + turn], there)
    if ready is not None:
        yield from ready(0)
    for copy in pending:
        yield copy
        copy.wait_recv()
    total[...] = src[me] + (slots[far - 1] + slots[n - 2])


def ring_gather(wires, buf, n, me, right, left, long=0, arrived=None):
    far = n // 2
    ways = ((right, 1, far if long == 0 else far - 1), (left, -1, far if long == 1 else far - 1))
    pending = [wires.send(buf.at[me], buf.at[me], there) for there, _, _ in ways]
    for step in range(1, far + 1):
        for index, (there, sign, hops) in enumerate(ways):
            if step > hops:
                continue
            origin = lax.rem(me - sign * step + n, n)
            yield pending[index]
            pending[index].wait_recv()
            block = buf.at[origin]
            if step < hops:
                pending[index] = wires.send(block, block, there)
            if arrived is not None:
                arrived(block)


def swift_reduce(wires, src, n, me, ways, slots, total, long=0):
    inner, sums = [], []
    for way, (near, far) in enumerate(ways):
        sign, base = (1, 0) if way == 0 else (-1, 4)
        dest = lambda hops: lax.rem(me + sign * hops + n, n)
        first = [wires.send(src.at[dest(3)], slots.at[base], near)]
        if way == long:
            first.append(wires.send(src.at[dest(4)], slots.at[base + 1], far))
        inner.append(first)
        sums.append(wires.send(src.at[dest(1)], slots.at[base + 2], near))
    for way in (1 - long, long):
        sign, base = (1, 0) if way == 0 else (-1, 4)
        for copy in inner[way]:
            yield copy
            copy.wait_recv()
        part = slots.at[base]
        held = src[lax.rem(me + sign * 2 + n, n)] + part[...]
        if way == long:
            held = held + slots[base + 1]
        part[...] = held
        sums.append(wires.send(part, slots.at[base + 3], ways[way][1]))
    for copy in sums:
        yield copy
        copy.wait_recv()
    total[...] = (src[me] + (slots[2] + slots[6])) + (slots[3] + slots[7])


def swift_gather(wires, buf, n, me, ways, long=0, arrived=None):
    block = lambda hops: buf.at[lax.rem(me + hops + n, n)]
    own = buf.at[me]
    far_copies = [wires.send(own, own, ways[way][1]) for way in (1 - long, long)]
    copies = [(wires.send(own, own, ways[way][0]), way, 1) for way in (0, 1)]
    for index, way in enumerate((1 - long, long)):
        sign = 1 if way == 0 else -1
        yield far_copies[index]
        far_copies[index].wait_recv()
        held = block(-2 * sign)
        copies.append((wires.send(held, held, ways[way][0]), way, 3))
        if way == long:
            copies.append((wires.send(held, held, ways[way][1]), way, 4))
        if arrived is not None:
            arrived(held)
    for copy, way, hops in copies:
        yield copy
        copy.wait_recv()
        if arrived is not None:
            arrived(block(-hops if way == 0 else hops))


def direct_gather(wires, buf, n, me, ways, long=0, arrived=None):
    own = buf.at[me]
    copies = []
    for way, (near, far) in enumerate(ways):
        sign = 1 if way == 0 else -1
        if way == long:
            copies.append((wires.send(own, own, far), 2))
        copies.append((wires.send(own, own, near), -sign))
    for copy, hops in copies:
        yield copy
        copy.wait_recv()
        if arrived is not None:
            arrived(buf.at[lax.rem(me + hops + n, n)])


def interleave(streams, order):
    streams = list(streams)
    for index in order:
        next(streams[index], None)
    alive = [] if order else list(streams)
    while alive:
        alive = [stream for stream in alive if next(stream, alive) is not alive]


def neighbours():
    col = lax.axis_index("col")
    y, z = col // NZ, lax.rem(col, NZ)
    at = lambda yy, zz: {"col": lax.rem(yy + NY, NY) * NZ + lax.rem(zz + NZ, NZ)}
    return y, z, at(y + 1, z), at(y - 1, z), at(y, z + 1), at(y, z - 1), at(y, z + 2), at(y, z - 2), at(y + 2, z)


def greet(devices):
    barrier = pltpu.get_barrier_semaphore()
    for device in devices:
        pl.semaphore_signal(barrier, inc=1, device_id=device, device_id_type=MESH)
    return lambda: pl.semaphore_wait(barrier, len(devices))


def sketch_streams(wires, where, pa, pb, oa, ob, slots_a, slots_b, mid_a, mid_b, tail_a, tail_b):
    y, z, y_up, y_down, z_up, z_down, z_up2, z_down2, _ = where
    z_ways = ((z_up, z_up2), (z_down, z_down2))

    def first(g):
        long = g % 2
        yield from ring_reduce(
            wires, pa.at[g], NZ, z, z_up, z_down, slots_a.at[g], mid_a.at[g], long
        )
        yield from ring_reduce(
            wires, mid_a.at[g], NY, y, y_up, y_down, tail_a.at[g], oa.at[g, z, y], long
        )
        yield from ring_gather(wires, oa.at[g, z], NY, y, y_up, y_down, long)
        yield from ring_gather(wires, oa.at[g], NZ, z, z_up, z_down, long)

    def second(g):
        long = g % 2
        yield from ring_reduce(
            wires, pb.at[g], NY, y, y_up, y_down, slots_b.at[g], mid_b.at[g], long
        )
        yield from swift_reduce(
            wires, mid_b.at[g], NZ, z, z_ways, tail_b.at[g], ob.at[g, y, z], long
        )
        yield from swift_gather(wires, ob.at[g, y], NZ, z, z_ways, long)
        yield from ring_gather(wires, ob.at[g], NY, y, y_up, y_down, long)

    return [stream(g) for g in range(GROUPS) for stream in (first, second)]


QUARTER = LANES // 4


def gram_streams(wires, where, core, sibling, others, g, theirs, mine, slots, ga, gb):
    y, z, y_up, y_down, z_up, z_down, z_up2, z_down2, y_far = where
    z_ways = ((z_up, z_up2), (z_down, z_down2))
    y_ways = ((y_up, y_far), (y_down, y_far))

    def relay(h):
        return lambda block: wires.relayed[h].append(wires.send(block, block, sibling))

    def start():
        copy = wires.send(g.at[1 - core], theirs, sibling)
        yield copy
        copy.wait_recv()
        mine[...] = g[core] + theirs[...]
        copies = [
            wires.send(mine, slots.at[step], device) for step, device in enumerate(others)
        ]
        for copy in copies:
            yield copy
            copy.wait_recv()
        total = (mine[...] + slots[1]) + (slots[0] + slots[2])
        ga[core, z, y] = total[:QUARTER]
        for k in range(3):
            gb[core, k, y, z] = total[(k + 1) * QUARTER:(k + 2) * QUARTER]
        wires.begun.append(True)

    def first():
        while not wires.begun:
            yield None
        yield from direct_gather(wires, ga.at[core, z], NY, y, y_ways, 0)
        relay(0)(ga.at[core, z])
        yield from swift_gather(wires, ga.at[core], NZ, z, z_ways, 0, relay(0))
        wires.ended[0].append(True)

    def second(k):
        h = min(k, 1)
        while not wires.begun:
            yield None
        yield from swift_gather(wires, gb.at[core, k, y], NZ, z, z_ways, k % 2)
        part = gb.at[core, k, :, pl.ds(h * NZ // 2, NZ - h * NZ // 2)]
        relay(h)(part.at[y])
        yield from ring_gather(wires, part, NY, y, y_up, y_down, k % 2, relay(h))
        wires.ended[h].append(True)

    return [start(), first(), second(0), second(1), second(2)]


def weight_streams(
    wires, x, sibling, right, left, prepare, compute, src, stage, inbox, slots, total
):
    order = (2, 1, 3, 0)
    sent, merged = wires.sent, []

    def produce():
        yield from prepare()
        for offset in order:
            dest = lax.rem(x + offset, NX)
            for part in range(2):
                compute(dest, part)
                if part == 1:
                    sent.append(wires.send(stage.at[dest], inbox.at[dest], sibling))
                yield None

    def ready(offset):
        turn = order.index(offset)
        while len(sent) <= turn:
            yield None
        if offset not in merged:
            merged.append(offset)
            sent[turn].wait_recv()
            dest = lax.rem(x + offset, NX)
            for h in (0, 1):
                src[h, dest] = src[h, dest] + inbox[dest, h]

    return [produce()] + [
        ring_reduce(wires, src.at[h], NX, x, right, left, slots.at[h], total.at[h], h, ready)
        for h in (0, 1)
    ]


def reduce_kernel(
    a_hbm, lists_ref, sh, sl, xh, xl, wt, tops_out, worst_out, ga_out, gb_out,
    a_ref, table, pa, pb, top, oa, ob, slots_a, slots_b, mid_a, mid_b, tail_a, tail_b,
    g_ref, theirs, mine, slots_g, ga, gb, tops, src, stage, inbox, slots_w, m, rh, rl,
    send_sems, recv_sems, keep_sems, *, scale,
):
    where = neighbours()
    y, z = where[:2]
    row = lax.axis_index("row")
    x, core = row // 2, lax.rem(row, 2)
    at = lambda xx, cc: {"row": lax.rem(xx, NX) * 2 + cc}
    sibling = at(x, 1 - core)
    others = [at(x + step, core) for step in range(1, NX)]
    crossed = [at(x + step, 1 - core) for step in range(1, NX)]
    arrive = greet(list(where[2:]) + [sibling] + others + crossed)
    rows, cols = a_ref.shape
    fetch = pltpu.make_async_copy(a_hbm, a_ref, keep_sems.at[2])
    fetch.start()
    signs = lists_ref[0:1, :].astype(F32)
    fill_table(table, lists_ref[1:2, :], (y * NZ + z) * cols)
    fetch.wait()
    sketch_group(0, a_ref, signs, table, pa, pb, scale)
    arrive()
    wires = Wires(send_sems, recv_sems)
    wires.relayed, wires.ended, wires.begun = ([], []), ([], []), []
    wires.sent, wires.halved, wires.worst = [], [], []
    streams = sketch_streams(
        wires, where, pa, pb, oa, ob, slots_a, slots_b, mid_a, mid_b, tail_a, tail_b
    )
    for g in range(GROUPS):
        if g > 0:
            sketch_group(g, a_ref, signs, table, pa, pb, scale)
        for stream in streams[2 * g:2 * g + 2]:
            next(stream)
    top[...] = jnp.max(jnp.abs(a_ref[...]).reshape(rows // 8, 8, cols), axis=0)
    told = [
        wires.send(top, tops.at[index], device)
        for index, device in enumerate([sibling] + others + crossed)
    ]
    interleave(streams, SKETCH_ORDER)
    interleave(streams, ())

    def block(index):
        parts = [oa[g, index, yy] for g in range(GROUPS) for yy in range(NY)]
        parts += [ob[g, yy, index] for g in range(GROUPS) for yy in range(NY)]
        return split(jnp.concatenate(parts, axis=0))

    right = block(z)
    half = LANES // 2
    left = [jnp.concatenate(pair, axis=1) for pair in zip(block(y), block(NY + y))]
    out = mm_pair(left, right, 0, 0)
    for h in (0, 1):
        for c in (0, 1):
            low = (2 * h + c) * half
            g_ref[c, h * half:(h + 1) * half] = out[low:low + half]

    def prepare():
        for copy in told:
            copy.wait_recv()
        most = top[...]
        for index in range(len(told)):
            most = jnp.maximum(most, tops[index])
        most = jnp.maximum(jnp.max(most, axis=0, keepdims=True), 1e-30)
        tops[0] = jnp.broadcast_to(most, top.shape)
        tops[1] = jnp.broadcast_to(1.0 / most, top.shape)
        tops_out[...] = tops[0, :, pl.ds(pl.multiple_of(row * LANES, LANES), LANES)]
        yield None
        for yy in range(NY):
            here = slice(yy * PERIOD, (yy + 1) * PERIOD)
            for zz in range(NZ):
                columns = slice(zz * LANES, (zz + 1) * LANES)
                pieces = [r for g in range(GROUPS) for r in (oa[g, zz, yy], ob[g, yy, zz])]
                sh[here, columns], sl[here, columns] = split(jnp.concatenate(pieces, axis=0))
            yield None

    def compute(dest, part):
        columns = pl.ds(pl.multiple_of(dest * 2 * LANES, 2 * LANES), 2 * LANES)
        wide = sh.shape[1] // 2
        samples = slice(part * wide, (part + 1) * wide)
        left = split(a_ref[:, columns] * tops[1, 0:1, columns])
        out = mm_pair(left, (sh[:, samples], sl[:, samples]), 0, 0)
        ours = jnp.where(core == 0, out[:LANES], out[LANES:])
        theirs = jnp.where(core == 0, out[LANES:], out[:LANES])
        for h in (0, 1):
            src[h, dest, :, samples] = ours[h * half:(h + 1) * half]
            stage[dest, h, :, samples] = theirs[h * half:(h + 1) * half]

    streams = gram_streams(
        wires, where, core, sibling, others, g_ref, theirs, mine, slots_g, ga, gb
    )
    next(streams[0])
    weights = weight_streams(
        wires, x, sibling, others[0], others[2], prepare, compute, src, stage, inbox, slots_w, wt
    )
    kept = [
        pltpu.make_async_copy(ga, ga_out, keep_sems.at[0]),
        pltpu.make_async_copy(gb, gb_out, keep_sems.at[1]),
    ]
    early = factor_first(wires, ga, gb, xh, xl, m, rh, rl)
    late = factor_second(wires, kept, ga, gb, xh, xl, m, rh, rl)
    streams = streams + [early] + weights + [late]
    interleave(streams, GRAM_ORDER)
    interleave(streams, ())
    worst = functools.reduce(jnp.maximum, wires.worst)
    worst_out[...] = jnp.broadcast_to(worst, worst_out.shape)
    wires.drain()
    for copy in kept:
        copy.wait()


SKETCH_ORDER = (
    0, 2, 1, 4, 3, 6, 0, 0, 2, 2, 4, 5, 4, 6, 6, 0, 1, 1, 0, 7, 2, 2, 4, 4, 3, 3, 6, 0,
    6, 1, 1, 5, 0, 1, 1, 1, 5, 2, 2, 4, 4, 3, 3, 7, 7, 0, 3, 3, 3, 4, 2, 6, 6, 1, 1, 0,
    0, 5, 5, 5, 5, 5, 4, 4, 3, 7, 2, 2, 7, 6, 7, 7, 7, 3, 0, 0, 1, 1, 1, 1, 4, 2, 4, 2,
    6, 6, 5, 5, 7, 7, 0, 3, 3, 3, 3, 4, 1, 1, 2, 6, 6, 1, 5, 5, 5, 5, 7, 7, 7, 7, 6, 0,
    0, 3, 3, 1, 1, 3, 4, 4, 2, 2, 5, 5, 5, 7, 7, 7, 6, 6, 0, 0, 4, 4, 1, 3, 3, 2, 2, 6,
    6, 0, 5, 0, 5, 4, 4, 2, 2, 7, 7, 6, 3, 6, 0, 2, 4, 5, 6, 7,
)
GRAM_ORDER = (
    6, 6, 6, 0, 6, 6, 6, 6, 6, 0, 0, 0, 2, 4, 3, 1, 6, 6, 2, 2, 2, 2, 6, 4, 4, 4, 4, 1,
    1, 1, 3, 3, 2, 2, 3, 3, 6, 6, 2, 4, 4, 6, 7, 4, 8, 1, 1, 2, 2, 1, 1, 3, 3, 3, 7, 4,
    4, 1, 1, 8, 2, 1, 5, 5, 5, 5, 5, 5, 5, 5, 5, 5, 5, 5, 5, 3, 3, 5, 5, 5, 4, 5, 3, 5,
    5, 5, 5, 5, 5, 5, 9, 9, 9, 9, 9, 9, 9, 9, 9, 9, 9, 9, 9, 9, 9, 9, 9, 9, 9, 9, 9, 9,
    7, 7, 8, 8,
)
COPIES = 300


def reduce_all(a, lists, scale):
    rows, cols = a.shape
    samples = lists.shape[1]
    half = LANES // 2
    array = lambda *shape: pltpu.VMEM(shape, F32)
    blocks_a = (GROUPS, NZ, NY, ROWS_A, LANES)
    blocks_b = (GROUPS, NY, NZ, ROWS_B, LANES)
    gram_a = (2, NZ, NY, QUARTER, LANES)
    gram_b = (2, 3, NY, NZ, QUARTER, LANES)
    far = pl.BlockSpec(memory_space=pltpu.HBM)
    return pl.pallas_call(
        functools.partial(reduce_kernel, scale=scale),
        out_shape=(
            jax.ShapeDtypeStruct((rows, samples), BF16),
            jax.ShapeDtypeStruct((rows, samples), BF16),
            jax.ShapeDtypeStruct((samples, samples), BF16),
            jax.ShapeDtypeStruct((samples, samples), BF16),
            jax.ShapeDtypeStruct((2, half, samples), F32),
            jax.ShapeDtypeStruct((8, LANES), F32),
            jax.ShapeDtypeStruct((8, NB), F32),
            jax.ShapeDtypeStruct(gram_a, F32),
            jax.ShapeDtypeStruct(gram_b, F32),
        ),
        in_specs=[far, VMEM],
        out_specs=(VMEM,) * 7 + (far,) * 2,
        scratch_shapes=[
            array(rows, cols),
            pltpu.VMEM((cols, samples), BF16),
            array(*blocks_a),
            array(*blocks_b),
            array(8, cols),
            array(*blocks_a),
            array(*blocks_b),
            array(GROUPS, NZ - 1, NY, ROWS_A, LANES),
            array(GROUPS, NY - 1, NZ, ROWS_B, LANES),
            array(GROUPS, NY, ROWS_A, LANES),
            array(GROUPS, NZ, ROWS_B, LANES),
            array(GROUPS, NY - 1, ROWS_A, LANES),
            array(GROUPS, NZ, ROWS_B, LANES),
            array(2, LANES, LANES),
            array(LANES, LANES),
            array(LANES, LANES),
            array(NX - 1, LANES, LANES),
            array(*gram_a),
            array(*gram_b),
            array(2 * NX - 1, 8, cols),
            array(2, NX, half, samples),
            array(NX, 2, half, samples),
            array(NX, 2, half, samples),
            array(2, NX - 1, half, samples),
            array(samples, samples),
            pltpu.VMEM((samples // 2, samples), BF16),
            pltpu.VMEM((samples // 2, samples), BF16),
            pltpu.SemaphoreType.DMA((COPIES,)),
            pltpu.SemaphoreType.DMA((COPIES,)),
            pltpu.SemaphoreType.DMA((3,)),
        ],
        compiler_params=pltpu.CompilerParams(
            collective_id=0, has_side_effects=True, vmem_limit_bytes=MEGA_LIMIT
        ),
    )(a, lists)


NB = 256
STEPS = 2
CONVERGED = 4e-4


def load_gram(ga, gb, m, h, upper):
    for core in range(2):
        for y in range(NY):
            low = (h * NY + y) * LANES + core * 2 * QUARTER
            for z in range(low // NB * 2 if upper else h * NZ // 2, NZ):
                columns = slice(z * LANES, (z + 1) * LANES)
                above = ga[core, z, y] if h == 0 else gb[core, 1, y, z]
                m[low:low + QUARTER, columns] = above
                m[low + QUARTER:low + 2 * QUARTER, columns] = gb[core, 2 * h, y, z]


def masks():
    rows = lax.broadcasted_iota(jnp.int32, (NB, NB), 0)
    cols = lax.broadcasted_iota(jnp.int32, (NB, NB), 1)
    eye = (rows == cols).astype(F32)
    half = jnp.where(rows > cols, 1.0, jnp.where(rows == cols, 0.5, 0.0)).astype(F32)
    return eye, half


def subtract(m, rest, columns, left, right):
    m[rest, columns] = m[rest, columns] - mm_pair(left, right, 0, 0)


def eliminate(wires, low, last, xh, xl, m, rh, rl):
    n, nb = m.shape[0], NB
    high = low + nb
    eye, half = masks()
    block = m[low:high, low:high]
    down = lax.rsqrt(jnp.sum(block * eye, axis=1, keepdims=True))
    across = lax.rsqrt(jnp.sum(block * eye, axis=0, keepdims=True))
    block = block * down * across
    x = eye - half * (block - eye)
    for step in range(STEPS + 2):
        dot = mm1 if step < STEPS else mm3
        residual = dot(dot(x, block, 1, 0), x, 1, 1) - eye
        x = x - mm1(half * residual, x, 1, 0)
        yield None
    off = jnp.where(jnp.abs(residual) < CONVERGED, 0.0, 1.0)
    wires.worst.append(jnp.max(off, axis=0, keepdims=True))
    x = x * across
    m[low:high, low:high] = eye
    pivot = mm3(x, m[low:high, :], 1, 0)
    keep = lax.broadcasted_iota(jnp.int32, (nb, n), 1) < high
    pair = split(pivot)
    xh[low:high, :] = jnp.where(keep, pair[0], 0)
    xl[low:high, :] = jnp.where(keep, pair[1], 0)
    if high < n // 2 + 1:
        rh[low:high, :], rl[low:high, :] = pair
    yield None
    if high < last:
        m[high:last, low:high] = jnp.zeros((last - high, nb), F32)
        left = (pair[0][:, high:last], pair[1][:, high:last])
        for columns in (slice(0, high), slice(high, n)):
            subtract(m, slice(high, last), columns, left, (pair[0][:, columns], pair[1][:, columns]))
        yield None


def factor_first(wires, ga, gb, xh, xl, m, rh, rl):
    while len(wires.ended[0]) < 2:
        yield None
    for copy in wires.relayed[0]:
        yield copy
        copy.wait_recv()
    n = m.shape[0]
    load_gram(ga, gb, m, 0, True)
    for low in range(0, n // 2, NB):
        yield from eliminate(wires, low, n // 2, xh, xl, m, rh, rl)
    wires.halved.append(True)


def factor_second(wires, kept, ga, gb, xh, xl, m, rh, rl):
    while not wires.halved or len(wires.ended[1]) < 2:
        yield None
    for copy in wires.relayed[1]:
        yield copy
        copy.wait_recv()
    for copy in kept:
        copy.start()
    n = m.shape[0]
    middle = n // 2
    load_gram(ga, gb, m, 1, True)
    m[middle:, :middle] = jnp.zeros((n - middle, middle), F32)
    for low in range(middle, n, NB):
        rest = slice(low, low + NB)
        left = (rh[:, rest], rl[:, rest])
        subtract(m, rest, slice(low, n), left, (rh[:, low:], rl[:, low:]))
        above = slice(0, middle)
        subtract(m, rest, above, left, (xh[above, above], xl[above, above]))
        yield None
    for low in range(middle, n, NB):
        yield from eliminate(wires, low, n, xh, xl, m, rh, rl)


def guard_kernel(worst, ga_in, gb_in, xh_in, xl_in, xh_out, xl_out, ga, gb, m, xh, xl, sems):
    @pl.when(jnp.max(worst[...]) > 0.0)
    def _():
        loads = [
            pltpu.make_async_copy(ga_in, ga, sems.at[0]),
            pltpu.make_async_copy(gb_in, gb, sems.at[1]),
        ]
        for copy in loads:
            copy.start()
        for copy in loads:
            copy.wait()
        load_gram(ga, gb, m, 0, False)
        load_gram(ga, gb, m, 1, False)
        n = m.shape[0]
        m[n // 2:, :n // 2] = m[:n // 2, n // 2:].T
        lane = lax.broadcasted_iota(jnp.int32, (1, n), 1)
        chunk = 128

        def column(j, carry):
            row = m[pl.ds(j, 1), :]
            scale = lax.rsqrt(jnp.sum(jnp.where(lane == j, row, 0.0), axis=1, keepdims=True))
            pivot = jnp.where(lane == j, 1.0, row) * scale
            m[pl.ds(j, 1), :] = jnp.where(lane <= j, pivot, 0.0)

            def update(part, carry):
                here = pl.ds(pl.multiple_of(part * chunk, chunk), chunk)
                below = part * chunk + lax.broadcasted_iota(jnp.int32, (chunk, 1), 0) > j
                old = m[here, :]
                entry = jnp.sum(jnp.where(lane == j, old, 0.0), axis=1, keepdims=True) * scale
                new = jnp.where(lane == j, 0.0, old) - entry * pivot
                m[here, :] = jnp.where(below, new, old)
                return carry

            return lax.fori_loop(j // chunk, n // chunk, update, carry)

        lax.fori_loop(0, n, column, 0)
        xh[...], xl[...] = split(m[...])
        stores = [
            pltpu.make_async_copy(xh, xh_out, sems.at[0]),
            pltpu.make_async_copy(xl, xl_out, sems.at[1]),
        ]
        for copy in stores:
            copy.start()
        for copy in stores:
            copy.wait()


def guard(worst, ga, gb, xh, xl):
    n = xh.shape[0]
    anywhere = pl.BlockSpec(memory_space=pl.ANY)
    return pl.pallas_call(
        guard_kernel,
        out_shape=(jax.ShapeDtypeStruct((n, n), BF16),) * 2,
        in_specs=[VMEM] + [anywhere] * 4,
        out_specs=(anywhere, anywhere),
        input_output_aliases={3: 0, 4: 1},
        scratch_shapes=[
            pltpu.VMEM(ga.shape, F32),
            pltpu.VMEM(gb.shape, F32),
            pltpu.VMEM((n, n), F32),
            pltpu.VMEM((n, n), BF16),
            pltpu.VMEM((n, n), BF16),
            pltpu.SemaphoreType.DMA((2,)),
        ],
        compiler_params=pltpu.CompilerParams(vmem_limit_bytes=GUARD_LIMIT),
    )(worst, ga, gb, xh, xl)


def outputs_kernel(
    sh, sl, xh, xl, wt, tops, basis_ref, proj_ref, stage, inbox, send_sems, recv_sems, *, root
):
    row = lax.axis_index("row")
    x, core = row // 2, lax.rem(row, 2)
    turns = [(step, flip) for step in (2, 1, 3) for flip in (0, 1)] + [(0, 1)]
    place_of = lambda step, flip: lax.rem(x + step, NX) * 2 + (1 - core if flip else core)
    peers = [place_of(step, flip) for step, flip in turns]
    arrive = greet([{"row": peer} for peer in peers])
    n = xh.shape[0]
    wide = 256
    pair = split(wt[...].reshape(LANES, xh.shape[0]))
    for low in range(0, n, wide):
        high = low + wide
        out = mm_pair(
            (xh[low:high, :high], xl[low:high, :high]), (pair[0][:, :high], pair[1][:, :high]), 1, 1
        )
        out = out * tops[0:1, :]
        for sub in range(wide // LANES):
            stage[low // LANES + sub] = out[sub * LANES:(sub + 1) * LANES]
    arrive()
    copies = []
    for index, peer in enumerate(peers):
        copy = pltpu.make_async_remote_copy(
            src_ref=stage.at[peer],
            dst_ref=inbox.at[index],
            send_sem=send_sems.at[index],
            recv_sem=recv_sems.at[index],
            device_id={"row": peer},
            device_id_type=MESH,
        )
        copy.start()
        copies.append(copy)
    for low in range(0, n, wide):
        high = low + wide
        basis = mm_pair(
            (sh[:, :high], sl[:, :high]), (xh[low:high, :high], xl[low:high, :high]), 1, 1
        )
        basis_ref[:, low:high] = basis * root
    columns = lambda owner: pl.ds(pl.multiple_of(owner * LANES, LANES), LANES)
    proj_ref[:, columns(row)] = stage[row]
    for index, copy in enumerate(copies):
        copy.wait()
        step, flip = turns[index]
        proj_ref[:, columns(place_of(NX - step, flip))] = inbox[index]


def outputs(sh, sl, xh, xl, wt, tops, root):
    rows, n = sh.shape
    count = 2 * NX
    return pl.pallas_call(
        functools.partial(outputs_kernel, root=root),
        out_shape=(
            jax.ShapeDtypeStruct((rows, n), F32),
            jax.ShapeDtypeStruct((n // count, count * LANES), F32),
        ),
        in_specs=[VMEM] * 6,
        out_specs=(VMEM, VMEM),
        scratch_shapes=[
            pltpu.VMEM((count, LANES, LANES), F32),
            pltpu.VMEM((count - 1, LANES, LANES), F32),
            pltpu.SemaphoreType.DMA((count - 1,)),
            pltpu.SemaphoreType.DMA((count - 1,)),
        ],
        compiler_params=pltpu.CompilerParams(
            collective_id=1, has_side_effects=True, vmem_limit_bytes=OUTPUT_LIMIT
        ),
    )(sh, sl, xh, xl, wt, tops)


def body(expert_matrix, col_signs, sample_ids):
    local_cols = expert_matrix.shape[1]
    col_total = local_cols * lax.axis_size("col")
    model_width = expert_matrix.shape[0] * lax.axis_size("row")
    lists = jnp.stack([col_signs, sample_ids])
    sh, sl, xh, xl, wt, tops, worst, ga, gb = reduce_all(
        expert_matrix, lists, 1.0 / math.sqrt(col_total)
    )
    xh, xl = guard(worst, ga, gb, xh, xl)
    return outputs(sh, sl, xh, xl, wt, tops, math.sqrt(model_width))


def solution(mesh):
    in_specs = (P("row", "col"), P("col"), P())
    out_specs = (P("row", None), P("row", "col"))
    return jax.shard_map(body, mesh=mesh, in_specs=in_specs, out_specs=out_specs, check_vma=False)
```
